32 devices in a mesh: gx: 4 (over z), gy: 8 (over y, x, core).
Axes of the slice: x: 2, y: 2, z: 4, core: 2. Of those that a mesh axis runs over, the one named last changes fastest.
Arguments:
- multipoles: float32 [35, 131072], P(None, ('gx', 'gy')), may hold values from -6 to 6
- proxy_list: int32 [32, 8, 512], P(('gx', 'gy')), may hold values from 0 to 4095
- proxy_count: int32 [32, 8], P(('gx', 'gy')), may hold values from 1 to 512, as said below
- pair_source: int32 [2097152], P(('gx', 'gy')), may hold values from 0 to 9215
- pair_target: int32 [2097152], P(('gx', 'gy')), may hold values from 0 to 8191, as said below
- block_class: int32 [32768], P(('gx', 'gy')), may hold values from 0 to 188
- m2l_ops: float32 [189, 35, 35], replicated, may hold values from -1 to 1
- cell_mesh: int32 [131072], P(('gx', 'gy')), may hold values from 0 to 2097151
- pm_density: float32 [64, 1024, 1024], P('gy', None, 'gx'), may hold values from -6 to 6
Outputs:
- field_tensors: float32 [35, 131072], P(None, ('gx', 'gy'))
- pm_spectrum: float32 [2, 64, 1024, 1024], P(None, 'gy', 'gx')
The draws below stay inside these ranges and needn't reach their ends.
Inputs may be any that keep to these rules, and one draw needn't show every extreme that they name: `proxy_count`: some neighbour slot of every domain holds all 512 slots live. `pair_target`: pairs are ordered by target: the pairs of block b of a domain target each column w * 64 to w * 64 + 63 exactly once, with w = (b * 128) // 1024.
All inputs are finite; a program needn't handle non-finite values.
Results may differ from the reference program's by a relative error of at most 0.000075.
Values sent between devices are 32-bit elements; how exact they have to be, the bound alone decides.
No kernel may reach another device: no remote copies, remote signals or barrier semaphores. Data moves between devices by JAX's collectives and lax.ppermute only.
A program may use at most 128 MiB of HBM per device.

```python
import jax
import jax.numpy as jnp
import numpy as np
from jax import lax

K = 35
CELLS = 4096
PROX = 512
TOP = 32
BLOCK = 64
NPAIR = 65536
NCLASS = 189
NG = 1024
ROWS_Y = 1024
PL_DEV = 8
PLANES = 64
NBLK = 1024
N_GX = 4
N_GY = 8


def draw_proxy_count(key, part):
    key = jax.random.fold_in(key, 11)
    first, second = jax.random.split(key)
    domains = N_GX * N_GY
    counts = jax.random.randint(first, (domains, 8), 1, PROX + 1)
    full_column = jax.random.randint(second, (), 0, 8)
    columns = jnp.arange(8)[None, :]
    return jnp.where(columns == full_column, PROX, counts).astype(jnp.int32)


def draw_pair_target(key, part):
    key = jax.random.fold_in(key, 23)
    domains = N_GX * N_GY
    block_total = NPAIR // BLOCK
    window_total = (CELLS + 8 * PROX) // BLOCK
    keys = jax.random.split(key, domains * block_total)
    offsets = jax.vmap(lambda item_key: jax.random.permutation(item_key, BLOCK))(keys).reshape(domains, block_total, BLOCK)
    windows = jnp.arange(block_total, dtype=jnp.int32) * window_total // block_total
    targets = windows[None, :, None] * BLOCK + offsets.astype(jnp.int32)
    return targets.reshape(-1).astype(jnp.int32)


def set_ends(values, key, low, largest):
    longest = values.shape.index(max(values.shape))
    spots = []
    for shift in (0, 1):
        where = [jax.random.randint(jax.random.fold_in(key, axis), (), 0, length) for axis, length in enumerate(values.shape)]
        where[longest] = (where[longest] + shift) % values.shape[longest]
        spots.append(tuple(where))
    return values.at[spots[0]].set(low).at[spots[1]].set(largest)


def steps_of(stream_key, shape, pieces, low, high):
    def one(position, parts):
        heights = jax.random.uniform(jax.random.fold_in(jax.random.fold_in(stream_key, 6), position), (parts,), jnp.float32, low / len(pieces), high / len(pieces))
        return jnp.repeat(jnp.exp(heights), shape[position] // parts).reshape((-1,) + (1,) * (len(shape) - position - 1))

    gain = one(*pieces[0])
    for cut in pieces[1:]:
        gain = gain * one(*cut)
    return gain


def scatter_about(own_key, shape, scale, limit, cuts=(), kind=jnp.bfloat16):
    array = scale * jax.random.normal(own_key, shape, jnp.float32)
    if cuts:
        array = array * steps_of(own_key, shape, cuts, -0.22, 0.18)
    return jnp.clip(array, -limit, limit).astype(kind)


def setup_inputs(seed: int = 0) -> dict:
    key_of = jax.random.split(jax.random.key(seed), 10)
    multipoles = scatter_about(key_of[0], (K, CELLS * N_GX * N_GY), 1.0, 6.0, ((1, 32),), jnp.float32)
    proxy_list = set_ends(jax.random.randint(key_of[1], (N_GX * N_GY, 8, PROX), 0, CELLS), jax.random.fold_in(key_of[1], 1), 0, CELLS - 1).astype(jnp.int32)
    proxy_count = draw_proxy_count(jax.random.fold_in(key_of[9], 71), 0)
    pair_source = set_ends(jax.random.randint(key_of[3], (NPAIR * N_GX * N_GY,), 0, CELLS + 8 * PROX + N_GX * N_GY * TOP), jax.random.fold_in(key_of[3], 1), 0, (CELLS + 8 * PROX + N_GX * N_GY * TOP) - 1).astype(jnp.int32)
    pair_target = draw_pair_target(jax.random.fold_in(key_of[9], 71), 0)
    block_class = set_ends(jax.random.randint(key_of[5], (NBLK * N_GX * N_GY,), 0, NCLASS), jax.random.fold_in(key_of[5], 1), 0, NCLASS - 1).astype(jnp.int32)
    m2l_ops = scatter_about(key_of[6], (NCLASS, K, K), K ** -0.5, 1.0, (), jnp.float32)
    cell_mesh = set_ends(jax.random.randint(key_of[7], (CELLS * N_GX * N_GY,), 0, PL_DEV * ROWS_Y * (NG // N_GX)), jax.random.fold_in(key_of[7], 1), 0, (PL_DEV * ROWS_Y * (NG // N_GX)) - 1).astype(jnp.int32)
    pm_density = scatter_about(key_of[8], (PLANES, ROWS_Y, NG), 1.0, 6.0, ((0, 8), (2, 4)), jnp.float32)
    return dict(multipoles=multipoles, proxy_list=proxy_list, proxy_count=proxy_count, pair_source=pair_source, pair_target=pair_target, block_class=block_class, m2l_ops=m2l_ops, cell_mesh=cell_mesh, pm_density=pm_density)


DEPOSIT_SCALE = 8.0

def partner_table():
    domains = N_GX * N_GY
    offsets = [(step_x, step_y) for step_x in (-1, 0, 1) for step_y in (-1, 0, 1) if step_x != 0 or step_y != 0]
    domain_ids = np.arange(domains)
    row_index = domain_ids // N_GY
    column_index = domain_ids % N_GY
    result = np.stack([(row_index + step_x) % N_GX * N_GY + (column_index + step_y) % N_GY for step_x, step_y in offsets], axis=1)
    return jnp.asarray(result, dtype=jnp.int32)

def reference(multipoles, proxy_list, proxy_count, pair_source, pair_target, block_class, m2l_ops, cell_mesh, pm_density):
    domains = N_GX * N_GY
    own_cells = multipoles.reshape(K, domains, CELLS).transpose(1, 0, 2)
    live_mask = (jnp.arange(PROX, dtype=jnp.int32)[None, None, :] < proxy_count[:, :, None]).astype(multipoles.dtype)
    sent_cells = jax.vmap(lambda cell_block, slot_ids: cell_block[:, slot_ids])(own_cells, proxy_list)
    sent_cells = sent_cells * live_mask[:, None, :, :]
    partners = partner_table()
    opposite = (7 - jnp.arange(8, dtype=jnp.int32))[None, :]
    received = sent_cells[partners, :, opposite].transpose(0, 2, 1, 3)
    top_table = own_cells[:, :, :TOP].transpose(1, 0, 2).reshape(K, domains * TOP)
    sources = pair_source.reshape(domains, NPAIR)
    targets = pair_target.reshape(domains, NPAIR)
    classes = block_class.reshape(domains, NPAIR // BLOCK)

    def m2l_domain(domain_items):
        own_block, remote, source_ids, target_ids, class_ids = domain_items
        table = jnp.concatenate([own_block, remote.reshape(K, 8 * PROX), top_table], axis=1)
        gathered = jnp.take(table, source_ids, axis=1).reshape(K, NPAIR // BLOCK, BLOCK)
        operators = m2l_ops[class_ids]
        terms = jnp.einsum('bkj,jbi->kbi', operators, gathered, precision=lax.Precision.HIGHEST).reshape(K, NPAIR)
        return jnp.zeros((K, CELLS + 8 * PROX), multipoles.dtype).at[:, target_ids].add(terms)
    accumulated = lax.map(m2l_domain, (own_cells, received, sources, targets, classes))
    local_part = accumulated[:, :, :CELLS]
    slot_fields = accumulated[:, :, CELLS:].reshape(domains, K, 8, PROX)
    returned = slot_fields[partners, :, opposite].transpose(0, 2, 1, 3) * live_mask[:, None, :, :]

    def add_back(local_fields, extra_fields, slot_ids):
        extra = jnp.zeros((K, CELLS), multipoles.dtype).at[:, slot_ids.reshape(-1)].add(extra_fields.reshape(K, 8 * PROX))
        return local_fields + extra
    fields = jax.vmap(add_back)(local_part, returned, proxy_list)
    field_tensors = fields.transpose(1, 0, 2).reshape(K, domains * CELLS)
    slab_width = NG // N_GX
    local_ids = cell_mesh.reshape(domains, CELLS)
    domain_ids = jnp.arange(domains, dtype=jnp.int32)[:, None]
    plane_ids = domain_ids % N_GY * PL_DEV + local_ids // (ROWS_Y * slab_width)
    row_ids = local_ids // slab_width % ROWS_Y
    column_ids = domain_ids // N_GY * slab_width + local_ids % slab_width
    density = pm_density.at[plane_ids, row_ids, column_ids].add(DEPOSIT_SCALE * own_cells[:, 0, :])
    spectrum = jnp.fft.fft(density, axis=-1)
    scale = 1.0 / jnp.sqrt(jnp.float32(NG))
    pm_spectrum = jnp.stack([jnp.real(spectrum) * scale, jnp.imag(spectrum) * scale]).astype(jnp.float32)
    return (field_tensors, pm_spectrum)
```

```python
import functools

import jax
import jax.numpy as jnp
import ml_dtypes
import numpy as np
from jax import lax
from jax.experimental import pallas as pl
from jax.experimental.pallas import tpu as pltpu
from jax.sharding import PartitionSpec as P

TOP = 32
BLOCK = 64
LANES = 128
KPAD = 40
COPIES = 3
PER_WINDOW = 8
VMEM_BYTES = 48 * 1024 * 1024
CHUNKS = (2, 2, 2, 2)

DEPOSIT_SCALE = 8.0
OFFSETS = tuple((a, b) for a in (-1, 0, 1) for b in (-1, 0, 1) if (a, b) != (0, 0))

SMEM_WHOLE = pl.BlockSpec(memory_space=pltpu.SMEM)
VMEM_WHOLE = pl.BlockSpec(memory_space=pltpu.VMEM)


def params():
    return pltpu.CompilerParams(vmem_limit_bytes=VMEM_BYTES)


def cost(flops, nbytes):
    return pl.CostEstimate(flops=flops, bytes_accessed=nbytes, transcendentals=0)


def spread(block):
    rest = jnp.zeros((LANES - COPIES * KPAD, LANES), jnp.float32)
    return jnp.concatenate([block] * COPIES + [rest], axis=0).T


def lane_ids(shape):
    return lax.broadcasted_iota(jnp.int32, shape, len(shape) - 1)


def pack_kernel(list_ref, count_ref, cells_ref, out_ref, top_ref, table, rows):
    tiles = cells_ref.shape[1] // LANES

    @pl.loop(0, tiles)
    def _(k):
        at = pl.multiple_of(k * LANES, LANES)
        table[pl.ds(at, LANES), :] = spread(cells_ref[:, pl.ds(at, LANES)])

    top_ref[...] = table[:TOP, :]
    slot_tiles = list_ref.shape[1] // LANES

    @pl.loop(0, 8 * slot_tiles)
    def _(i):
        n = i // slot_tiles
        first = pl.multiple_of((i % slot_tiles) * LANES, LANES)
        for r in range(LANES):
            rows[pl.ds(r, 1), :] = table[pl.ds(list_ref[n, first + r], 1), :]
        live = (lane_ids((KPAD, LANES)) + first) < count_ref[n]
        out_ref[n, :, pl.ds(first, LANES)] = jnp.where(live, rows[...].T[:KPAD], 0.0)


def pack(cells, proxy_list, proxy_count):
    slots = proxy_list.shape[1]
    return pl.pallas_call(
        pack_kernel,
        out_shape=(
            jax.ShapeDtypeStruct((8, KPAD, slots), jnp.float32),
            jax.ShapeDtypeStruct((TOP, LANES), jnp.float32),
        ),
        in_specs=[SMEM_WHOLE, SMEM_WHOLE, VMEM_WHOLE],
        out_specs=(VMEM_WHOLE, VMEM_WHOLE),
        scratch_shapes=[
            pltpu.VMEM((cells.shape[1], LANES), jnp.float32),
            pltpu.VMEM((LANES, LANES), jnp.float32),
        ],
        compiler_params=params(),
        cost_estimate=cost(10**6, 16 * 10**6),
        name="pack",
    )(proxy_list, proxy_count, cells)


def exchange(blocks, n_gx, n_gy):
    arrived = [None] * 8
    for m, (a, b) in enumerate(OFFSETS):
        pairs = [
            (x * n_gy + y, (x + a) % n_gx * n_gy + (y + b) % n_gy)
            for x in range(n_gx)
            for y in range(n_gy)
        ]
        arrived[7 - m] = lax.ppermute(blocks[m], ("gx", "gy"), pairs)
    return arrived


def order_kernel(packed_ref, out_ref):
    lanes = lane_ids((LANES, LANES))
    within = lanes % BLOCK
    base = lanes - within

    @pl.loop(0, packed_ref.shape[0] // LANES)
    def _(k):
        at = pl.ds(pl.multiple_of(k * LANES, LANES), LANES)
        packed = packed_ref[at, :]

        def step(i, ordered):
            value = jnp.take_along_axis(packed, base + i, axis=1, mode="promise_in_bounds")
            return jnp.where(value % BLOCK == within, value // BLOCK, ordered)

        out_ref[at, :] = lax.fori_loop(0, BLOCK, step, jnp.zeros_like(packed), unroll=8)


def order(packed):
    return pl.pallas_call(
        order_kernel,
        out_shape=jax.ShapeDtypeStruct(packed.shape, jnp.int32),
        in_specs=[VMEM_WHOLE],
        out_specs=VMEM_WHOLE,
        compiler_params=params(),
        cost_estimate=cost(10**6, 16 * 10**6),
        name="order",
    )(packed)


def table_kernel(*refs):
    cells_ref, top_ref, out_ref = refs[0], refs[9], refs[10]
    cell_count = cells_ref.shape[1]

    @pl.loop(0, cell_count // LANES)
    def _(k):
        at = pl.multiple_of(k * LANES, LANES)
        out_ref[pl.ds(at, LANES), :] = spread(cells_ref[:, pl.ds(at, LANES)])

    for n in range(8):
        slots = refs[1 + n].shape[1]
        for k in range(slots // LANES):
            at = cell_count + n * slots + k * LANES
            out_ref[at : at + LANES, :] = spread(refs[1 + n][:, k * LANES : (k + 1) * LANES])
    out_ref[cell_count + 8 * refs[1].shape[1] :, :] = top_ref[...]


def make_table(cells, arrived, top_rows):
    rows = cells.shape[1] + 8 * arrived[0].shape[1] + top_rows.shape[0]
    return pl.pallas_call(
        table_kernel,
        out_shape=jax.ShapeDtypeStruct((rows, LANES), jnp.float32),
        in_specs=[VMEM_WHOLE] * 10,
        out_specs=VMEM_WHOLE,
        compiler_params=params(),
        cost_estimate=cost(10**6, 16 * 10**6),
        name="table",
    )(cells, *arrived, top_rows)


def m2l_kernel(source_ref, class_ref, table_ref, ops_ref, out_ref, gathered, *, turned):
    step = pl.program_id(0)
    lanes = lane_ids((1, LANES))
    in_first = lanes < KPAD
    in_second = lanes < 2 * KPAD

    def row(b, t):
        return table_ref[pl.ds(source_ref[b // 2, (b % 2) * BLOCK + t], 1), :]

    for u in range(2):

        @pl.loop(0, BLOCK, step=8)
        def _(first):
            for t in range(8):
                for g in range(3):
                    b = u * PER_WINDOW + 3 * g
                    one, two = row(b, first + t), row(b + 1, first + t)
                    three = row(b + 2, first + t) if g < 2 else two
                    gathered[g, pl.ds(u * BLOCK + first + t, 1), :] = jnp.where(
                        in_first, one, jnp.where(in_second, two, three)
                    )

    rest = jnp.zeros((LANES - COPIES * KPAD, LANES), jnp.float32)
    none = jnp.zeros((KPAD, LANES), jnp.float32)
    results = []
    for u in range(2):
        total = jnp.zeros((BLOCK, LANES), jnp.float32)
        for g in range(3):
            held = []
            for s in range(3):
                b = 3 * g + s
                if b < PER_WINDOW:
                    held.append(ops_ref[class_ref[step * 2 * PER_WINDOW + u * PER_WINDOW + b]])
                else:
                    held.append(none)
            weights = jnp.concatenate(held + [rest], axis=0).astype(jnp.bfloat16)
            values = gathered[g, u * BLOCK : (u + 1) * BLOCK, :]
            high = values.astype(jnp.bfloat16)
            low = (values - high.astype(jnp.float32)).astype(jnp.bfloat16)
            total += jnp.dot(high, weights, preferred_element_type=jnp.float32)
            total += jnp.dot(low, weights, preferred_element_type=jnp.float32)
        results.append(total)
    both = jnp.concatenate(results, axis=0)
    both = both + pltpu.roll(both, LANES - KPAD, 1)
    if turned:
        out_ref[0] = both.T[:KPAD]
    else:
        out_ref[...] = both


def m2l(sources, classes, table, ops, turned, slots):
    steps = classes.shape[0] // (2 * PER_WINDOW)
    if turned:
        per = slots // LANES
        shape = (steps // per, KPAD, slots)
        out_spec = pl.BlockSpec((1, KPAD, LANES), lambda i: (i // per, 0, i % per))
    else:
        shape = (steps * LANES, LANES)
        out_spec = pl.BlockSpec((LANES, LANES), lambda i: (i, 0))
    return pl.pallas_call(
        functools.partial(m2l_kernel, turned=turned),
        grid=(steps,),
        out_shape=jax.ShapeDtypeStruct(shape, jnp.float32),
        in_specs=[
            pl.BlockSpec((8, LANES), lambda i: (i, 0), memory_space=pltpu.SMEM),
            SMEM_WHOLE,
            VMEM_WHOLE,
            VMEM_WHOLE,
        ],
        out_specs=out_spec,
        scratch_shapes=[pltpu.VMEM((3, LANES, LANES), jnp.float32)],
        compiler_params=params(),
        cost_estimate=cost(10**6, 100 * 10**6),
        name="m2l_slots" if turned else "m2l_cells",
    )(sources, classes, table, ops)


def add_back_kernel(list_ref, count_ref, own_ref, *refs):
    slot_refs, out_ref = refs[:8], refs[8]
    rows, sums = refs[9], refs[10:]
    slots = list_ref.shape[1]
    sums[0][...] = own_ref[...]
    for held in sums[1:]:
        held[...] = jnp.zeros_like(held)
    for n in range(8):
        for k in range(slots // LANES):
            live = (lane_ids((KPAD, LANES)) + k * LANES) < count_ref[n]
            values = jnp.where(live, slot_refs[n][:, k * LANES : (k + 1) * LANES], 0.0)
            at = n * slots + k * LANES
            rows[at : at + LANES, :] = spread(values)
    for half in range(2):

        @pl.loop(0, slots, step=4)
        def _(first):
            for j in range(4):
                for s, held in enumerate(sums):
                    n = 4 * half + s
                    to = pl.ds(list_ref[n, first + j], 1)
                    held[to, :] = held[to, :] + rows[pl.ds(n * slots + first + j, 1), :]

    @pl.loop(0, own_ref.shape[0] // LANES)
    def _(k):
        at = pl.ds(pl.multiple_of(k * LANES, LANES), LANES)
        total = (sums[0][at, :] + sums[1][at, :]) + (sums[2][at, :] + sums[3][at, :])
        out_ref[:, at] = total.T[: out_ref.shape[0]]


def add_back(proxy_list, proxy_count, own_rows, slot_fields, coef_count):
    cell_count = own_rows.shape[0]
    slots = proxy_list.shape[1]
    return pl.pallas_call(
        add_back_kernel,
        out_shape=jax.ShapeDtypeStruct((coef_count, cell_count), jnp.float32),
        in_specs=[SMEM_WHOLE, SMEM_WHOLE] + [VMEM_WHOLE] * 9,
        out_specs=VMEM_WHOLE,
        scratch_shapes=[pltpu.VMEM((8 * slots, LANES), jnp.float32)]
        + [pltpu.VMEM((cell_count, LANES), jnp.float32)] * 4,
        compiler_params=params(),
        cost_estimate=cost(10**6, 30 * 10**6),
        name="add_back",
    )(proxy_list, proxy_count, own_rows, *slot_fields)


def deposit_kernel(code_ref, value_ref, *outs):
    lanes = lane_ids((1, LANES))
    for out_ref in outs:
        out_ref[...] = jnp.zeros_like(out_ref)

    @pl.loop(0, code_ref.shape[1], step=4)
    def _(first):
        for j in range(4):
            for s, out_ref in enumerate(outs):
                code = code_ref[s, first + j]
                to = pl.ds(code // LANES, 1)
                value = jnp.where(lanes == code % LANES, value_ref[s, first + j], 0.0)
                out_ref[to, :] = out_ref[to, :] + value


def deposit(codes, values, rows):
    sources = codes.shape[0]
    return pl.pallas_call(
        deposit_kernel,
        out_shape=(jax.ShapeDtypeStruct((rows, LANES), jnp.float32),) * sources,
        in_specs=[SMEM_WHOLE, SMEM_WHOLE],
        out_specs=(VMEM_WHOLE,) * sources,
        compiler_params=params(),
        cost_estimate=cost(10**6, 100 * 10**6),
        name="deposit",
    )(codes, values)


def fourier_tables(length):
    positions = np.arange(length)
    angles = (positions[:, None] * positions[None, : length // 2] % length) * (2.0 * np.pi / length)
    scale = 1.0 / np.sqrt(length)
    imag = -np.sin(angles) * scale
    imag[:, 0] = np.where(positions % 2 == 0, scale, -scale)
    whole = np.concatenate([np.cos(angles) * scale, imag], axis=1)
    high = whole.astype(ml_dtypes.bfloat16)
    low = (whole - high.astype(np.float64)).astype(ml_dtypes.bfloat16)
    return high, low


def fourier_kernel(*refs, sources, linked):
    mesh_ref, add_refs = refs[0], refs[1 : 1 + sources]
    high_ref, low_ref = refs[1 + sources], refs[2 + sources]
    out_ref = refs[-1]
    rows = mesh_ref.shape[2]
    width = mesh_ref.shape[3]
    pieces = []
    for s in range(sources):
        for h in range(width // LANES):
            pieces.append(
                mesh_ref[s, 0, :, h * LANES : (h + 1) * LANES]
                + add_refs[s][h * rows : (h + 1) * rows, :]
            )
    values = jnp.concatenate(pieces, axis=1)
    length = values.shape[1]
    high = values.astype(jnp.bfloat16)
    low = (values - high.astype(jnp.float32)).astype(jnp.bfloat16)
    half = jnp.dot(high, high_ref[...], preferred_element_type=jnp.float32)
    half += jnp.dot(low, high_ref[...], preferred_element_type=jnp.float32)
    half += jnp.dot(high, low_ref[...], preferred_element_type=jnp.float32)
    lanes = lane_ids((rows, LANES))
    is_first = lanes == 0
    mirror = (LANES - lanes) % LANES
    tiles = length // LANES
    per = tiles // 2

    def tile(part, j):
        at = (part * per + j) * LANES
        return half[:, at : at + LANES]

    for j in range(per):
        real, imag = tile(0, j), tile(1, j)
        if j == 0:
            imag = jnp.where(is_first, 0.0, imag)
        out_ref[0, 0, :, j * LANES : (j + 1) * LANES] = real
        out_ref[1, 0, :, j * LANES : (j + 1) * LANES] = imag
    for j in range(per, tiles):
        back = tiles - 1 - j
        real = jnp.take_along_axis(tile(0, back), mirror, axis=1, mode="promise_in_bounds")
        imag = -jnp.take_along_axis(tile(1, back), mirror, axis=1, mode="promise_in_bounds")
        if j == per:
            real = jnp.where(is_first, tile(1, 0), real)
            imag = jnp.where(is_first, 0.0, imag)
        else:
            real = jnp.where(is_first, tile(0, back + 1), real)
            imag = jnp.where(is_first, -tile(1, back + 1), imag)
        out_ref[0, 0, :, j * LANES : (j + 1) * LANES] = real
        out_ref[1, 0, :, j * LANES : (j + 1) * LANES] = imag


def fourier(mesh_part, adds, tables, first, planes, so_far):
    sources, count, rows, width = mesh_part.shape
    length = sources * width
    add_rows = (width // LANES) * rows
    operands = [mesh_part, *adds, *tables]
    in_specs = (
        [pl.BlockSpec((sources, 1, rows, width), lambda p: (0, p, 0, 0))]
        + [pl.BlockSpec((add_rows, LANES), lambda p: (first + p, 0))] * sources
        + [pl.BlockSpec((length, length), lambda p: (0, 0), pipeline_mode=pl.Buffered(1))] * 2
    )
    aliases = {}
    if so_far is not None:
        aliases = {len(operands): 0}
        operands.append(so_far)
        in_specs.append(pl.BlockSpec(memory_space=pl.ANY))
    return pl.pallas_call(
        functools.partial(fourier_kernel, sources=sources, linked=so_far is not None),
        grid=(count,),
        out_shape=jax.ShapeDtypeStruct((2, planes, rows, length), jnp.float32),
        in_specs=in_specs,
        out_specs=pl.BlockSpec((2, 1, rows, length), lambda p: (0, first + p, 0, 0)),
        input_output_aliases=aliases,
        compiler_params=params(),
        cost_estimate=cost(2 * count * rows * length * length * 3, count * rows * length * 16 + 4 * length * length),
        name="fourier",
    )(*operands)


def on_device(
    multipoles,
    proxy_list,
    proxy_count,
    pair_source,
    pair_target,
    block_class,
    m2l_ops,
    cell_mesh,
    pm_density,
    *,
    n_gx,
    n_gy,
):
    coef_count, cell_count = multipoles.shape
    slots = proxy_list.shape[2]
    planes, mesh_rows, width = pm_density.shape
    own_rows = mesh_rows // n_gx
    lists, counts = proxy_list[0], proxy_count[0]

    spans = []
    first = 0
    for size in CHUNKS:
        spans.append((first, size))
        first += size

    def send(span):
        part = pm_density[span[0] : span[0] + span[1]]
        part = part.reshape(span[1], n_gx, own_rows, width).transpose(1, 0, 2, 3)
        return lax.all_to_all(part, "gx", 0, 0, tiled=True)

    cells = jnp.pad(multipoles, ((0, KPAD - coef_count), (0, 0)))
    outgoing, top_own = pack(cells, lists, counts)
    arrived = exchange(outgoing, n_gx, n_gy)
    top_rows = lax.all_gather(top_own, ("gx", "gy"), axis=0, tiled=True)

    held = jnp.stack(
        [cell_mesh.astype(jnp.float32), DEPOSIT_SCALE * multipoles[0]]
    ).reshape(2, cell_count // LANES, LANES)
    near = lax.all_gather(held, "gx", axis=0)
    place = near[:, 0].reshape(n_gx, cell_count).astype(jnp.int32)
    amount = near[:, 1].reshape(n_gx, cell_count)
    plane = place // (mesh_rows * width)
    row = place // width % mesh_rows
    column = place % width
    parts = width // LANES
    add_rows = planes * parts * own_rows
    at_row = (plane * parts + column // LANES) * own_rows + row % own_rows
    mine = row // own_rows == lax.axis_index("gx")
    codes = jnp.where(mine, at_row, add_rows) * LANES + column % LANES

    packed = (pair_source * BLOCK + pair_target % BLOCK).reshape(-1, LANES)
    sources = order(packed)

    turned_ops = jnp.pad(
        m2l_ops.transpose(0, 2, 1), ((0, 0), (0, KPAD - coef_count), (0, KPAD - coef_count))
    )
    high = lax.reduce_precision(turned_ops, 8, 7)
    ops = jnp.concatenate([high, turned_ops - high], axis=2)
    ops = jnp.pad(ops, ((0, 0), (0, 0), (0, LANES - 2 * KPAD)))

    table = make_table(cells, arrived, top_rows)
    cell_blocks = cell_count // BLOCK * PER_WINDOW
    cut = cell_blocks * BLOCK // LANES
    slot_fields = m2l(sources[cut:], block_class[cell_blocks:], table, ops, True, slots)
    returned = exchange(slot_fields, n_gx, n_gy)
    own_fields = m2l(sources[:cut], block_class[:cell_blocks], table, ops, False, slots)

    adds = deposit(codes, amount, add_rows + 8)
    tables = fourier_tables(n_gx * width)
    spectrum = None
    for span in spans:
        spectrum = fourier(send(span), adds, tables, span[0], planes, spectrum)

    field_tensors = add_back(lists, counts, own_fields, returned, coef_count)
    return (field_tensors, spectrum)


def solution(mesh):
    placed = (
        P(None, ("gx", "gy")),
        P(("gx", "gy"), None, None),
        P(("gx", "gy"), None),
        P(("gx", "gy")),
        P(("gx", "gy")),
        P(("gx", "gy")),
        P(),
        P(("gx", "gy")),
        P("gy", None, "gx"),
    )
    return jax.shard_map(
        functools.partial(on_device, n_gx=mesh.shape["gx"], n_gy=mesh.shape["gy"]),
        mesh=mesh,
        in_specs=placed,
        out_specs=(P(None, ("gx", "gy")), P(None, "gy", "gx", None)),
        check_vma=False,
    )
```

```python
import functools

import jax
import jax.numpy as jnp
import ml_dtypes
import numpy as np
from jax import lax
from jax.experimental import pallas as pl
from jax.experimental.pallas import tpu as pltpu
from jax.sharding import PartitionSpec as P

TOP = 32
BLOCK = 64
LANES = 128
KPAD = 40
COPIES = 3
PER_WINDOW = 8
SHIFT = 6
LANE_SHIFT = 7
VMEM_BYTES = 48 * 1024 * 1024
CHUNKS = (1, 3, 3, 1)
TOP_ROWS = TOP // 2

DEPOSIT_SCALE = 8.0
OFFSETS = tuple((a, b) for a in (-1, 0, 1) for b in (-1, 0, 1) if (a, b) != (0, 0))

SMEM_WHOLE = pl.BlockSpec(memory_space=pltpu.SMEM)
VMEM_WHOLE = pl.BlockSpec(memory_space=pltpu.VMEM)


def params():
    return pltpu.CompilerParams(vmem_limit_bytes=VMEM_BYTES)


def cost(flops, nbytes):
    return pl.CostEstimate(flops=flops, bytes_accessed=nbytes, transcendentals=0)


def spread(block):
    rest = jnp.zeros((LANES - COPIES * KPAD, LANES), jnp.float32)
    return jnp.concatenate([block] * COPIES + [rest], axis=0).T


def lane_ids(shape):
    return lax.broadcasted_iota(jnp.int32, shape, len(shape) - 1)


def own_table_kernel(cells_ref, out_ref, top_ref):
    @pl.loop(0, cells_ref.shape[1] // LANES)
    def _(k):
        at = pl.multiple_of(k * LANES, LANES)
        out_ref[pl.ds(at, LANES), :] = spread(cells_ref[:, pl.ds(at, LANES)])

    is_first = lane_ids((TOP_ROWS, LANES)) < KPAD
    top_ref[...] = jnp.where(is_first, out_ref[:TOP_ROWS, :], out_ref[TOP_ROWS : 2 * TOP_ROWS, :])


def own_table(cells, rows):
    count = cells.shape[1]
    return pl.pallas_call(
        own_table_kernel,
        grid=(1,),
        out_shape=(
            jax.ShapeDtypeStruct((rows, LANES), jnp.float32),
            jax.ShapeDtypeStruct((TOP_ROWS, LANES), jnp.float32),
        ),
        in_specs=[pl.BlockSpec((KPAD, count), lambda i: (0, 0))],
        out_specs=(
            pl.BlockSpec((count, LANES), lambda i: (0, 0)),
            pl.BlockSpec((TOP_ROWS, LANES), lambda i: (0, 0)),
        ),
        compiler_params=params(),
        cost_estimate=cost(10**6, 12 * 10**6),
        name="own_table",
    )(cells)


def whole_table_kernel(*refs, slot_steps):
    top_ref, out_ref = refs[8], refs[10]
    step = pl.program_id(0)
    for k in range(slot_steps):

        @pl.when(step == k)
        def _():
            at = 0
            for n in (2 * k, 2 * k + 1):
                for c in range(refs[n].shape[1] // LANES):
                    out_ref[at : at + LANES, :] = spread(refs[n][:, c * LANES : (c + 1) * LANES])
                    at += LANES

    rows = out_ref.shape[0]
    total = top_ref.shape[0]
    lanes = lane_ids((rows, LANES))
    for k in range(2 * total // rows):

        @pl.when(step == slot_steps + k)
        def _():
            pieces = []
            for first in range(k * rows, (k + 1) * rows, min(rows, total)):
                group, at = first // total, first % total
                value = top_ref[at : at + min(rows, total), :]
                pieces.append(pltpu.roll(value, LANES - KPAD, 1) if group else value)
            value = jnp.concatenate(pieces, axis=0) if len(pieces) > 1 else pieces[0]
            value = jnp.where(lanes < KPAD, value, 0.0)
            out_ref[...] = value + pltpu.roll(value, KPAD, 1) + pltpu.roll(value, 2 * KPAD, 1)


def whole_table(table, arrived, top_rows):
    slots = arrived[0].shape[1]
    rows = 2 * slots
    own = table.shape[0] - 8 * slots - 2 * top_rows.shape[0]
    first = own // rows
    steps = 4 + 2 * top_rows.shape[0] // rows
    return pl.pallas_call(
        functools.partial(whole_table_kernel, slot_steps=4),
        grid=(steps,),
        out_shape=jax.ShapeDtypeStruct(table.shape, jnp.float32),
        in_specs=[VMEM_WHOLE] * 9 + [pl.BlockSpec(memory_space=pl.ANY)],
        out_specs=pl.BlockSpec((rows, LANES), lambda i: (first + i, 0)),
        input_output_aliases={9: 0},
        compiler_params=params(),
        cost_estimate=cost(10**6, 16 * 10**6),
        name="whole_table",
    )(*arrived, top_rows, table)


def as_rows(table):
    return table.reshape(table.shape[0], 1, LANES)


def pack_kernel(list_ref, count_ref, table_ref, *refs):
    outs, rows = refs[:8], refs[8]
    slot_tiles = list_ref.shape[1] // LANES
    for n in range(8):

        @pl.loop(0, slot_tiles)
        def _(i):
            first = pl.multiple_of(i * LANES, LANES)
            for r in range(LANES):
                rows[r : r + 1, :] = table_ref[list_ref[n, first + r]]
            live = (lane_ids((KPAD, LANES)) + first) < count_ref[n]
            outs[n][:, pl.ds(first, LANES)] = jnp.where(live, rows[...].T[:KPAD], 0.0)


def pack(table, cell_count, proxy_list, proxy_count):
    slots = proxy_list.shape[1]
    return pl.pallas_call(
        pack_kernel,
        grid=(1,),
        out_shape=(jax.ShapeDtypeStruct((KPAD, slots), jnp.float32),) * 8,
        in_specs=[
            SMEM_WHOLE,
            SMEM_WHOLE,
            pl.BlockSpec((cell_count, 1, LANES), lambda i: (0, 0, 0)),
        ],
        out_specs=(pl.BlockSpec((KPAD, slots), lambda i: (0, 0)),) * 8,
        scratch_shapes=[pltpu.VMEM((LANES, LANES), jnp.float32)],
        compiler_params=params(),
        cost_estimate=cost(10**6, 25 * 10**6),
        name="pack",
    )(proxy_list, proxy_count, as_rows(table))


def exchange(blocks, n_gx, n_gy):
    arrived = [None] * 8
    for m, (a, b) in enumerate(OFFSETS):
        pairs = [
            (x * n_gy + y, (x + a) % n_gx * n_gy + (y + b) % n_gy)
            for x in range(n_gx)
            for y in range(n_gy)
        ]
        arrived[7 - m] = lax.ppermute(blocks[m], ("gx", "gy"), pairs)
    return arrived


def order_kernel(packed_ref, out_ref):
    lanes = lane_ids((LANES, LANES))
    within = lanes & (BLOCK - 1)
    base = lanes - within

    @pl.loop(0, packed_ref.shape[0] // LANES)
    def _(k):
        at = pl.ds(pl.multiple_of(k * LANES, LANES), LANES)
        packed = packed_ref[at, :]

        def step(i, ordered):
            value = jnp.take_along_axis(packed, base + i, axis=1, mode="promise_in_bounds")
            return jnp.where((value & (BLOCK - 1)) == within, value, ordered)

        ordered = lax.fori_loop(0, BLOCK, step, jnp.zeros_like(packed), unroll=8)
        out_ref[at, :] = ordered >> SHIFT


def order(packed):
    return pl.pallas_call(
        order_kernel,
        out_shape=jax.ShapeDtypeStruct(packed.shape, jnp.int32),
        in_specs=[VMEM_WHOLE],
        out_specs=VMEM_WHOLE,
        compiler_params=params(),
        cost_estimate=cost(10**6, 20 * 10**6),
        name="order",
    )(packed)


def m2l_kernel(source_ref, class_ref, table_ref, ops_ref, out_ref, *gathered, first, turned):
    step = first + pl.program_id(0)
    lanes = lane_ids((1, LANES))
    in_first = lanes < KPAD
    in_second = lanes < 2 * KPAD

    def row(b, t):
        return table_ref[source_ref[b // 2, (b % 2) * BLOCK + t]]

    for u in range(2):
        for t in range(BLOCK):
            for g in range(3):
                b = u * PER_WINDOW + 3 * g
                one, two = row(b, t), row(b + 1, t)
                three = row(b + 2, t) if g < 2 else two
                gathered[u][g, t : t + 1, :] = jnp.where(
                    in_first, one, jnp.where(in_second, two, three)
                )

    rest = jnp.zeros((LANES - COPIES * KPAD, LANES), jnp.float32)
    none = jnp.zeros((KPAD, LANES), jnp.float32)
    results = []
    for u in range(2):
        total = jnp.zeros((BLOCK, LANES), jnp.float32)
        for g in range(3):
            held = []
            for s in range(3):
                b = 3 * g + s
                if b < PER_WINDOW:
                    held.append(ops_ref[class_ref[step * 2 * PER_WINDOW + u * PER_WINDOW + b]])
                else:
                    held.append(none)
            weights = jnp.concatenate(held + [rest], axis=0).astype(jnp.bfloat16)
            values = gathered[u][g]
            high = values.astype(jnp.bfloat16)
            low = (values - high.astype(jnp.float32)).astype(jnp.bfloat16)
            total += jnp.dot(high, weights, preferred_element_type=jnp.float32)
            total += jnp.dot(low, weights, preferred_element_type=jnp.float32)
        results.append(total)
    both = jnp.concatenate(results, axis=0)
    both = both + pltpu.roll(both, LANES - KPAD, 1)
    if turned:
        out_ref[0] = both.T[:KPAD]
    else:
        out_ref[...] = both


def m2l(sources, classes, table, ops, first, steps, turned, slots):
    if turned:
        per = slots // LANES
        shape = (steps // per, KPAD, slots)
        out_spec = pl.BlockSpec((1, KPAD, LANES), lambda i: (i // per, 0, i % per))
    else:
        shape = (steps * LANES, LANES)
        out_spec = pl.BlockSpec((LANES, LANES), lambda i: (i, 0))
    return pl.pallas_call(
        functools.partial(m2l_kernel, first=first, turned=turned),
        grid=(steps,),
        out_shape=jax.ShapeDtypeStruct(shape, jnp.float32),
        in_specs=[
            pl.BlockSpec((8, LANES), lambda i: (first + i, 0), memory_space=pltpu.SMEM),
            SMEM_WHOLE,
            VMEM_WHOLE,
            VMEM_WHOLE,
        ],
        out_specs=out_spec,
        scratch_shapes=[pltpu.VMEM((3, BLOCK, LANES), jnp.float32)] * 2,
        compiler_params=params(),
        cost_estimate=cost(10**6, 150 * 10**6),
        name="m2l_slots" if turned else "m2l_cells",
    )(sources, classes, as_rows(table), ops)


def add_back_kernel(list_ref, count_ref, own_ref, *refs):
    slot_refs, out_ref = refs[:8], refs[8]
    rows, sums = refs[9], refs[10:]
    slots = list_ref.shape[1]
    sums[0][...] = own_ref[...]
    for held in sums[1:]:
        held[...] = jnp.zeros_like(held)
    for n in range(8):
        for k in range(slots // LANES):
            live = (lane_ids((KPAD, LANES)) + k * LANES) < count_ref[n]
            values = jnp.where(live, slot_refs[n][:, k * LANES : (k + 1) * LANES], 0.0)
            at = n * slots + k * LANES
            rows[at : at + LANES, :] = spread(values)

    @pl.loop(0, slots, step=4)
    def _(first):
        for j in range(4):
            to = [pl.ds(list_ref[n, first + j], 1) for n in range(8)]
            old = [sums[n][to[n], :] for n in range(8)]
            new = [old[n] + rows[pl.ds(n * slots + first + j, 1), :] for n in range(8)]
            for n in range(8):
                sums[n][to[n], :] = new[n]

    @pl.loop(0, own_ref.shape[0] // LANES)
    def _(k):
        at = pl.ds(pl.multiple_of(k * LANES, LANES), LANES)
        parts = [held[at, :] for held in sums]
        while len(parts) > 1:
            parts = [a + b for a, b in zip(parts[::2], parts[1::2])]
        out_ref[:, at] = parts[0].T[: out_ref.shape[0]]


def add_back(proxy_list, proxy_count, own_rows, slot_fields, coef_count):
    cell_count = own_rows.shape[0]
    slots = proxy_list.shape[1]
    return pl.pallas_call(
        add_back_kernel,
        out_shape=jax.ShapeDtypeStruct((coef_count, cell_count), jnp.float32),
        in_specs=[SMEM_WHOLE, SMEM_WHOLE] + [VMEM_WHOLE] * 9,
        out_specs=VMEM_WHOLE,
        scratch_shapes=[pltpu.VMEM((8 * slots, LANES), jnp.float32)]
        + [pltpu.VMEM((cell_count, LANES), jnp.float32)] * 8,
        compiler_params=params(),
        cost_estimate=cost(10**6, 30 * 10**6),
        name="add_back",
    )(proxy_list, proxy_count, own_rows, *slot_fields)


def carve_kernel(mesh_ref, out_ref, sems, *, first):
    sources, count, rows, width = out_ref.shape
    copies = [
        pltpu.make_async_copy(
            mesh_ref.at[pl.ds(first, count), pl.ds(s * rows, rows), :], out_ref.at[s], sems.at[s]
        )
        for s in range(sources)
    ]
    for copy in copies:
        copy.start()
    for copy in copies:
        copy.wait()


def carve(mesh, first, count, sources):
    rows, width = mesh.shape[1] // sources, mesh.shape[2]
    return pl.pallas_call(
        functools.partial(carve_kernel, first=first),
        out_shape=jax.ShapeDtypeStruct((sources, count, rows, width), jnp.float32),
        in_specs=[pl.BlockSpec(memory_space=pl.ANY)],
        out_specs=pl.BlockSpec(memory_space=pl.ANY),
        scratch_shapes=[pltpu.SemaphoreType.DMA((sources,))],
        compiler_params=params(),
        cost_estimate=cost(0, 8 * count * sources * rows * width),
        name="carve",
    )(mesh)


def deposit_kernel(code_ref, value_ref, *refs):
    sources = code_ref.shape[0]
    outs, others = refs[:sources], refs[sources:]
    lanes = lane_ids((1, LANES))
    for held in refs:
        held[...] = jnp.zeros_like(held)
    half = code_ref.shape[1] // 2

    @pl.loop(0, half, step=4)
    def _(first):
        for j in range(4):
            at = [(s, first + j + h * half) for h in range(2) for s in range(sources)]
            codes = [code_ref[i] for i in at]
            to = [pl.ds(code >> LANE_SHIFT, 1) for code in codes]
            old = [held[rows, :] for held, rows in zip(refs, to)]
            new = [
                row + jnp.where(lanes == (code & (LANES - 1)), value_ref[i], 0.0)
                for row, code, i in zip(old, codes, at)
            ]
            for held, rows, row in zip(refs, to, new):
                held[rows, :] = row

    for out_ref, held in zip(outs, others):
        out_ref[...] = out_ref[...] + held[...]


def deposit(codes, values, rows):
    sources = codes.shape[0]
    return pl.pallas_call(
        deposit_kernel,
        out_shape=(jax.ShapeDtypeStruct((rows, LANES), jnp.float32),) * sources,
        in_specs=[SMEM_WHOLE, SMEM_WHOLE],
        out_specs=(VMEM_WHOLE,) * sources,
        scratch_shapes=[pltpu.VMEM((rows, LANES), jnp.float32)] * sources,
        compiler_params=params(),
        cost_estimate=cost(10**6, 75 * 10**6),
        name="deposit",
    )(codes, values)


def fourier_tables(length):
    points, half = length // 2, length // 4
    positions = np.arange(points)
    scale = 1.0 / np.sqrt(length)
    parts = []
    for odd in range(2):
        ks = 2 * np.arange(half) + odd
        angles = (positions[:, None] * ks[None, :] % length) * (2.0 * np.pi / length)
        imag = -np.sin(angles) * scale
        if not odd:
            imag[:, 0] = np.where(positions % 2 == 0, scale, -scale)
        parts.append(np.concatenate([np.cos(angles) * scale, imag], axis=1))
    whole = np.stack(parts)
    high = whole.astype(ml_dtypes.bfloat16)
    low = (whole - high.astype(np.float64)).astype(ml_dtypes.bfloat16)
    return high, low


def fourier_kernel(*refs, sources):
    mesh_ref, add_refs = refs[0], refs[1 : 1 + sources]
    high_ref, low_ref = refs[1 + sources], refs[2 + sources]
    out_ref = refs[-1]
    rows, width = mesh_ref.shape[1:]
    pieces = []
    for s in range(sources):
        for h in range(width // LANES):
            pieces.append(
                mesh_ref[s, :, h * LANES : (h + 1) * LANES]
                + add_refs[s][h * rows : (h + 1) * rows, :]
            )
    mid = len(pieces) // 2
    halves = []
    for odd in range(2):
        if odd:
            folded = [a - b for a, b in zip(pieces[:mid], pieces[mid:])]
        else:
            folded = [a + b for a, b in zip(pieces[:mid], pieces[mid:])]
        values = jnp.concatenate(folded, axis=1)
        high = values.astype(jnp.bfloat16)
        low = (values - high.astype(jnp.float32)).astype(jnp.bfloat16)
        both = jnp.dot(
            jnp.concatenate([high, low], axis=0), high_ref[odd], preferred_element_type=jnp.float32
        )
        halves.append(
            both[:rows]
            + both[rows:]
            + jnp.dot(high, low_ref[odd], preferred_element_type=jnp.float32)
        )
    lanes = lane_ids((rows, LANES))
    is_first = lanes == 0
    is_odd = (lanes & 1) == 1
    steps = lanes >> 1
    tiles = len(pieces)
    per = tiles // 4

    def tile(odd, part, j):
        at = (part * per + j) * LANES
        return halves[odd][:, at : at + LANES]

    def pick(value, lane):
        return jnp.take_along_axis(value, lane, axis=1, mode="promise_in_bounds")

    for j in range(tiles):
        for part in range(2):
            if j < tiles // 2:
                at = BLOCK * j
                lane = (at % LANES) + steps
                even = pick(tile(0, part, at // LANES), lane)
                odd = pick(tile(1, part, at // LANES), lane)
                if j == 0 and part == 1:
                    even = jnp.where(is_first, 0.0, even)
            else:
                at = BLOCK * (tiles - j)
                last = (at - 1) // LANES
                even = pick(tile(0, part, last), (at - steps) & (LANES - 1))
                odd = pick(tile(1, part, last), ((at - 1) % LANES) - steps)
                if at % LANES == 0 and j > tiles // 2:
                    even = jnp.where(is_first, tile(0, part, at // LANES), even)
                if part == 1:
                    even, odd = -even, -odd
                if j == tiles // 2:
                    even = jnp.where(is_first, 0.0 if part else tile(0, 1, 0), even)
            out_ref[part, 0, :, j * LANES : (j + 1) * LANES] = jnp.where(is_odd, odd, even)


def fourier(mesh_part, count, adds, tables, first, planes, so_far, rows):
    sources, _, width = mesh_part.shape
    length = sources * width
    add_rows = (width // LANES) * rows
    operands = [mesh_part, *adds, *tables]
    in_specs = (
        [pl.BlockSpec((sources, rows, width), lambda p: (0, p, 0))]
        + [pl.BlockSpec((add_rows, LANES), lambda p: (first + p, 0))] * sources
        + [
            pl.BlockSpec((2, length // 2, length // 2), lambda p: (0, 0, 0), pipeline_mode=pl.Buffered(1))
        ]
        * 2
    )
    aliases = {}
    if so_far is not None:
        aliases = {len(operands): 0}
        operands.append(so_far)
        in_specs.append(pl.BlockSpec(memory_space=pl.ANY))
    return pl.pallas_call(
        functools.partial(fourier_kernel, sources=sources),
        grid=(count,),
        out_shape=jax.ShapeDtypeStruct((2, planes, rows, length), jnp.float32),
        in_specs=in_specs,
        out_specs=pl.BlockSpec((2, 1, rows, length), lambda p: (0, first + p, 0, 0)),
        input_output_aliases=aliases,
        compiler_params=params(),
        cost_estimate=cost(10**6, count * 10 * 10**6),
        name="fourier",
    )(*operands)


def after(value, *others):
    return lax.optimization_barrier((value, *others))[0]


def on_device(
    multipoles,
    proxy_list,
    proxy_count,
    pair_source,
    pair_target,
    block_class,
    m2l_ops,
    cell_mesh,
    pm_density,
    *,
    n_gx,
    n_gy,
):
    coef_count, cell_count = multipoles.shape
    slots = proxy_list.shape[2]
    planes, mesh_rows, width = pm_density.shape
    own_rows = mesh_rows // n_gx
    domains = n_gx * n_gy
    lists, counts = proxy_list[0], proxy_count[0]

    def send(part):
        return lax.all_to_all(part, "gx", 0, 0, tiled=True)

    spans = []
    first = 0
    for size in CHUNKS:
        spans.append((first, size))
        first += size

    held = jnp.stack([cell_mesh.astype(jnp.float32), DEPOSIT_SCALE * multipoles[0]])
    held = held.reshape(1, -1, width)
    start = pm_density[0].reshape(n_gx, own_rows, width)
    parts = [send(jnp.concatenate([start, jnp.broadcast_to(held, (n_gx, *held.shape[1:]))], axis=1))]
    carved = [
        carve(pm_density, at, size, n_gx).reshape(n_gx, size * own_rows, width)
        for at, size in spans[1:]
    ]

    cells = jnp.pad(multipoles, ((0, KPAD - coef_count), (0, 0)))
    base = cell_count + 8 * slots
    table, top_own = own_table(cells, base + TOP * domains)
    outgoing = pack(table, cell_count, lists, counts)
    arrived = exchange(outgoing, n_gx, n_gy)

    top = pair_source - base
    top = base + ((top >> 4) & 1) * (TOP_ROWS * domains) + (top >> 5) * TOP_ROWS + (top & 15)
    wanted = jnp.where(pair_source < base, pair_source, top)
    sources = order(((wanted << SHIFT) | (pair_target & (BLOCK - 1))).reshape(-1, LANES))

    turned_ops = jnp.pad(
        m2l_ops.transpose(0, 2, 1), ((0, 0), (0, KPAD - coef_count), (0, KPAD - coef_count))
    )
    high = lax.reduce_precision(turned_ops, 8, 7)
    ops = jnp.concatenate([high, turned_ops - high], axis=2)
    ops = jnp.pad(ops, ((0, 0), (0, 0), (0, LANES - 2 * KPAD)))

    tops = jnp.broadcast_to(top_own, (domains, TOP_ROWS, LANES))
    tops = after(tops, parts[0], outgoing[0], sources, ops)
    tops = lax.all_to_all(tops, ("gx", "gy"), 0, 0, tiled=True)
    parts.append(send(after(carved[0], tops)))

    near = parts[0][:, own_rows:].reshape(n_gx, 2, cell_count)
    place = near[:, 0].astype(jnp.int32)
    plane = place // (mesh_rows * width)
    row = place // width % mesh_rows
    column = place % width
    tiles = width // LANES
    add_rows = planes * tiles * own_rows
    at_row = (plane * tiles + column // LANES) * own_rows + row % own_rows
    mine = row // own_rows == lax.axis_index("gx")
    codes = jnp.where(mine, at_row, add_rows) * LANES + column % LANES
    adds = deposit(codes, near[:, 1], add_rows + 8)

    table = whole_table(table, arrived, tops.reshape(-1, LANES))
    cell_steps = cell_count // LANES
    slot_steps = 8 * slots // LANES
    slot_fields = m2l(sources, block_class, table, ops, cell_steps, slot_steps, True, slots)
    returned = exchange([slot_fields[m] for m in range(8)], n_gx, n_gy)
    parts.append(send(after(carved[1], parts[1], slot_fields, adds[0])))
    own_fields = m2l(sources, block_class, table, ops, 0, cell_steps, False, slots)

    tables = fourier_tables(n_gx * width)
    spectrum = None
    for i, (at, size) in enumerate(spans):
        if i == 2:
            parts.append(send(after(carved[2], parts[2], own_fields, spectrum)))
        spectrum = fourier(parts[i], size, adds, tables, at, planes, spectrum, own_rows)

    field_tensors = add_back(lists, counts, own_fields, returned, coef_count)
    return (field_tensors, spectrum)


def solution(mesh):
    placed = (
        P(None, ("gx", "gy")),
        P(("gx", "gy"), None, None),
        P(("gx", "gy"), None),
        P(("gx", "gy")),
        P(("gx", "gy")),
        P(("gx", "gy")),
        P(),
        P(("gx", "gy")),
        P("gy", None, "gx"),
    )
    return jax.shard_map(
        functools.partial(on_device, n_gx=mesh.shape["gx"], n_gy=mesh.shape["gy"]),
        mesh=mesh,
        in_specs=placed,
        out_specs=(P(None, ("gx", "gy")), P(None, "gy", "gx", None)),
        check_vma=False,
    )
```

```python
import functools

import jax
import jax.numpy as jnp
import ml_dtypes
import numpy as np
from jax import lax
from jax.experimental import pallas as pl
from jax.experimental.pallas import tpu as pltpu
from jax.sharding import PartitionSpec as P

TOP = 32
BLOCK = 64
LANES = 128
KPAD = 40
COPIES = 3
PER_WINDOW = 8
SHIFT = 6
LANE_SHIFT = 7
VMEM_BYTES = 48 * 1024 * 1024
CHUNKS = (1, 2, 4, 1)
TOP_ROWS = TOP // 2

DEPOSIT_SCALE = 8.0
OFFSETS = tuple((a, b) for a in (-1, 0, 1) for b in (-1, 0, 1) if (a, b) != (0, 0))

SMEM_WHOLE = pl.BlockSpec(memory_space=pltpu.SMEM)
VMEM_WHOLE = pl.BlockSpec(memory_space=pltpu.VMEM)


def params():
    return pltpu.CompilerParams(vmem_limit_bytes=VMEM_BYTES)


def cost(flops, nbytes):
    return pl.CostEstimate(flops=flops, bytes_accessed=nbytes, transcendentals=0)


def spread(block):
    rest = jnp.zeros((LANES - COPIES * KPAD, LANES), jnp.float32)
    return jnp.concatenate([block] * COPIES + [rest], axis=0).T


def lane_ids(shape):
    return lax.broadcasted_iota(jnp.int32, shape, len(shape) - 1)


def own_table_kernel(cells_ref, out_ref):
    @pl.loop(0, cells_ref.shape[1] // LANES)
    def _(k):
        at = pl.multiple_of(k * LANES, LANES)
        out_ref[pl.ds(at, LANES), :] = spread(cells_ref[:, pl.ds(at, LANES)])


def own_table(cells, rows):
    count = cells.shape[1]
    return pl.pallas_call(
        own_table_kernel,
        grid=(1,),
        out_shape=jax.ShapeDtypeStruct((rows, LANES), jnp.float32),
        in_specs=[pl.BlockSpec((KPAD, count), lambda i: (0, 0))],
        out_specs=pl.BlockSpec((count, LANES), lambda i: (0, 0)),
        compiler_params=params(),
        cost_estimate=cost(10**6, 12 * 10**6),
        name="own_table",
    )(cells)


def cut_rows(refs, first, stop):
    pieces, at = [], 0
    for ref in refs:
        low, high = max(first - at, 0), min(stop - at, ref.shape[0])
        if low < high:
            pieces.append(ref[low:high, :])
        at += ref.shape[0]
    return jnp.concatenate(pieces, axis=0) if len(pieces) > 1 else pieces[0]


def whole_table_kernel(*refs, slot_steps):
    top_refs, out_ref = refs[8:-2], refs[-1]
    step = pl.program_id(0)
    for k in range(slot_steps):

        @pl.when(step == k)
        def _():
            at = 0
            for n in (2 * k, 2 * k + 1):
                for c in range(refs[n].shape[1] // LANES):
                    out_ref[at : at + LANES, :] = spread(refs[n][:, c * LANES : (c + 1) * LANES])
                    at += LANES

    rows = out_ref.shape[0]
    total = sum(ref.shape[0] for ref in top_refs)
    lanes = lane_ids((rows, LANES))
    for k in range(2 * total // rows):

        @pl.when(step == slot_steps + k)
        def _():
            pieces = []
            for first in range(k * rows, (k + 1) * rows, min(rows, total)):
                group, at = first // total, first % total
                value = cut_rows(top_refs, at, at + min(rows, total))
                pieces.append(pltpu.roll(value, LANES - KPAD, 1) if group else value)
            value = jnp.concatenate(pieces, axis=0) if len(pieces) > 1 else pieces[0]
            value = jnp.where(lanes < KPAD, value, 0.0)
            out_ref[...] = value + pltpu.roll(value, KPAD, 1) + pltpu.roll(value, 2 * KPAD, 1)


def whole_table(table, arrived, tops):
    slots = arrived[0].shape[1]
    rows = 2 * slots
    top_rows = 2 * sum(part.shape[0] for part in tops)
    first = (table.shape[0] - 8 * slots - top_rows) // rows
    return pl.pallas_call(
        functools.partial(whole_table_kernel, slot_steps=4),
        grid=(4 + top_rows // rows,),
        out_shape=jax.ShapeDtypeStruct(table.shape, jnp.float32),
        in_specs=[VMEM_WHOLE] * (8 + len(tops)) + [pl.BlockSpec(memory_space=pl.ANY)],
        out_specs=pl.BlockSpec((rows, LANES), lambda i: (first + i, 0)),
        input_output_aliases={8 + len(tops): 0},
        compiler_params=params(),
        cost_estimate=cost(10**6, 16 * 10**6),
        name="whole_table",
    )(*arrived, *tops, table)


def as_rows(table):
    return table.reshape(table.shape[0], 1, LANES)


def pack_kernel(list_ref, count_ref, table_ref, *refs):
    outs, held = refs[:8], refs[8:]
    slot_tiles = list_ref.shape[1] // LANES
    for n in range(8):

        @pl.loop(0, slot_tiles, step=len(held))
        def _(i):
            firsts = [pl.multiple_of((i + k) * LANES, LANES) for k in range(len(held))]
            for first, rows in zip(firsts, held):
                for r in range(LANES):
                    rows[r : r + 1, :] = table_ref[list_ref[n, first + r]]
            for first, rows in zip(firsts, held):
                live = (lane_ids((KPAD, LANES)) + first) < count_ref[n]
                outs[n][:, pl.ds(first, LANES)] = jnp.where(live, rows[...].T[:KPAD], 0.0)


def pack(table, cell_count, proxy_list, proxy_count):
    slots = proxy_list.shape[1]
    return pl.pallas_call(
        pack_kernel,
        grid=(1,),
        out_shape=(jax.ShapeDtypeStruct((KPAD, slots), jnp.float32),) * 8,
        in_specs=[
            SMEM_WHOLE,
            SMEM_WHOLE,
            pl.BlockSpec((cell_count, 1, LANES), lambda i: (0, 0, 0)),
        ],
        out_specs=(pl.BlockSpec((KPAD, slots), lambda i: (0, 0)),) * 8,
        scratch_shapes=[pltpu.VMEM((LANES, LANES), jnp.float32)] * 2,
        compiler_params=params(),
        cost_estimate=cost(10**6, 25 * 10**6),
        name="pack",
    )(proxy_list, proxy_count, as_rows(table))


def exchange(blocks, n_gx, n_gy):
    arrived = [None] * 8
    for m, (a, b) in enumerate(OFFSETS):
        pairs = [
            (x * n_gy + y, (x + a) % n_gx * n_gy + (y + b) % n_gy)
            for x in range(n_gx)
            for y in range(n_gy)
        ]
        arrived[7 - m] = lax.ppermute(blocks[m], ("gx", "gy"), pairs)
    return arrived


def order_kernel(packed_ref, out_ref):
    lanes = lane_ids((LANES, LANES))
    within = lanes & (BLOCK - 1)
    base = lanes - within

    @pl.loop(0, packed_ref.shape[0] // LANES)
    def _(k):
        at = pl.ds(pl.multiple_of(k * LANES, LANES), LANES)
        packed = packed_ref[at, :]

        def step(i, ordered):
            value = jnp.take_along_axis(packed, base + i, axis=1, mode="promise_in_bounds")
            return jnp.where((value & (BLOCK - 1)) == within, value, ordered)

        ordered = lax.fori_loop(0, BLOCK, step, jnp.zeros_like(packed), unroll=8)
        out_ref[at, :] = ordered >> SHIFT


def order(packed):
    return pl.pallas_call(
        order_kernel,
        out_shape=jax.ShapeDtypeStruct(packed.shape, jnp.int32),
        in_specs=[VMEM_WHOLE],
        out_specs=VMEM_WHOLE,
        compiler_params=params(),
        cost_estimate=cost(10**6, 20 * 10**6),
        name="order",
    )(packed)


def m2l_kernel(source_ref, class_ref, table_ref, ops_ref, out_ref, *gathered, first, turned):
    step = first + pl.program_id(0)
    lanes = lane_ids((1, LANES))
    in_first = lanes < KPAD
    in_second = lanes < 2 * KPAD

    def row(b, t):
        return table_ref[source_ref[b // 2, (b % 2) * BLOCK + t]]

    for u in range(2):
        for t in range(BLOCK):
            for g in range(3):
                b = u * PER_WINDOW + 3 * g
                one, two = row(b, t), row(b + 1, t)
                three = row(b + 2, t) if g < 2 else two
                gathered[u][g, t : t + 1, :] = jnp.where(
                    in_first, one, jnp.where(in_second, two, three)
                )

    rest = jnp.zeros((LANES - COPIES * KPAD, LANES), jnp.float32)
    none = jnp.zeros((KPAD, LANES), jnp.float32)
    results = []
    for u in range(2):
        total = jnp.zeros((BLOCK, LANES), jnp.float32)
        for g in range(3):
            held = []
            for s in range(3):
                b = 3 * g + s
                if b < PER_WINDOW:
                    held.append(ops_ref[class_ref[step * 2 * PER_WINDOW + u * PER_WINDOW + b]])
                else:
                    held.append(none)
            weights = jnp.concatenate(held + [rest], axis=0).astype(jnp.bfloat16)
            values = gathered[u][g]
            high = values.astype(jnp.bfloat16)
            low = (values - high.astype(jnp.float32)).astype(jnp.bfloat16)
            total += jnp.dot(high, weights, preferred_element_type=jnp.float32)
            total += jnp.dot(low, weights, preferred_element_type=jnp.float32)
        results.append(total)
    both = jnp.concatenate(results, axis=0)
    both = both + pltpu.roll(both, LANES - KPAD, 1)
    if turned:
        out_ref[0] = both.T[:KPAD]
    else:
        out_ref[...] = both


def m2l(sources, classes, table, ops, first, steps, turned, slots):
    if turned:
        per = slots // LANES
        shape = (steps // per, KPAD, slots)
        out_spec = pl.BlockSpec((1, KPAD, LANES), lambda i: (i // per, 0, i % per))
    else:
        shape = (steps * LANES, LANES)
        out_spec = pl.BlockSpec((LANES, LANES), lambda i: (i, 0))
    return pl.pallas_call(
        functools.partial(m2l_kernel, first=first, turned=turned),
        grid=(steps,),
        out_shape=jax.ShapeDtypeStruct(shape, jnp.float32),
        in_specs=[
            pl.BlockSpec((8, LANES), lambda i: (first + i, 0), memory_space=pltpu.SMEM),
            SMEM_WHOLE,
            VMEM_WHOLE,
            VMEM_WHOLE,
        ],
        out_specs=out_spec,
        scratch_shapes=[pltpu.VMEM((3, BLOCK, LANES), jnp.float32)] * 2,
        compiler_params=params(),
        cost_estimate=cost(10**6, 150 * 10**6),
        name="m2l_slots" if turned else "m2l_cells",
    )(sources, classes, as_rows(table), ops)


def add_back_kernel(list_ref, count_ref, own_ref, *refs):
    slot_refs, out_ref = refs[:8], refs[8]
    rows, sums = refs[9], refs[10:]
    slots = list_ref.shape[1]
    sums[0][...] = own_ref[...]
    for held in sums[1:]:
        held[...] = jnp.zeros_like(held)
    for n in range(8):
        for k in range(slots // LANES):
            live = (lane_ids((KPAD, LANES)) + k * LANES) < count_ref[n]
            values = jnp.where(live, slot_refs[n][:, k * LANES : (k + 1) * LANES], 0.0)
            at = n * slots + k * LANES
            rows[at : at + LANES, :] = spread(values)

    @pl.loop(0, slots, step=4)
    def _(first):
        for j in range(4):
            to = [pl.ds(list_ref[n, first + j], 1) for n in range(8)]
            old = [sums[n][to[n], :] for n in range(8)]
            new = [old[n] + rows[pl.ds(n * slots + first + j, 1), :] for n in range(8)]
            for n in range(8):
                sums[n][to[n], :] = new[n]

    @pl.loop(0, own_ref.shape[0] // LANES)
    def _(k):
        at = pl.ds(pl.multiple_of(k * LANES, LANES), LANES)
        parts = [held[at, :] for held in sums]
        while len(parts) > 1:
            parts = [a + b for a, b in zip(parts[::2], parts[1::2])]
        out_ref[:, at] = parts[0].T[: out_ref.shape[0]]


def add_back(proxy_list, proxy_count, own_rows, slot_fields, coef_count):
    cell_count = own_rows.shape[0]
    slots = proxy_list.shape[1]
    return pl.pallas_call(
        add_back_kernel,
        out_shape=jax.ShapeDtypeStruct((coef_count, cell_count), jnp.float32),
        in_specs=[SMEM_WHOLE, SMEM_WHOLE] + [VMEM_WHOLE] * 9,
        out_specs=VMEM_WHOLE,
        scratch_shapes=[pltpu.VMEM((8 * slots, LANES), jnp.float32)]
        + [pltpu.VMEM((cell_count, LANES), jnp.float32)] * 8,
        compiler_params=params(),
        cost_estimate=cost(10**6, 30 * 10**6),
        name="add_back",
    )(proxy_list, proxy_count, own_rows, *slot_fields)


def carve_kernel(mesh_ref, out_ref, sems, *, first):
    sources, count, rows, width = out_ref.shape
    copies = [
        pltpu.make_async_copy(
            mesh_ref.at[pl.ds(first, count), pl.ds(s * rows, rows), :], out_ref.at[s], sems.at[s]
        )
        for s in range(sources)
    ]
    for copy in copies:
        copy.start()
    for copy in copies:
        copy.wait()


def carve(mesh, first, count, sources):
    rows, width = mesh.shape[1] // sources, mesh.shape[2]
    return pl.pallas_call(
        functools.partial(carve_kernel, first=first),
        out_shape=jax.ShapeDtypeStruct((sources, count, rows, width), jnp.float32),
        in_specs=[pl.BlockSpec(memory_space=pl.ANY)],
        out_specs=pl.BlockSpec(memory_space=pl.ANY),
        scratch_shapes=[pltpu.SemaphoreType.DMA((sources,))],
        compiler_params=params(),
        cost_estimate=cost(0, 8 * count * sources * rows * width),
        name="carve",
    )(mesh)


def first_part_kernel(mesh_ref, place_ref, cells_ref, out_ref, ride, sems):
    sources, whole_rows, width = out_ref.shape
    extra = ride.shape[0]
    rows = whole_rows - extra
    copies = [
        pltpu.make_async_copy(
            mesh_ref.at[0, pl.ds(s * rows, rows), :], out_ref.at[s, pl.ds(0, rows), :], sems.at[s]
        )
        for s in range(sources)
    ]
    for copy in copies:
        copy.start()
    is_first = lane_ids((TOP_ROWS, LANES)) < KPAD
    table = spread(jnp.concatenate([cells_ref[:, :LANES], jnp.zeros((KPAD - cells_ref.shape[0], LANES), jnp.float32)], axis=0))
    top = jnp.where(is_first, table[:TOP_ROWS, :], table[TOP_ROWS : 2 * TOP_ROWS, :])
    blocks = [place_ref[...].astype(jnp.float32), cell_lines(cells_ref), top]
    at = 0
    for block in blocks:
        high = block.shape[0] * LANES // width
        for h in range(width // LANES):
            ride[at : at + high, h * LANES : (h + 1) * LANES] = block[h * high : (h + 1) * high, :]
        at += high
    more = [
        pltpu.make_async_copy(ride, out_ref.at[s, pl.ds(rows, extra), :], sems.at[sources + s])
        for s in range(sources)
    ]
    for copy in more:
        copy.start()
    for copy in copies + more:
        copy.wait()


def cell_lines(cells_ref):
    lines = [cells_ref[0:1, k : k + LANES] for k in range(0, cells_ref.shape[1], LANES)]
    return DEPOSIT_SCALE * jnp.concatenate(lines, axis=0)


def first_part(mesh, place, multipoles, sources):
    rows, width = mesh.shape[1] // sources, mesh.shape[2]
    extra = (2 * place.size + TOP_ROWS * LANES) // width
    return pl.pallas_call(
        first_part_kernel,
        out_shape=jax.ShapeDtypeStruct((sources, rows + extra, width), jnp.float32),
        in_specs=[pl.BlockSpec(memory_space=pl.ANY), VMEM_WHOLE, VMEM_WHOLE],
        out_specs=pl.BlockSpec(memory_space=pl.ANY),
        scratch_shapes=[
            pltpu.VMEM((extra, width), jnp.float32),
            pltpu.SemaphoreType.DMA((2 * sources,)),
        ],
        compiler_params=params(),
        cost_estimate=cost(0, 8 * sources * rows * width),
        name="first_part",
    )(mesh, place.reshape(-1, LANES), multipoles)


def log2(value):
    return value.bit_length() - 1


def sift_kernel(mine_ref, part_ref, code_ref, value_ref, bound_ref, top_ref, ride, sem, *, planes, rows):
    sources, extra, width = ride.shape
    lines = code_ref.shape[0] // sources
    copy = pltpu.make_async_copy(part_ref.at[:, pl.ds(rows, extra), :], ride, sem)
    copy.start()
    copy.wait()

    def unfold(first, count):
        high = count * LANES // width
        return jnp.concatenate(
            [
                ride[s, first : first + high, h * LANES : (h + 1) * LANES]
                for s in range(sources)
                for h in range(width // LANES)
            ],
            axis=0,
        )

    step = lines * LANES // width
    place = unfold(0, lines).astype(jnp.int32)
    value = unfold(step, lines)
    top_ref[...] = unfold(2 * step, TOP_ROWS)

    row_at, mesh_rows = log2(width), rows * sources
    plane = place >> (row_at + log2(mesh_rows))
    row = (place >> row_at) & (mesh_rows - 1)
    column = place & (width - 1)
    tiles = width // LANES
    target = (plane * tiles + (column >> LANE_SHIFT)) * rows + (row & (rows - 1))
    none = planes * tiles * rows * LANES
    mine = (row >> log2(rows)) == mine_ref[0]
    lanes = lane_ids(place.shape)
    code = jnp.where(mine, target * LANES + (column & (LANES - 1)), none)
    value = jnp.where(mine, value, 0.0)
    ahead = jnp.where(mine, 1, 0)
    for b in range(LANE_SHIFT):
        ahead = ahead + jnp.where(lanes >= (1 << b), pltpu.roll(ahead, 1 << b, 1), 0)
    shift = jnp.where(mine, lanes + 1 - ahead, 0)
    for b in range(LANE_SHIFT):
        back = LANES - (1 << b)
        moves = (shift >> b) & 1
        comes = pltpu.roll(moves, back, 1) == 1
        goes = moves == 1
        code = jnp.where(comes, pltpu.roll(code, back, 1), jnp.where(goes, none, code))
        value = jnp.where(comes, pltpu.roll(value, back, 1), jnp.where(goes, 0.0, value))
        shift = jnp.where(comes, pltpu.roll(shift, back, 1), jnp.where(goes, 0, shift))
    code_ref[...] = code
    value_ref[...] = value
    counts = jnp.sum(jnp.where(mine, 1.0, 0.0), axis=1, keepdims=True)
    counts = jnp.broadcast_to(counts, mine.shape).reshape(2 * sources, lines // 2, LANES)
    bound_ref[...] = jnp.max(counts, axis=0).astype(jnp.int32)


def sift(part, mine, planes, rows, lines):
    sources, whole_rows, width = part.shape
    extra = whole_rows - rows
    shape = (sources * lines, LANES)
    return pl.pallas_call(
        functools.partial(sift_kernel, planes=planes, rows=rows),
        out_shape=(
            jax.ShapeDtypeStruct(shape, jnp.int32),
            jax.ShapeDtypeStruct(shape, jnp.float32),
            jax.ShapeDtypeStruct((lines // 2, LANES), jnp.int32),
            jax.ShapeDtypeStruct((sources * TOP_ROWS, LANES), jnp.float32),
        ),
        in_specs=[SMEM_WHOLE, pl.BlockSpec(memory_space=pl.ANY)],
        out_specs=(VMEM_WHOLE,) * 4,
        scratch_shapes=[pltpu.VMEM((sources, extra, width), jnp.float32), pltpu.SemaphoreType.DMA],
        compiler_params=params(),
        cost_estimate=cost(10**6, 8 * 10**6),
        name="sift",
    )(mine, part)


def deposit_kernel(code_ref, value_ref, bound_ref, *refs):
    sources = len(refs) // 2
    outs, others = refs[:sources], refs[sources:]
    lines = code_ref.shape[0] // (2 * sources)
    lanes = lane_ids((1, LANES))
    for held in refs:
        held[...] = jnp.zeros_like(held)

    def line(g, _):
        def one(j, _):
            at = [((2 * s + h) * lines + g, j) for h in range(2) for s in range(sources)]
            codes = [code_ref[i] for i in at]
            to = [pl.ds(code >> LANE_SHIFT, 1) for code in codes]
            old = [held[rows, :] for held, rows in zip(refs, to)]
            new = [
                row + jnp.where(lanes == (code & (LANES - 1)), value_ref[i], 0.0)
                for row, code, i in zip(old, codes, at)
            ]
            for held, rows, row in zip(refs, to, new):
                held[rows, :] = row
            return 0

        return lax.fori_loop(0, bound_ref[g, 0], one, 0)

    lax.fori_loop(0, lines, line, 0)
    for out_ref, held in zip(outs, others):
        out_ref[...] = out_ref[...] + held[...]


def deposit(codes, values, bounds, rows, sources):
    return pl.pallas_call(
        deposit_kernel,
        out_shape=(jax.ShapeDtypeStruct((rows, LANES), jnp.float32),) * sources,
        in_specs=[SMEM_WHOLE] * 3,
        out_specs=(VMEM_WHOLE,) * sources,
        scratch_shapes=[pltpu.VMEM((rows, LANES), jnp.float32)] * sources,
        compiler_params=params(),
        cost_estimate=cost(10**6, 40 * 10**6),
        name="deposit",
    )(codes, values, bounds)


def fourier_tables(length):
    points, half = length // 2, length // 4
    positions = np.arange(points)
    scale = 1.0 / np.sqrt(length)
    parts = []
    for odd in range(2):
        ks = 2 * np.arange(half) + odd
        angles = (positions[:, None] * ks[None, :] % length) * (2.0 * np.pi / length)
        imag = -np.sin(angles) * scale
        if not odd:
            imag[:, 0] = np.where(positions % 2 == 0, scale, -scale)
        parts.append(np.concatenate([np.cos(angles) * scale, imag], axis=1))
    whole = np.stack(parts)
    high = whole.astype(ml_dtypes.bfloat16)
    low = (whole - high.astype(np.float64)).astype(ml_dtypes.bfloat16)
    return high, low


def fourier_kernel(*refs, sources):
    mesh_ref, add_refs = refs[0], refs[1 : 1 + sources]
    high_ref, low_ref = refs[1 + sources], refs[2 + sources]
    out_ref = refs[-1]
    rows, width = mesh_ref.shape[1:]
    pieces = []
    for s in range(sources):
        for h in range(width // LANES):
            pieces.append(
                mesh_ref[s, :, h * LANES : (h + 1) * LANES]
                + add_refs[s][h * rows : (h + 1) * rows, :]
            )
    mid = len(pieces) // 2
    halves = []
    for odd in range(2):
        if odd:
            folded = [a - b for a, b in zip(pieces[:mid], pieces[mid:])]
        else:
            folded = [a + b for a, b in zip(pieces[:mid], pieces[mid:])]
        values = jnp.concatenate(folded, axis=1)
        high = values.astype(jnp.bfloat16)
        low = (values - high.astype(jnp.float32)).astype(jnp.bfloat16)
        both = jnp.dot(
            jnp.concatenate([high, low], axis=0), high_ref[odd], preferred_element_type=jnp.float32
        )
        halves.append(
            both[:rows]
            + both[rows:]
            + jnp.dot(high, low_ref[odd], preferred_element_type=jnp.float32)
        )
    lanes = lane_ids((rows, LANES))
    is_first = lanes == 0
    is_odd = (lanes & 1) == 1
    steps = lanes >> 1
    tiles = len(pieces)
    per = tiles // 4

    def tile(odd, part, j):
        at = (part * per + j) * LANES
        return halves[odd][:, at : at + LANES]

    def pick(value, lane):
        return jnp.take_along_axis(value, lane, axis=1, mode="promise_in_bounds")

    for j in range(tiles):
        for part in range(2):
            if j < tiles // 2:
                at = BLOCK * j
                lane = (at % LANES) + steps
                even = pick(tile(0, part, at // LANES), lane)
                odd = pick(tile(1, part, at // LANES), lane)
                if j == 0 and part == 1:
                    even = jnp.where(is_first, 0.0, even)
            else:
                at = BLOCK * (tiles - j)
                last = (at - 1) // LANES
                even = pick(tile(0, part, last), (at - steps) & (LANES - 1))
                odd = pick(tile(1, part, last), ((at - 1) % LANES) - steps)
                if at % LANES == 0 and j > tiles // 2:
                    even = jnp.where(is_first, tile(0, part, at // LANES), even)
                if part == 1:
                    even, odd = -even, -odd
                if j == tiles // 2:
                    even = jnp.where(is_first, 0.0 if part else tile(0, 1, 0), even)
            out_ref[part, 0, :, j * LANES : (j + 1) * LANES] = jnp.where(is_odd, odd, even)


def fourier(mesh_part, count, adds, tables, first, planes, so_far, rows):
    sources, _, width = mesh_part.shape
    length = sources * width
    add_rows = (width // LANES) * rows
    operands = [mesh_part, *adds, *tables]
    in_specs = (
        [pl.BlockSpec((sources, rows, width), lambda p: (0, p, 0))]
        + [pl.BlockSpec((add_rows, LANES), lambda p: (first + p, 0))] * sources
        + [
            pl.BlockSpec((2, length // 2, length // 2), lambda p: (0, 0, 0), pipeline_mode=pl.Buffered(1))
        ]
        * 2
    )
    aliases = {}
    if so_far is not None:
        aliases = {len(operands): 0}
        operands.append(so_far)
        in_specs.append(pl.BlockSpec(memory_space=pl.ANY))
    return pl.pallas_call(
        functools.partial(fourier_kernel, sources=sources),
        grid=(count,),
        out_shape=jax.ShapeDtypeStruct((2, planes, rows, length), jnp.float32),
        in_specs=in_specs,
        out_specs=pl.BlockSpec((2, 1, rows, length), lambda p: (0, first + p, 0, 0)),
        input_output_aliases=aliases,
        compiler_params=params(),
        cost_estimate=cost(10**6, count * 10 * 10**6),
        name="fourier",
    )(*operands)


def after(value, *others):
    return lax.optimization_barrier((value, *others))[0]


def on_device(
    multipoles,
    proxy_list,
    proxy_count,
    pair_source,
    pair_target,
    block_class,
    m2l_ops,
    cell_mesh,
    pm_density,
    *,
    n_gx,
    n_gy,
):
    coef_count, cell_count = multipoles.shape
    slots = proxy_list.shape[2]
    planes, mesh_rows, width = pm_density.shape
    own_rows = mesh_rows // n_gx
    domains = n_gx * n_gy
    lists, counts = proxy_list[0], proxy_count[0]

    def send(part):
        return lax.all_to_all(part, "gx", 0, 0, tiled=True)

    spans = []
    first = 0
    for size in CHUNKS:
        spans.append((first, size))
        first += size

    parts = [send(first_part(pm_density, cell_mesh, multipoles, n_gx))]
    carved = [
        carve(pm_density, at, size, n_gx).reshape(n_gx, size * own_rows, width)
        for at, size in spans[1:]
    ]

    cells = jnp.pad(multipoles, ((0, KPAD - coef_count), (0, 0)))
    base = cell_count + 8 * slots
    table = own_table(cells, base + TOP * domains)
    outgoing = pack(table, cell_count, lists, counts)
    arrived = exchange(outgoing, n_gx, n_gy)

    top = pair_source - base
    domain = top >> log2(TOP)
    along = (domain & (n_gy - 1)) ^ lax.axis_index("gy")
    place = (along * n_gx + (domain >> log2(n_gy))) * TOP_ROWS + (top & (TOP_ROWS - 1))
    top = base + ((top >> log2(TOP_ROWS)) & 1) * (TOP_ROWS * domains) + place
    wanted = jnp.where(pair_source < base, pair_source, top)
    sources = order(((wanted << SHIFT) | (pair_target & (BLOCK - 1))).reshape(-1, LANES))

    turned_ops = jnp.pad(
        m2l_ops.transpose(0, 2, 1), ((0, 0), (0, KPAD - coef_count), (0, KPAD - coef_count))
    )
    high = lax.reduce_precision(turned_ops, 8, 7)
    ops = jnp.concatenate([high, turned_ops - high], axis=2)
    ops = jnp.pad(ops, ((0, 0), (0, 0), (0, LANES - 2 * KPAD)))

    tiles = width // LANES
    add_rows = planes * tiles * own_rows
    mine = lax.axis_index("gx").astype(jnp.int32).reshape(1)
    codes, amounts, bounds, top_own = sift(parts[0], mine, planes, own_rows, cell_count // LANES)
    tops = [top_own]
    for bit in range(log2(n_gy)):
        held = jnp.concatenate(tops, axis=0) if bit else top_own
        tops.append(lax.ppermute(held, "gy", [(i, i ^ (1 << bit)) for i in range(n_gy)]))

    parts.append(send(after(carved[0], parts[0], sources, ops, *arrived)))
    adds = deposit(codes, amounts, bounds, add_rows + 8, n_gx)
    table = whole_table(table, arrived, tops)
    cell_steps = cell_count // LANES
    slot_steps = 8 * slots // LANES
    slot_fields = m2l(sources, block_class, table, ops, cell_steps, slot_steps, True, slots)
    returned = exchange([slot_fields[m] for m in range(8)], n_gx, n_gy)
    parts.append(send(after(carved[1], parts[1], adds[0], *returned)))
    own_fields = m2l(sources, block_class, table, ops, 0, cell_steps, False, slots)

    tables = fourier_tables(n_gx * width)
    spectrum = None
    for i, (at, size) in enumerate(spans):
        if i == 2:
            parts.append(send(after(carved[2], parts[2], own_fields, spectrum)))
        spectrum = fourier(parts[i], size, adds, tables, at, planes, spectrum, own_rows)

    field_tensors = add_back(lists, counts, own_fields, returned, coef_count)
    return (field_tensors, spectrum)


def solution(mesh):
    placed = (
        P(None, ("gx", "gy")),
        P(("gx", "gy"), None, None),
        P(("gx", "gy"), None),
        P(("gx", "gy")),
        P(("gx", "gy")),
        P(("gx", "gy")),
        P(),
        P(("gx", "gy")),
        P("gy", None, "gx"),
    )
    return jax.shard_map(
        functools.partial(on_device, n_gx=mesh.shape["gx"], n_gy=mesh.shape["gy"]),
        mesh=mesh,
        in_specs=placed,
        out_specs=(P(None, ("gx", "gy")), P(None, "gy", "gx", None)),
        check_vma=False,
    )
```

```python
import functools

import jax
import jax.numpy as jnp
import ml_dtypes
import numpy as np
from jax import lax
from jax.experimental import pallas as pl
from jax.experimental.pallas import tpu as pltpu
from jax.sharding import PartitionSpec as P

TOP = 32
BLOCK = 64
LANES = 128
KPAD = 40
COPIES = 3
PER_WINDOW = 8
SHIFT = 6
LANE_SHIFT = 7
VMEM_BYTES = 48 * 1024 * 1024
CHUNKS = (1, 3, 3, 1)
TOP_ROWS = TOP // 2

DEPOSIT_SCALE = 8.0
SENT = ((0, 0), (2, 0), (1, 0), (0, 1), (1, 1), (0, 2), (2, 1), (1, 2))
GOT = ((3, 2), (3, 1), (3, 0), (1, 1), (0, 1), (2, 2), (2, 1), (2, 0))
IN_ROW = 0x57241360

SMEM_WHOLE = pl.BlockSpec(memory_space=pltpu.SMEM)
VMEM_WHOLE = pl.BlockSpec(memory_space=pltpu.VMEM)


def params():
    return pltpu.CompilerParams(vmem_limit_bytes=VMEM_BYTES)


def cost(flops, nbytes):
    return pl.CostEstimate(flops=flops, bytes_accessed=nbytes, transcendentals=0)


def spread(block):
    rest = jnp.zeros((LANES - COPIES * KPAD, LANES), jnp.float32)
    return jnp.concatenate([block] * COPIES + [rest], axis=0).T


def lane_ids(shape):
    return lax.broadcasted_iota(jnp.int32, shape, len(shape) - 1)


def own_table_kernel(cells_ref, out_ref):
    @pl.loop(0, cells_ref.shape[1] // LANES)
    def _(k):
        at = pl.multiple_of(k * LANES, LANES)
        out_ref[pl.ds(at, LANES), :] = spread(cells_ref[:, pl.ds(at, LANES)])


def own_table(cells, rows):
    count = cells.shape[1]
    return pl.pallas_call(
        own_table_kernel,
        grid=(1,),
        out_shape=jax.ShapeDtypeStruct((rows, LANES), jnp.float32),
        in_specs=[pl.BlockSpec((KPAD, count), lambda i: (0, 0))],
        out_specs=pl.BlockSpec((count, LANES), lambda i: (0, 0)),
        compiler_params=params(),
        cost_estimate=cost(10**6, 12 * 10**6),
        name="own_table",
    )(cells)


def cut_rows(refs, first, stop):
    pieces, at = [], 0
    for ref in refs:
        low, high = max(first - at, 0), min(stop - at, ref.shape[0])
        if low < high:
            pieces.append(ref[low:high, :])
        at += ref.shape[0]
    return jnp.concatenate(pieces, axis=0) if len(pieces) > 1 else pieces[0]


def whole_table_kernel(*refs, slot_steps):
    top_refs, out_ref = refs[4:-2], refs[-1]
    step = pl.program_id(0)
    for k in range(slot_steps):

        @pl.when(step == k)
        def _():
            at = 0
            for n in (2 * k, 2 * k + 1):
                part, place = GOT[n]
                for c in range(refs[part].shape[2] // LANES):
                    block = refs[part][place, :, c * LANES : (c + 1) * LANES]
                    out_ref[at : at + LANES, :] = spread(block)
                    at += LANES

    rows = out_ref.shape[0]
    total = sum(ref.shape[0] for ref in top_refs)
    lanes = lane_ids((rows, LANES))
    for k in range(2 * total // rows):

        @pl.when(step == slot_steps + k)
        def _():
            pieces = []
            for first in range(k * rows, (k + 1) * rows, min(rows, total)):
                group, at = first // total, first % total
                value = cut_rows(top_refs, at, at + min(rows, total))
                pieces.append(pltpu.roll(value, LANES - KPAD, 1) if group else value)
            value = jnp.concatenate(pieces, axis=0) if len(pieces) > 1 else pieces[0]
            value = jnp.where(lanes < KPAD, value, 0.0)
            out_ref[...] = value + pltpu.roll(value, KPAD, 1) + pltpu.roll(value, 2 * KPAD, 1)


def whole_table(table, arrived, tops):
    slots = arrived[0].shape[2]
    rows = 2 * slots
    top_rows = 2 * sum(part.shape[0] for part in tops)
    first = (table.shape[0] - 8 * slots - top_rows) // rows
    return pl.pallas_call(
        functools.partial(whole_table_kernel, slot_steps=4),
        grid=(4 + top_rows // rows,),
        out_shape=jax.ShapeDtypeStruct(table.shape, jnp.float32),
        in_specs=[VMEM_WHOLE] * (4 + len(tops)) + [pl.BlockSpec(memory_space=pl.ANY)],
        out_specs=pl.BlockSpec((rows, LANES), lambda i: (first + i, 0)),
        input_output_aliases={4 + len(tops): 0},
        compiler_params=params(),
        cost_estimate=cost(10**6, 16 * 10**6),
        name="whole_table",
    )(*arrived, *tops, table)


def as_rows(table):
    return table.reshape(table.shape[0], 1, LANES)


def pack_kernel(list_ref, count_ref, table_ref, *refs):
    outs, held = refs[:3], refs[3:]
    slot_tiles = list_ref.shape[1] // LANES
    for n in range(8):

        @pl.loop(0, slot_tiles, step=len(held))
        def _(i):
            firsts = [pl.multiple_of((i + k) * LANES, LANES) for k in range(len(held))]
            for first, rows in zip(firsts, held):
                for r in range(LANES):
                    rows[r : r + 1, :] = table_ref[list_ref[n, first + r]]
            for first, rows in zip(firsts, held):
                live = (lane_ids((KPAD, LANES)) + first) < count_ref[n]
                part, at = SENT[n]
                outs[part][at, :, pl.ds(first, LANES)] = jnp.where(live, rows[...].T[:KPAD], 0.0)


def pack(table, cell_count, proxy_list, proxy_count):
    slots = proxy_list.shape[1]
    return pl.pallas_call(
        pack_kernel,
        grid=(1,),
        out_shape=tuple(jax.ShapeDtypeStruct((size, KPAD, slots), jnp.float32) for size in (3, 3, 2)),
        in_specs=[
            SMEM_WHOLE,
            SMEM_WHOLE,
            pl.BlockSpec((cell_count, 1, LANES), lambda i: (0, 0, 0)),
        ],
        out_specs=tuple(
            pl.BlockSpec((size, KPAD, slots), lambda i: (0, 0, 0)) for size in (3, 3, 2)
        ),
        scratch_shapes=[pltpu.VMEM((LANES, LANES), jnp.float32)] * 2,
        compiler_params=params(),
        cost_estimate=cost(10**6, 25 * 10**6),
        name="pack",
    )(proxy_list, proxy_count, as_rows(table))


def exchange(down, up, mid):
    def shift(value, axis, by):
        count = lax.axis_size(axis)
        return lax.ppermute(value, axis, [(i, (i + by) % count) for i in range(count)])

    down, up = shift(down, "gy", -1), shift(up, "gy", 1)
    left = shift(jnp.stack([down[0], mid[0], up[0]]), "gx", -1)
    right = shift(jnp.stack([down[2], mid[1], up[2]]), "gx", 1)
    return down, up, left, right


def order_kernel(packed_ref, out_ref):
    lanes = lane_ids((LANES, LANES))
    within = lanes & (BLOCK - 1)
    base = lanes - within

    @pl.loop(0, packed_ref.shape[0] // LANES)
    def _(k):
        at = pl.ds(pl.multiple_of(k * LANES, LANES), LANES)
        packed = packed_ref[at, :]

        def step(i, ordered):
            value = jnp.take_along_axis(packed, base + i, axis=1, mode="promise_in_bounds")
            return jnp.where((value & (BLOCK - 1)) == within, value, ordered)

        ordered = lax.fori_loop(0, BLOCK, step, jnp.zeros_like(packed), unroll=8)
        out_ref[at, :] = ordered >> SHIFT


def order(packed):
    return pl.pallas_call(
        order_kernel,
        out_shape=jax.ShapeDtypeStruct(packed.shape, jnp.int32),
        in_specs=[VMEM_WHOLE],
        out_specs=VMEM_WHOLE,
        compiler_params=params(),
        cost_estimate=cost(10**6, 20 * 10**6),
        name="order",
    )(packed)


def m2l_kernel(source_ref, class_ref, table_ref, ops_ref, out_ref, *gathered, first, turned):
    step = first + pl.program_id(0)
    lanes = lane_ids((1, LANES))
    in_first = lanes < KPAD
    in_second = lanes < 2 * KPAD

    def row(b, t):
        return table_ref[source_ref[b // 2, (b % 2) * BLOCK + t]]

    for u in range(2):
        for t in range(BLOCK):
            for g in range(3):
                b = u * PER_WINDOW + 3 * g
                one, two = row(b, t), row(b + 1, t)
                three = row(b + 2, t) if g < 2 else two
                gathered[u][g, t : t + 1, :] = jnp.where(
                    in_first, one, jnp.where(in_second, two, three)
                )

    rest = jnp.zeros((LANES - COPIES * KPAD, LANES), jnp.float32)
    none = jnp.zeros((KPAD, LANES), jnp.float32)
    results = []
    for u in range(2):
        total = jnp.zeros((BLOCK, LANES), jnp.float32)
        for g in range(3):
            held = []
            for s in range(3):
                b = 3 * g + s
                if b < PER_WINDOW:
                    held.append(ops_ref[class_ref[step * 2 * PER_WINDOW + u * PER_WINDOW + b]])
                else:
                    held.append(none)
            weights = jnp.concatenate(held + [rest], axis=0).astype(jnp.bfloat16)
            values = gathered[u][g]
            high = values.astype(jnp.bfloat16)
            low = (values - high.astype(jnp.float32)).astype(jnp.bfloat16)
            total += jnp.dot(high, weights, preferred_element_type=jnp.float32)
            total += jnp.dot(low, weights, preferred_element_type=jnp.float32)
        results.append(total)
    both = jnp.concatenate(results, axis=0)
    both = both + pltpu.roll(both, LANES - KPAD, 1)
    if turned:
        out_ref[0] = both.T[:KPAD]
    else:
        out_ref[...] = both


def m2l(sources, classes, table, ops, first, steps, turned, slots):
    if turned:
        per = slots // LANES
        shape = (steps // per, KPAD, slots)
        out_spec = pl.BlockSpec(
            (1, KPAD, LANES), lambda i: ((IN_ROW >> (4 * (i // per))) & 7, 0, i % per)
        )
    else:
        shape = (steps * LANES, LANES)
        out_spec = pl.BlockSpec((LANES, LANES), lambda i: (i, 0))
    return pl.pallas_call(
        functools.partial(m2l_kernel, first=first, turned=turned),
        grid=(steps,),
        out_shape=jax.ShapeDtypeStruct(shape, jnp.float32),
        in_specs=[
            pl.BlockSpec((8, LANES), lambda i: (first + i, 0), memory_space=pltpu.SMEM),
            SMEM_WHOLE,
            VMEM_WHOLE,
            VMEM_WHOLE,
        ],
        out_specs=out_spec,
        scratch_shapes=[pltpu.VMEM((3, BLOCK, LANES), jnp.float32)] * 2,
        compiler_params=params(),
        cost_estimate=cost(10**6, 150 * 10**6),
        name="m2l_slots" if turned else "m2l_cells",
    )(sources, classes, as_rows(table), ops)


def add_back_kernel(list_ref, count_ref, own_ref, *refs):
    slot_refs, out_ref = refs[:4], refs[4]
    rows, sums = refs[5], refs[6:]
    slots = list_ref.shape[1]
    sums[0][...] = own_ref[...]
    for held in sums[1:]:
        held[...] = jnp.zeros_like(held)
    for n in range(8):
        for k in range(slots // LANES):
            live = (lane_ids((KPAD, LANES)) + k * LANES) < count_ref[n]
            part, place = GOT[n]
            values = jnp.where(live, slot_refs[part][place, :, k * LANES : (k + 1) * LANES], 0.0)
            at = n * slots + k * LANES
            rows[at : at + LANES, :] = spread(values)

    @pl.loop(0, slots, step=4)
    def _(first):
        for j in range(4):
            to = [pl.ds(list_ref[n, first + j], 1) for n in range(8)]
            old = [sums[n][to[n], :] for n in range(8)]
            new = [old[n] + rows[pl.ds(n * slots + first + j, 1), :] for n in range(8)]
            for n in range(8):
                sums[n][to[n], :] = new[n]

    @pl.loop(0, own_ref.shape[0] // LANES)
    def _(k):
        at = pl.ds(pl.multiple_of(k * LANES, LANES), LANES)
        parts = [held[at, :] for held in sums]
        while len(parts) > 1:
            parts = [a + b for a, b in zip(parts[::2], parts[1::2])]
        out_ref[:, at] = parts[0].T[: out_ref.shape[0]]


def add_back(proxy_list, proxy_count, own_rows, slot_fields, coef_count):
    cell_count = own_rows.shape[0]
    slots = proxy_list.shape[1]
    return pl.pallas_call(
        add_back_kernel,
        out_shape=jax.ShapeDtypeStruct((coef_count, cell_count), jnp.float32),
        in_specs=[SMEM_WHOLE, SMEM_WHOLE] + [VMEM_WHOLE] * 5,
        out_specs=VMEM_WHOLE,
        scratch_shapes=[pltpu.VMEM((8 * slots, LANES), jnp.float32)]
        + [pltpu.VMEM((cell_count, LANES), jnp.float32)] * 8,
        compiler_params=params(),
        cost_estimate=cost(10**6, 30 * 10**6),
        name="add_back",
    )(proxy_list, proxy_count, own_rows, *slot_fields)


def carve_kernel(mesh_ref, out_ref, sems, *, first):
    sources, count, rows, width = out_ref.shape
    copies = [
        pltpu.make_async_copy(
            mesh_ref.at[pl.ds(first, count), pl.ds(s * rows, rows), :], out_ref.at[s], sems.at[s]
        )
        for s in range(sources)
    ]
    for copy in copies:
        copy.start()
    for copy in copies:
        copy.wait()


def carve(mesh, first, count, sources):
    rows, width = mesh.shape[1] // sources, mesh.shape[2]
    return pl.pallas_call(
        functools.partial(carve_kernel, first=first),
        out_shape=jax.ShapeDtypeStruct((sources, count, rows, width), jnp.float32),
        in_specs=[pl.BlockSpec(memory_space=pl.ANY)],
        out_specs=VMEM_WHOLE,
        scratch_shapes=[pltpu.SemaphoreType.DMA((sources,))],
        compiler_params=params(),
        cost_estimate=cost(0, 8 * count * sources * rows * width),
        name="carve",
    )(mesh)


def first_part_kernel(mesh_ref, place_ref, cells_ref, out_ref, sems, *, rows):
    sources, _, width = out_ref.shape
    copies = [
        pltpu.make_async_copy(
            mesh_ref.at[0, pl.ds(s * rows, rows), :], out_ref.at[s, pl.ds(0, rows), :], sems.at[s]
        )
        for s in range(sources)
    ]
    for copy in copies:
        copy.start()
    is_first = lane_ids((TOP_ROWS, LANES)) < KPAD
    rest = jnp.zeros((KPAD - cells_ref.shape[0], LANES), jnp.float32)
    table = spread(jnp.concatenate([cells_ref[:, :LANES], rest], axis=0))
    top = jnp.where(is_first, table[:TOP_ROWS, :], table[TOP_ROWS : 2 * TOP_ROWS, :])
    blocks = [place_ref[...].astype(jnp.float32), cell_lines(cells_ref), top]
    at = rows
    for block in blocks:
        high = block.shape[0] * LANES // width
        for h in range(width // LANES):
            for s in range(sources):
                out_ref[s, at : at + high, h * LANES : (h + 1) * LANES] = block[
                    h * high : (h + 1) * high, :
                ]
        at += high
    for copy in copies:
        copy.wait()


def cell_lines(cells_ref):
    lines = [cells_ref[0:1, k : k + LANES] for k in range(0, cells_ref.shape[1], LANES)]
    return DEPOSIT_SCALE * jnp.concatenate(lines, axis=0)


def first_part(mesh, place, multipoles, sources):
    rows, width = mesh.shape[1] // sources, mesh.shape[2]
    extra = (2 * place.size + TOP_ROWS * LANES) // width
    return pl.pallas_call(
        functools.partial(first_part_kernel, rows=rows),
        out_shape=jax.ShapeDtypeStruct((sources, rows + extra, width), jnp.float32),
        in_specs=[pl.BlockSpec(memory_space=pl.ANY), VMEM_WHOLE, VMEM_WHOLE],
        out_specs=VMEM_WHOLE,
        scratch_shapes=[
            pltpu.SemaphoreType.DMA((sources,)),
        ],
        compiler_params=params(),
        cost_estimate=cost(0, 8 * sources * rows * width),
        name="first_part",
    )(mesh, place.reshape(-1, LANES), multipoles)


def log2(value):
    return value.bit_length() - 1


def sift_kernel(mine_ref, part_ref, code_ref, value_ref, bound_ref, top_ref, ride, sem, *, planes, rows):
    sources, extra, width = ride.shape
    lines = code_ref.shape[0] // sources
    copy = pltpu.make_async_copy(part_ref.at[:, pl.ds(rows, extra), :], ride, sem)
    copy.start()
    copy.wait()

    def unfold(first, count):
        high = count * LANES // width
        return jnp.concatenate(
            [
                ride[s, first : first + high, h * LANES : (h + 1) * LANES]
                for s in range(sources)
                for h in range(width // LANES)
            ],
            axis=0,
        )

    step = lines * LANES // width
    place = unfold(0, lines).astype(jnp.int32)
    value = unfold(step, lines)
    top_ref[...] = unfold(2 * step, TOP_ROWS)

    row_at, mesh_rows = log2(width), rows * sources
    plane = place >> (row_at + log2(mesh_rows))
    row = (place >> row_at) & (mesh_rows - 1)
    column = place & (width - 1)
    tiles = width // LANES
    target = (plane * tiles + (column >> LANE_SHIFT)) * rows + (row & (rows - 1))
    none = planes * tiles * rows * LANES
    mine = (row >> log2(rows)) == mine_ref[0]
    lanes = lane_ids(place.shape)
    code = jnp.where(mine, target * LANES + (column & (LANES - 1)), none)
    value = jnp.where(mine, value, 0.0)
    ahead = jnp.where(mine, 1, 0)
    for b in range(LANE_SHIFT):
        ahead = ahead + jnp.where(lanes >= (1 << b), pltpu.roll(ahead, 1 << b, 1), 0)
    shift = jnp.where(mine, lanes + 1 - ahead, 0)
    for b in range(LANE_SHIFT):
        back = LANES - (1 << b)
        moves = (shift >> b) & 1
        comes = pltpu.roll(moves, back, 1) == 1
        goes = moves == 1
        code = jnp.where(comes, pltpu.roll(code, back, 1), jnp.where(goes, none, code))
        value = jnp.where(comes, pltpu.roll(value, back, 1), jnp.where(goes, 0.0, value))
        shift = jnp.where(comes, pltpu.roll(shift, back, 1), jnp.where(goes, 0, shift))
    code_ref[...] = code
    value_ref[...] = value
    counts = jnp.sum(jnp.where(mine, 1.0, 0.0), axis=1, keepdims=True)
    counts = jnp.broadcast_to(counts, mine.shape).reshape(2 * sources, lines // 2, LANES)
    bound_ref[...] = jnp.max(counts, axis=0).astype(jnp.int32)


def sift(part, mine, planes, rows, lines):
    sources, whole_rows, width = part.shape
    extra = whole_rows - rows
    shape = (sources * lines, LANES)
    return pl.pallas_call(
        functools.partial(sift_kernel, planes=planes, rows=rows),
        out_shape=(
            jax.ShapeDtypeStruct(shape, jnp.int32),
            jax.ShapeDtypeStruct(shape, jnp.float32),
            jax.ShapeDtypeStruct((lines // 2, LANES), jnp.int32),
            jax.ShapeDtypeStruct((sources * TOP_ROWS, LANES), jnp.float32),
        ),
        in_specs=[SMEM_WHOLE, pl.BlockSpec(memory_space=pl.ANY)],
        out_specs=(VMEM_WHOLE,) * 4,
        scratch_shapes=[pltpu.VMEM((sources, extra, width), jnp.float32), pltpu.SemaphoreType.DMA],
        compiler_params=params(),
        cost_estimate=cost(10**6, 8 * 10**6),
        name="sift",
    )(mine, part)


def deposit_kernel(code_ref, value_ref, bound_ref, *refs):
    sources = len(refs) // 2
    outs, others = refs[:sources], refs[sources:]
    lines = code_ref.shape[0] // (2 * sources)
    lanes = lane_ids((1, LANES))
    for held in refs:
        held[...] = jnp.zeros_like(held)

    def line(g, _):
        def one(j):
            at = [((2 * s + h) * lines + g, j) for h in range(2) for s in range(sources)]
            codes = [code_ref[i] for i in at]
            to = [pl.ds(code >> LANE_SHIFT, 1) for code in codes]
            old = [held[rows, :] for held, rows in zip(refs, to)]
            new = [
                row + jnp.where(lanes == (code & (LANES - 1)), value_ref[i], 0.0)
                for row, code, i in zip(old, codes, at)
            ]
            for held, rows, row in zip(refs, to, new):
                held[rows, :] = row

        def four(i, _):
            for j in range(4):
                one(4 * i + j)
            return 0

        return lax.fori_loop(0, (bound_ref[g, 0] + 3) >> 2, four, 0)

    lax.fori_loop(0, lines, line, 0)
    for out_ref, held in zip(outs, others):
        out_ref[...] = out_ref[...] + held[...]


def deposit(codes, values, bounds, rows, sources):
    return pl.pallas_call(
        deposit_kernel,
        out_shape=(jax.ShapeDtypeStruct((rows, LANES), jnp.float32),) * sources,
        in_specs=[SMEM_WHOLE] * 3,
        out_specs=(VMEM_WHOLE,) * sources,
        scratch_shapes=[pltpu.VMEM((rows, LANES), jnp.float32)] * sources,
        compiler_params=params(),
        cost_estimate=cost(10**6, 40 * 10**6),
        name="deposit",
    )(codes, values, bounds)


def fourier_tables(length):
    points, half = length // 2, length // 4
    positions = np.arange(points)
    scale = 1.0 / np.sqrt(length)
    parts = []
    for odd in range(2):
        ks = 2 * np.arange(half) + odd
        angles = (positions[:, None] * ks[None, :] % length) * (2.0 * np.pi / length)
        imag = -np.sin(angles) * scale
        if not odd:
            imag[:, 0] = np.where(positions % 2 == 0, scale, -scale)
        parts.append(np.concatenate([np.cos(angles) * scale, imag], axis=1))
    whole = np.stack(parts)
    high = whole.astype(ml_dtypes.bfloat16)
    low = (whole - high.astype(np.float64)).astype(ml_dtypes.bfloat16)
    return high, low


def fourier_kernel(*refs, sources):
    mesh_ref, add_refs = refs[0], refs[1 : 1 + sources]
    high_ref, low_ref = refs[1 + sources], refs[2 + sources]
    out_ref = refs[-1]
    rows, width = mesh_ref.shape[1:]
    pieces = []
    for s in range(sources):
        for h in range(width // LANES):
            pieces.append(
                mesh_ref[s, :, h * LANES : (h + 1) * LANES]
                + add_refs[s][h * rows : (h + 1) * rows, :]
            )
    mid = len(pieces) // 2
    halves = []
    for odd in range(2):
        if odd:
            folded = [a - b for a, b in zip(pieces[:mid], pieces[mid:])]
        else:
            folded = [a + b for a, b in zip(pieces[:mid], pieces[mid:])]
        values = jnp.concatenate(folded, axis=1)
        high = values.astype(jnp.bfloat16)
        low = (values - high.astype(jnp.float32)).astype(jnp.bfloat16)
        both = jnp.dot(
            jnp.concatenate([high, low], axis=0), high_ref[odd], preferred_element_type=jnp.float32
        )
        halves.append(
            both[:rows]
            + both[rows:]
            + jnp.dot(high, low_ref[odd], preferred_element_type=jnp.float32)
        )
    lanes = lane_ids((rows, LANES))
    is_first = lanes == 0
    is_odd = (lanes & 1) == 1
    steps = lanes >> 1
    tiles = len(pieces)
    per = tiles // 4

    def tile(odd, part, j):
        at = (part * per + j) * LANES
        return halves[odd][:, at : at + LANES]

    def pick(value, lane):
        return jnp.take_along_axis(value, lane, axis=1, mode="promise_in_bounds")

    for j in range(tiles):
        for part in range(2):
            if j < tiles // 2:
                at = BLOCK * j
                lane = (at % LANES) + steps
                even = pick(tile(0, part, at // LANES), lane)
                odd = pick(tile(1, part, at // LANES), lane)
                if j == 0 and part == 1:
                    even = jnp.where(is_first, 0.0, even)
            else:
                at = BLOCK * (tiles - j)
                last = (at - 1) // LANES
                even = pick(tile(0, part, last), (at - steps) & (LANES - 1))
                odd = pick(tile(1, part, last), ((at - 1) % LANES) - steps)
                if at % LANES == 0 and j > tiles // 2:
                    even = jnp.where(is_first, tile(0, part, at // LANES), even)
                if part == 1:
                    even, odd = -even, -odd
                if j == tiles // 2:
                    even = jnp.where(is_first, 0.0 if part else tile(0, 1, 0), even)
            out_ref[part, 0, :, j * LANES : (j + 1) * LANES] = jnp.where(is_odd, odd, even)


def fourier(mesh_part, count, adds, tables, first, planes, so_far, rows):
    sources, _, width = mesh_part.shape
    length = sources * width
    add_rows = (width // LANES) * rows
    operands = [mesh_part, *adds, *tables]
    in_specs = (
        [pl.BlockSpec((sources, rows, width), lambda p: (0, p, 0))]
        + [pl.BlockSpec((add_rows, LANES), lambda p: (first + p, 0))] * sources
        + [
            pl.BlockSpec((2, length // 2, length // 2), lambda p: (0, 0, 0), pipeline_mode=pl.Buffered(1))
        ]
        * 2
    )
    aliases = {}
    if so_far is not None:
        aliases = {len(operands): 0}
        operands.append(so_far)
        in_specs.append(pl.BlockSpec(memory_space=pl.ANY))
    return pl.pallas_call(
        functools.partial(fourier_kernel, sources=sources),
        grid=(count,),
        out_shape=jax.ShapeDtypeStruct((2, planes, rows, length), jnp.float32),
        in_specs=in_specs,
        out_specs=pl.BlockSpec((2, 1, rows, length), lambda p: (0, first + p, 0, 0)),
        input_output_aliases=aliases,
        compiler_params=params(),
        cost_estimate=cost(10**6, count * 10 * 10**6),
        name="fourier",
    )(*operands)


def after(value, *others):
    return lax.optimization_barrier((value, *others))[0]


def on_device(
    multipoles,
    proxy_list,
    proxy_count,
    pair_source,
    pair_target,
    block_class,
    m2l_ops,
    cell_mesh,
    pm_density,
    *,
    n_gx,
    n_gy,
):
    coef_count, cell_count = multipoles.shape
    slots = proxy_list.shape[2]
    planes, mesh_rows, width = pm_density.shape
    own_rows = mesh_rows // n_gx
    domains = n_gx * n_gy
    lists, counts = proxy_list[0], proxy_count[0]

    def send(part):
        return lax.all_to_all(part, "gx", 0, 0, tiled=True)

    spans = []
    first = 0
    for size in CHUNKS:
        spans.append((first, size))
        first += size

    parts = [send(first_part(pm_density, cell_mesh, multipoles, n_gx))]
    carved = [
        carve(pm_density, at, size, n_gx).reshape(n_gx, size * own_rows, width)
        for at, size in spans[1:]
    ]

    cells = jnp.pad(multipoles, ((0, KPAD - coef_count), (0, 0)))
    base = cell_count + 8 * slots
    table = own_table(cells, base + TOP * domains)
    outgoing = pack(table, cell_count, lists, counts)
    arrived = exchange(*outgoing)

    top = pair_source - base
    domain = top >> log2(TOP)
    along = (domain & (n_gy - 1)) ^ lax.axis_index("gy")
    place = (along * n_gx + (domain >> log2(n_gy))) * TOP_ROWS + (top & (TOP_ROWS - 1))
    top = base + ((top >> log2(TOP_ROWS)) & 1) * (TOP_ROWS * domains) + place
    wanted = jnp.where(pair_source < base, pair_source, top)
    sources = order(((wanted << SHIFT) | (pair_target & (BLOCK - 1))).reshape(-1, LANES))

    turned_ops = jnp.pad(
        m2l_ops.transpose(0, 2, 1), ((0, 0), (0, KPAD - coef_count), (0, KPAD - coef_count))
    )
    high = lax.reduce_precision(turned_ops, 8, 7)
    ops = jnp.concatenate([high, turned_ops - high], axis=2)
    ops = jnp.pad(ops, ((0, 0), (0, 0), (0, LANES - 2 * KPAD)))

    tiles = width // LANES
    add_rows = planes * tiles * own_rows
    mine = lax.axis_index("gx").astype(jnp.int32).reshape(1)
    codes, amounts, bounds, top_own = sift(parts[0], mine, planes, own_rows, cell_count // LANES)
    tops = [top_own]
    for bit in range(log2(n_gy)):
        held = jnp.concatenate(tops, axis=0) if bit else top_own
        tops.append(lax.ppermute(held, "gy", [(i, i ^ (1 << bit)) for i in range(n_gy)]))

    parts.append(send(after(carved[0], parts[0], *arrived)))
    adds = deposit(codes, amounts, bounds, add_rows + 8, n_gx)
    table = whole_table(table, arrived, tops)
    cell_steps = cell_count // LANES
    slot_steps = 8 * slots // LANES
    slot_fields = m2l(sources, block_class, table, ops, cell_steps, slot_steps, True, slots)
    returned = exchange(slot_fields[:3], slot_fields[3:6], slot_fields[6:])
    parts.append(send(after(carved[1], parts[1], slot_fields)))
    own_fields = m2l(sources, block_class, table, ops, 0, cell_steps, False, slots)

    tables = fourier_tables(n_gx * width)
    spectrum = None
    for i, (at, size) in enumerate(spans):
        if i == 2:
            parts.append(send(after(carved[2], parts[2], own_fields, spectrum, *returned)))
        spectrum = fourier(parts[i], size, adds, tables, at, planes, spectrum, own_rows)

    field_tensors = add_back(lists, counts, own_fields, returned, coef_count)
    return (field_tensors, spectrum)


def solution(mesh):
    placed = (
        P(None, ("gx", "gy")),
        P(("gx", "gy"), None, None),
        P(("gx", "gy"), None),
        P(("gx", "gy")),
        P(("gx", "gy")),
        P(("gx", "gy")),
        P(),
        P(("gx", "gy")),
        P("gy", None, "gx"),
    )
    return jax.shard_map(
        functools.partial(on_device, n_gx=mesh.shape["gx"], n_gy=mesh.shape["gy"]),
        mesh=mesh,
        in_specs=placed,
        out_specs=(P(None, ("gx", "gy")), P(None, "gy", "gx", None)),
        check_vma=False,
    )
```

```python
import functools

import jax
import jax.numpy as jnp
import ml_dtypes
import numpy as np
from jax import lax
from jax.experimental import pallas as pl
from jax.experimental.pallas import tpu as pltpu
from jax.sharding import PartitionSpec as P

TOP = 32
BLOCK = 64
LANES = 128
KPAD = 40
COPIES = 3
PER_WINDOW = 8
SHIFT = 6
LANE_SHIFT = 7
VMEM_BYTES = 48 * 1024 * 1024
CHUNKS = (2, 4, 2)
TOP_ROWS = TOP // 2

DEPOSIT_SCALE = 8.0
SENT = ((0, 0), (2, 0), (1, 0), (0, 1), (1, 1), (0, 2), (2, 1), (1, 2))
GOT = ((3, 2), (3, 1), (3, 0), (1, 1), (0, 1), (2, 2), (2, 1), (2, 0))
IN_ROW = 0x57241360

SMEM_WHOLE = pl.BlockSpec(memory_space=pltpu.SMEM)
VMEM_WHOLE = pl.BlockSpec(memory_space=pltpu.VMEM)


def params():
    return pltpu.CompilerParams(vmem_limit_bytes=VMEM_BYTES)


def cost(flops, nbytes):
    return pl.CostEstimate(flops=flops, bytes_accessed=nbytes, transcendentals=0)


def spread(block):
    rest = jnp.zeros((LANES - COPIES * KPAD, LANES), jnp.float32)
    return jnp.concatenate([block] * COPIES + [rest], axis=0).T


def lane_ids(shape):
    return lax.broadcasted_iota(jnp.int32, shape, len(shape) - 1)


def own_table_kernel(cells_ref, out_ref):
    @pl.loop(0, cells_ref.shape[1] // LANES)
    def _(k):
        at = pl.multiple_of(k * LANES, LANES)
        out_ref[pl.ds(at, LANES), :] = spread(cells_ref[:, pl.ds(at, LANES)])


def own_table(cells, rows):
    count = cells.shape[1]
    return pl.pallas_call(
        own_table_kernel,
        grid=(1,),
        out_shape=jax.ShapeDtypeStruct((rows, LANES), jnp.float32),
        in_specs=[pl.BlockSpec((KPAD, count), lambda i: (0, 0))],
        out_specs=pl.BlockSpec((count, LANES), lambda i: (0, 0)),
        compiler_params=params(),
        cost_estimate=cost(10**6, 12 * 10**6),
        name="own_table",
    )(cells)


def cut_rows(refs, first, stop):
    pieces, at = [], 0
    for ref in refs:
        low, high = max(first - at, 0), min(stop - at, ref.shape[0])
        if low < high:
            pieces.append(ref[low:high, :])
        at += ref.shape[0]
    return jnp.concatenate(pieces, axis=0) if len(pieces) > 1 else pieces[0]


def whole_table_kernel(*refs, slot_steps):
    top_refs, out_ref = refs[4:-2], refs[-1]
    step = pl.program_id(0)
    for k in range(slot_steps):

        @pl.when(step == k)
        def _():
            at = 0
            for n in (2 * k, 2 * k + 1):
                part, place = GOT[n]
                for c in range(refs[part].shape[2] // LANES):
                    block = refs[part][place, :, c * LANES : (c + 1) * LANES]
                    out_ref[at : at + LANES, :] = spread(block)
                    at += LANES

    rows = out_ref.shape[0]
    total = sum(ref.shape[0] for ref in top_refs)
    lanes = lane_ids((rows, LANES))
    for k in range(2 * total // rows):

        @pl.when(step == slot_steps + k)
        def _():
            pieces = []
            for first in range(k * rows, (k + 1) * rows, min(rows, total)):
                group, at = first // total, first % total
                value = cut_rows(top_refs, at, at + min(rows, total))
                pieces.append(pltpu.roll(value, LANES - KPAD, 1) if group else value)
            value = jnp.concatenate(pieces, axis=0) if len(pieces) > 1 else pieces[0]
            value = jnp.where(lanes < KPAD, value, 0.0)
            out_ref[...] = value + pltpu.roll(value, KPAD, 1) + pltpu.roll(value, 2 * KPAD, 1)


def whole_table(table, arrived, tops):
    slots = arrived[0].shape[2]
    rows = 2 * slots
    top_rows = 2 * sum(part.shape[0] for part in tops)
    first = (table.shape[0] - 8 * slots - top_rows) // rows
    return pl.pallas_call(
        functools.partial(whole_table_kernel, slot_steps=4),
        grid=(4 + top_rows // rows,),
        out_shape=jax.ShapeDtypeStruct(table.shape, jnp.float32),
        in_specs=[VMEM_WHOLE] * (4 + len(tops)) + [pl.BlockSpec(memory_space=pl.ANY)],
        out_specs=pl.BlockSpec((rows, LANES), lambda i: (first + i, 0)),
        input_output_aliases={4 + len(tops): 0},
        compiler_params=params(),
        cost_estimate=cost(10**6, 16 * 10**6),
        name="whole_table",
    )(*arrived, *tops, table)


def as_rows(table):
    return table.reshape(table.shape[0], 1, LANES)


def pack_kernel(list_ref, count_ref, table_ref, *refs):
    outs, held = refs[:3], refs[3:]
    slot_tiles = list_ref.shape[1] // LANES
    for n in range(8):

        @pl.loop(0, slot_tiles, step=len(held))
        def _(i):
            firsts = [pl.multiple_of((i + k) * LANES, LANES) for k in range(len(held))]
            for first, rows in zip(firsts, held):
                for r in range(LANES):
                    rows[r : r + 1, :] = table_ref[list_ref[n, first + r]]
            for first, rows in zip(firsts, held):
                live = (lane_ids((KPAD, LANES)) + first) < count_ref[n]
                part, at = SENT[n]
                outs[part][at, :, pl.ds(first, LANES)] = jnp.where(live, rows[...].T[:KPAD], 0.0)


def pack(table, cell_count, proxy_list, proxy_count):
    slots = proxy_list.shape[1]
    return pl.pallas_call(
        pack_kernel,
        grid=(1,),
        out_shape=tuple(jax.ShapeDtypeStruct((size, KPAD, slots), jnp.float32) for size in (3, 3, 2)),
        in_specs=[
            SMEM_WHOLE,
            SMEM_WHOLE,
            pl.BlockSpec((cell_count, 1, LANES), lambda i: (0, 0, 0)),
        ],
        out_specs=tuple(
            pl.BlockSpec((size, KPAD, slots), lambda i: (0, 0, 0)) for size in (3, 3, 2)
        ),
        scratch_shapes=[pltpu.VMEM((LANES, LANES), jnp.float32)] * 2,
        compiler_params=params(),
        cost_estimate=cost(10**6, 25 * 10**6),
        name="pack",
    )(proxy_list, proxy_count, as_rows(table))


def exchange(down, up, mid, *before_gx):
    def shift(value, axis, by):
        count = lax.axis_size(axis)
        return lax.ppermute(value, axis, [(i, (i + by) % count) for i in range(count)])

    down, up = shift(down, "gy", -1), shift(up, "gy", 1)
    if before_gx:
        mid = after(mid, *before_gx)
    left = shift(jnp.stack([down[0], mid[0], up[0]]), "gx", -1)
    right = shift(jnp.stack([down[2], mid[1], up[2]]), "gx", 1)
    return down, up, left, right


def order_kernel(packed_ref, out_ref):
    lanes = lane_ids((LANES, LANES))
    within = lanes & (BLOCK - 1)
    base = lanes - within

    @pl.loop(0, packed_ref.shape[0] // LANES)
    def _(k):
        at = pl.ds(pl.multiple_of(k * LANES, LANES), LANES)
        packed = packed_ref[at, :]

        def step(i, ordered):
            value = jnp.take_along_axis(packed, base + i, axis=1, mode="promise_in_bounds")
            return jnp.where((value & (BLOCK - 1)) == within, value, ordered)

        ordered = lax.fori_loop(0, BLOCK, step, jnp.zeros_like(packed), unroll=8)
        out_ref[at, :] = ordered >> SHIFT


def order(packed):
    return pl.pallas_call(
        order_kernel,
        out_shape=jax.ShapeDtypeStruct(packed.shape, jnp.int32),
        in_specs=[VMEM_WHOLE],
        out_specs=VMEM_WHOLE,
        compiler_params=params(),
        cost_estimate=cost(10**6, 20 * 10**6),
        name="order",
    )(packed)


def split_kernel(ops_ref, out_ref, *, group):
    coefs = ops_ref.shape[1]

    @pl.loop(0, ops_ref.shape[0], step=group)
    def _(c):
        at = pl.ds(c, group)
        value = ops_ref[at]
        high = value.astype(jnp.bfloat16).astype(jnp.float32)
        out_ref[at] = jnp.zeros((group, KPAD, LANES), jnp.float32)
        out_ref[at, :coefs, :coefs] = high
        out_ref[at, :coefs, KPAD : KPAD + coefs] = value - high


def split(turned_ops):
    classes = turned_ops.shape[0]
    group = max(size for size in range(1, 10) if classes % size == 0)
    return pl.pallas_call(
        functools.partial(split_kernel, group=group),
        out_shape=jax.ShapeDtypeStruct((classes, KPAD, LANES), jnp.float32),
        in_specs=[VMEM_WHOLE],
        out_specs=VMEM_WHOLE,
        compiler_params=params(),
        cost_estimate=cost(10**6, 12 * 10**6),
        name="split",
    )(turned_ops)


def m2l_kernel(source_ref, class_ref, table_ref, ops_ref, out_ref, *gathered, first, turned):
    steps = source_ref.shape[0] // 8
    lanes = lane_ids((1, LANES))
    in_first = lanes < KPAD
    in_second = lanes < 2 * KPAD
    rest = jnp.zeros((LANES - COPIES * KPAD, LANES), jnp.float32)
    none = jnp.zeros((KPAD, LANES), jnp.float32)

    def one_step(step, _):
        def row(b, t):
            return table_ref[source_ref[step * 8 + b // 2, (b % 2) * BLOCK + t]]

        def gather(u, g):
            b = u * PER_WINDOW + COPIES * g
            for t in range(BLOCK):
                one, two = row(b, t), row(b + 1, t)
                three = row(b + 2, t) if g < 2 else two
                gathered[3 * u + g][t : t + 1, :] = jnp.where(
                    in_first, one, jnp.where(in_second, two, three)
                )

        def product(u, g):
            held = []
            for b in range(COPIES * g, COPIES * g + COPIES):
                if b < PER_WINDOW:
                    block = (first + step) * 2 * PER_WINDOW + u * PER_WINDOW + b
                    held.append(ops_ref[class_ref[block]])
                else:
                    held.append(none)
            weights = jnp.concatenate(held + [rest], axis=0).astype(jnp.bfloat16)
            values = gathered[3 * u + g][...]
            high = values.astype(jnp.bfloat16)
            low = (values - high.astype(jnp.float32)).astype(jnp.bfloat16)
            return jnp.dot(high, weights, preferred_element_type=jnp.float32) + jnp.dot(
                low, weights, preferred_element_type=jnp.float32
            )

        order = [(u, g) for u in range(2) for g in range(3)]
        terms = []
        for i, pair in enumerate(order):
            gather(*pair)
            if i:
                terms.append(product(*order[i - 1]))
        terms.append(product(*order[-1]))
        both = jnp.concatenate([terms[0] + terms[1] + terms[2], terms[3] + terms[4] + terms[5]], axis=0)
        both = both + pltpu.roll(both, LANES - KPAD, 1)
        if turned:
            per = out_ref.shape[2] // LANES
            slot = (IN_ROW >> (4 * (step // per))) & 7
            out_ref[slot, :, pl.ds(pl.multiple_of((step % per) * LANES, LANES), LANES)] = both.T[:KPAD]
        else:
            out_ref[pl.ds(pl.multiple_of(step * LANES, LANES), LANES), :] = both
        return 0

    lax.fori_loop(0, steps, one_step, 0)


def m2l(sources, classes, table, ops, first, steps, turned, slots):
    if turned:
        shape = (steps * LANES // slots, KPAD, slots)
    else:
        shape = (steps * LANES, LANES)
    return pl.pallas_call(
        functools.partial(m2l_kernel, first=first, turned=turned),
        out_shape=jax.ShapeDtypeStruct(shape, jnp.float32),
        in_specs=[SMEM_WHOLE, SMEM_WHOLE, VMEM_WHOLE, VMEM_WHOLE],
        out_specs=VMEM_WHOLE,
        scratch_shapes=[pltpu.VMEM((BLOCK, LANES), jnp.float32)] * 6,
        compiler_params=params(),
        cost_estimate=cost(10**6, 120 * 10**6),
        name="m2l_slots" if turned else "m2l_cells",
    )(sources[first * 8 : (first + steps) * 8], classes, as_rows(table), ops)


def add_back_kernel(list_ref, count_ref, own_ref, *refs):
    slot_refs, out_ref = refs[:4], refs[4]
    rows, sums = refs[5], refs[6:]
    slots = list_ref.shape[1]
    sums[0][...] = own_ref[...]
    for held in sums[1:]:
        held[...] = jnp.zeros_like(held)
    for n in range(8):
        for k in range(slots // LANES):
            live = (lane_ids((KPAD, LANES)) + k * LANES) < count_ref[n]
            part, place = GOT[n]
            values = jnp.where(live, slot_refs[part][place, :, k * LANES : (k + 1) * LANES], 0.0)
            at = n * slots + k * LANES
            rows[at : at + LANES, :] = spread(values)

    @pl.loop(0, slots, step=4)
    def _(first):
        for j in range(4):
            to = [pl.ds(list_ref[n, first + j], 1) for n in range(8)]
            old = [sums[n][to[n], :] for n in range(8)]
            new = [old[n] + rows[pl.ds(n * slots + first + j, 1), :] for n in range(8)]
            for n in range(8):
                sums[n][to[n], :] = new[n]

    @pl.loop(0, own_ref.shape[0] // LANES)
    def _(k):
        at = pl.ds(pl.multiple_of(k * LANES, LANES), LANES)
        parts = [held[at, :] for held in sums]
        while len(parts) > 1:
            parts = [a + b for a, b in zip(parts[::2], parts[1::2])]
        out_ref[:, at] = parts[0].T[: out_ref.shape[0]]


def add_back(proxy_list, proxy_count, own_rows, slot_fields, coef_count):
    cell_count = own_rows.shape[0]
    slots = proxy_list.shape[1]
    return pl.pallas_call(
        add_back_kernel,
        out_shape=jax.ShapeDtypeStruct((coef_count, cell_count), jnp.float32),
        in_specs=[SMEM_WHOLE, SMEM_WHOLE] + [VMEM_WHOLE] * 5,
        out_specs=VMEM_WHOLE,
        scratch_shapes=[pltpu.VMEM((8 * slots, LANES), jnp.float32)]
        + [pltpu.VMEM((cell_count, LANES), jnp.float32)] * 8,
        compiler_params=params(),
        cost_estimate=cost(10**6, 30 * 10**6),
        name="add_back",
    )(proxy_list, proxy_count, own_rows, *slot_fields)


def carve_kernel(mesh_ref, out_ref, sems, *, first):
    sources, count, rows, width = out_ref.shape
    copies = [
        pltpu.make_async_copy(
            mesh_ref.at[pl.ds(first, count), pl.ds(s * rows, rows), :], out_ref.at[s], sems.at[s]
        )
        for s in range(sources)
    ]
    for copy in copies:
        copy.start()
    for copy in copies:
        copy.wait()


def carve(mesh, first, count, sources):
    rows, width = mesh.shape[1] // sources, mesh.shape[2]
    return pl.pallas_call(
        functools.partial(carve_kernel, first=first),
        out_shape=jax.ShapeDtypeStruct((sources, count, rows, width), jnp.float32),
        in_specs=[pl.BlockSpec(memory_space=pl.ANY)],
        out_specs=VMEM_WHOLE,
        scratch_shapes=[pltpu.SemaphoreType.DMA((sources,))],
        compiler_params=params(),
        cost_estimate=cost(0, 8 * count * sources * rows * width),
        name="carve",
    )(mesh)


def first_part_kernel(mesh_ref, place_ref, cells_ref, out_ref, sems, *, count, rows):
    sources, _, width = out_ref.shape
    copies = [
        pltpu.make_async_copy(
            mesh_ref.at[p, pl.ds(s * rows, rows), :],
            out_ref.at[s, pl.ds(p * rows, rows), :],
            sems.at[p, s],
        )
        for p in range(count)
        for s in range(sources)
    ]
    for copy in copies:
        copy.start()
    is_first = lane_ids((TOP_ROWS, LANES)) < KPAD
    rest = jnp.zeros((KPAD - cells_ref.shape[0], LANES), jnp.float32)
    table = spread(jnp.concatenate([cells_ref[:, :LANES], rest], axis=0))
    top = jnp.where(is_first, table[:TOP_ROWS, :], table[TOP_ROWS : 2 * TOP_ROWS, :])
    blocks = [place_ref[...].astype(jnp.float32), cell_lines(cells_ref), top]
    at = count * rows
    for block in blocks:
        high = block.shape[0] * LANES // width
        for h in range(width // LANES):
            for s in range(sources):
                out_ref[s, at : at + high, h * LANES : (h + 1) * LANES] = block[
                    h * high : (h + 1) * high, :
                ]
        at += high
    for copy in copies:
        copy.wait()


def cell_lines(cells_ref):
    lines = [cells_ref[0:1, k : k + LANES] for k in range(0, cells_ref.shape[1], LANES)]
    return DEPOSIT_SCALE * jnp.concatenate(lines, axis=0)


def first_part(mesh, place, multipoles, sources, count):
    rows, width = mesh.shape[1] // sources, mesh.shape[2]
    extra = (2 * place.size + TOP_ROWS * LANES) // width
    return pl.pallas_call(
        functools.partial(first_part_kernel, count=count, rows=rows),
        out_shape=jax.ShapeDtypeStruct((sources, count * rows + extra, width), jnp.float32),
        in_specs=[pl.BlockSpec(memory_space=pl.ANY), VMEM_WHOLE, VMEM_WHOLE],
        out_specs=VMEM_WHOLE,
        scratch_shapes=[
            pltpu.SemaphoreType.DMA((count, sources)),
        ],
        compiler_params=params(),
        cost_estimate=cost(0, 8 * sources * rows * width),
        name="first_part",
    )(mesh, place.reshape(-1, LANES), multipoles)


def log2(value):
    return value.bit_length() - 1


def sift_kernel(mine_ref, part_ref, code_ref, lane_ref, value_ref, bound_ref, top_ref, ride, sem, *, count, planes, rows):
    sources, extra, width = ride.shape
    lines = code_ref.shape[0] // sources
    copy = pltpu.make_async_copy(part_ref.at[:, pl.ds(count * rows, extra), :], ride, sem)
    copy.start()
    copy.wait()

    def unfold(first, count):
        high = count * LANES // width
        return jnp.concatenate(
            [
                ride[s, first : first + high, h * LANES : (h + 1) * LANES]
                for s in range(sources)
                for h in range(width // LANES)
            ],
            axis=0,
        )

    step = lines * LANES // width
    place = unfold(0, lines).astype(jnp.int32)
    value = unfold(step, lines)
    top_ref[...] = unfold(2 * step, TOP_ROWS)

    row_at, mesh_rows = log2(width), rows * sources
    plane = place >> (row_at + log2(mesh_rows))
    row = (place >> row_at) & (mesh_rows - 1)
    column = place & (width - 1)
    tiles = width // LANES
    target = (plane * tiles + (column >> LANE_SHIFT)) * rows + (row & (rows - 1))
    none = planes * tiles * rows * LANES
    mine = (row >> log2(rows)) == mine_ref[0]
    lanes = lane_ids(place.shape)
    code = jnp.where(mine, target * LANES + (column & (LANES - 1)), none)
    value = jnp.where(mine, value, 0.0)
    ahead = jnp.where(mine, 1, 0)
    for b in range(LANE_SHIFT):
        ahead = ahead + jnp.where(lanes >= (1 << b), pltpu.roll(ahead, 1 << b, 1), 0)
    shift = jnp.where(mine, lanes + 1 - ahead, 0)
    for b in range(LANE_SHIFT):
        back = LANES - (1 << b)
        moves = (shift >> b) & 1
        comes = pltpu.roll(moves, back, 1) == 1
        goes = moves == 1
        code = jnp.where(comes, pltpu.roll(code, back, 1), jnp.where(goes, none, code))
        value = jnp.where(comes, pltpu.roll(value, back, 1), jnp.where(goes, 0.0, value))
        shift = jnp.where(comes, pltpu.roll(shift, back, 1), jnp.where(goes, 0, shift))
    code_ref[...] = code >> LANE_SHIFT
    lane_ref[...] = (code & (LANES - 1)).astype(jnp.float32)
    value_ref[...] = value
    counts = jnp.sum(jnp.where(mine, 1.0, 0.0), axis=1, keepdims=True)
    counts = jnp.broadcast_to(counts, mine.shape).reshape(2 * sources, lines // 2, LANES)
    bound_ref[...] = jnp.max(counts, axis=0).astype(jnp.int32)


def sift(part, mine, count, planes, rows, lines):
    sources, whole_rows, width = part.shape
    extra = whole_rows - count * rows
    shape = (sources * lines, LANES)
    return pl.pallas_call(
        functools.partial(sift_kernel, count=count, planes=planes, rows=rows),
        out_shape=(
            jax.ShapeDtypeStruct(shape, jnp.int32),
            jax.ShapeDtypeStruct(shape, jnp.float32),
            jax.ShapeDtypeStruct(shape, jnp.float32),
            jax.ShapeDtypeStruct((lines // 2, LANES), jnp.int32),
            jax.ShapeDtypeStruct((sources * TOP_ROWS, LANES), jnp.float32),
        ),
        in_specs=[SMEM_WHOLE, pl.BlockSpec(memory_space=pl.ANY)],
        out_specs=(VMEM_WHOLE,) * 5,
        scratch_shapes=[pltpu.VMEM((sources, extra, width), jnp.float32), pltpu.SemaphoreType.DMA],
        compiler_params=params(),
        cost_estimate=cost(10**6, 8 * 10**6),
        name="sift",
    )(mine, part)


def deposit_kernel(target_ref, lane_ref, value_ref, bound_ref, *refs):
    sources = len(refs) // 2
    outs, others, ready = refs[:sources], refs[sources:-1], refs[-1]
    held = outs + others
    whole = lane_ref.shape[0]
    lines = whole // (2 * sources)
    for ref in held:
        ref[...] = jnp.zeros_like(ref)

    lanes = lane_ids((LANES, LANES))
    spots = lanes.astype(jnp.float32)
    for first in range(0, whole, LANES):
        turned_lane = lane_ref[first : first + LANES, :].T
        turned_value = value_ref[first : first + LANES, :].T

        @pl.loop(0, LANES)
        def _(k):
            pick = jnp.zeros((LANES, LANES), jnp.int32) + k
            lane = jnp.take_along_axis(turned_lane, pick, axis=1, mode="promise_in_bounds")
            value = jnp.take_along_axis(turned_value, pick, axis=1, mode="promise_in_bounds")
            at = pl.multiple_of((first + k) * LANES, LANES)
            ready[pl.ds(at, LANES), :] = jnp.where(spots == lane, value, 0.0)

    def line(g, _):
        def one(j):
            at = [(2 * s + h) * lines + g for h in range(2) for s in range(sources)]
            to = [pl.ds(target_ref[i, j], 1) for i in at]
            new = [
                ref[rows, :] + ready[pl.ds(i * LANES + j, 1), :]
                for ref, rows, i in zip(held, to, at)
            ]
            for ref, rows, row in zip(held, to, new):
                ref[rows, :] = row

        def four(i, _):
            for j in range(4):
                one(4 * i + j)
            return 0

        return lax.fori_loop(0, (bound_ref[g, 0] + 3) >> 2, four, 0)

    lax.fori_loop(0, lines, line, 0)
    for out_ref, other in zip(outs, others):
        out_ref[...] = out_ref[...] + other[...]


def deposit(targets, lanes, values, bounds, rows, sources):
    return pl.pallas_call(
        deposit_kernel,
        out_shape=(jax.ShapeDtypeStruct((rows, LANES), jnp.float32),) * sources,
        in_specs=[SMEM_WHOLE, VMEM_WHOLE, VMEM_WHOLE, SMEM_WHOLE],
        out_specs=(VMEM_WHOLE,) * sources,
        scratch_shapes=[pltpu.VMEM((rows, LANES), jnp.float32)] * sources
        + [pltpu.VMEM((values.size, LANES), jnp.float32)],
        compiler_params=params(),
        cost_estimate=cost(10**6, 40 * 10**6),
        name="deposit",
    )(targets, lanes, values, bounds)


def fourier_tables(length):
    points, half = length // 2, length // 4
    positions = np.arange(points)
    scale = 1.0 / np.sqrt(length)
    parts = []
    for odd in range(2):
        ks = 2 * np.arange(half) + odd
        angles = (positions[:, None] * ks[None, :] % length) * (2.0 * np.pi / length)
        imag = -np.sin(angles) * scale
        if not odd:
            imag[:, 0] = np.where(positions % 2 == 0, scale, -scale)
        parts.append(np.concatenate([np.cos(angles) * scale, imag], axis=1))
    whole = np.stack(parts)
    high = whole.astype(ml_dtypes.bfloat16)
    low = (whole - high.astype(np.float64)).astype(ml_dtypes.bfloat16)
    return high, low


def fourier_kernel(*refs, sources):
    mesh_ref, add_refs = refs[0], refs[1 : 1 + sources]
    high_ref, low_ref = refs[1 + sources], refs[2 + sources]
    out_ref = refs[-1]
    rows, width = mesh_ref.shape[1:]
    pieces = []
    for s in range(sources):
        for h in range(width // LANES):
            pieces.append(
                mesh_ref[s, :, h * LANES : (h + 1) * LANES]
                + add_refs[s][h * rows : (h + 1) * rows, :]
            )
    mid = len(pieces) // 2
    halves = []
    for odd in range(2):
        if odd:
            folded = [a - b for a, b in zip(pieces[:mid], pieces[mid:])]
        else:
            folded = [a + b for a, b in zip(pieces[:mid], pieces[mid:])]
        values = jnp.concatenate(folded, axis=1)
        high = values.astype(jnp.bfloat16)
        low = (values - high.astype(jnp.float32)).astype(jnp.bfloat16)
        both = jnp.dot(
            jnp.concatenate([high, low], axis=0), high_ref[odd], preferred_element_type=jnp.float32
        )
        halves.append(
            both[:rows]
            + both[rows:]
            + jnp.dot(high, low_ref[odd], preferred_element_type=jnp.float32)
        )
    lanes = lane_ids((rows, LANES))
    is_first = lanes == 0
    is_odd = (lanes & 1) == 1
    steps = lanes >> 1
    tiles = len(pieces)
    per = tiles // 4

    def tile(odd, part, j):
        at = (part * per + j) * LANES
        return halves[odd][:, at : at + LANES]

    def pick(value, lane):
        return jnp.take_along_axis(value, lane, axis=1, mode="promise_in_bounds")

    for j in range(tiles):
        for part in range(2):
            if j < tiles // 2:
                at = BLOCK * j
                lane = (at % LANES) + steps
                even = pick(tile(0, part, at // LANES), lane)
                odd = pick(tile(1, part, at // LANES), lane)
                if j == 0 and part == 1:
                    even = jnp.where(is_first, 0.0, even)
            else:
                at = BLOCK * (tiles - j)
                last = (at - 1) // LANES
                even = pick(tile(0, part, last), (at - steps) & (LANES - 1))
                odd = pick(tile(1, part, last), ((at - 1) % LANES) - steps)
                if at % LANES == 0 and j > tiles // 2:
                    even = jnp.where(is_first, tile(0, part, at // LANES), even)
                if part == 1:
                    even, odd = -even, -odd
                if j == tiles // 2:
                    even = jnp.where(is_first, 0.0 if part else tile(0, 1, 0), even)
            out_ref[part, 0, :, j * LANES : (j + 1) * LANES] = jnp.where(is_odd, odd, even)


def fourier(mesh_part, count, adds, tables, first, planes, so_far, rows):
    sources, _, width = mesh_part.shape
    length = sources * width
    add_rows = (width // LANES) * rows
    operands = [mesh_part, *adds, *tables]
    in_specs = (
        [pl.BlockSpec((sources, rows, width), lambda p: (0, p, 0))]
        + [pl.BlockSpec((add_rows, LANES), lambda p: (first + p, 0))] * sources
        + [
            pl.BlockSpec((2, length // 2, length // 2), lambda p: (0, 0, 0), pipeline_mode=pl.Buffered(1))
        ]
        * 2
    )
    aliases = {}
    if so_far is not None:
        aliases = {len(operands): 0}
        operands.append(so_far)
        in_specs.append(pl.BlockSpec(memory_space=pl.ANY))
    return pl.pallas_call(
        functools.partial(fourier_kernel, sources=sources),
        grid=(count,),
        out_shape=jax.ShapeDtypeStruct((2, planes, rows, length), jnp.float32),
        in_specs=in_specs,
        out_specs=pl.BlockSpec((2, 1, rows, length), lambda p: (0, first + p, 0, 0)),
        input_output_aliases=aliases,
        compiler_params=params(),
        cost_estimate=cost(10**6, count * 10 * 10**6),
        name="fourier",
    )(*operands)


def after(value, *others):
    return lax.optimization_barrier((value, *others))[0]


def on_device(
    multipoles,
    proxy_list,
    proxy_count,
    pair_source,
    pair_target,
    block_class,
    m2l_ops,
    cell_mesh,
    pm_density,
    *,
    n_gx,
    n_gy,
):
    coef_count, cell_count = multipoles.shape
    slots = proxy_list.shape[2]
    planes, mesh_rows, width = pm_density.shape
    own_rows = mesh_rows // n_gx
    domains = n_gx * n_gy
    lists, counts = proxy_list[0], proxy_count[0]

    def send(part):
        return lax.all_to_all(part, "gx", 0, 0, tiled=True)

    spans = []
    first = 0
    for size in CHUNKS:
        spans.append((first, size))
        first += size

    parts = [send(first_part(pm_density, cell_mesh, multipoles, n_gx, spans[0][1]))]
    carved = [
        carve(pm_density, at, size, n_gx).reshape(n_gx, size * own_rows, width)
        for at, size in spans[1:]
    ]

    cells = jnp.pad(multipoles, ((0, KPAD - coef_count), (0, 0)))
    base = cell_count + 8 * slots
    table = own_table(cells, base + TOP * domains)
    outgoing = pack(table, cell_count, lists, counts)
    arrived = exchange(*outgoing)

    top = pair_source - base
    domain = top >> log2(TOP)
    along = (domain & (n_gy - 1)) ^ lax.axis_index("gy")
    place = (along * n_gx + (domain >> log2(n_gy))) * TOP_ROWS + (top & (TOP_ROWS - 1))
    top = base + ((top >> log2(TOP_ROWS)) & 1) * (TOP_ROWS * domains) + place
    wanted = jnp.where(pair_source < base, pair_source, top)
    sources = order(((wanted << SHIFT) | (pair_target & (BLOCK - 1))).reshape(-1, LANES))

    ops = split(m2l_ops.transpose(0, 2, 1))

    tiles = width // LANES
    add_rows = planes * tiles * own_rows
    mine = lax.axis_index("gx").astype(jnp.int32).reshape(1)
    targets, spots, amounts, bounds, top_own = sift(
        parts[0], mine, spans[0][1], planes, own_rows, cell_count // LANES
    )
    tops = [top_own]
    for bit in range(log2(n_gy)):
        held = jnp.concatenate(tops, axis=0) if bit else top_own
        tops.append(lax.ppermute(held, "gy", [(i, i ^ (1 << bit)) for i in range(n_gy)]))

    parts.append(send(after(carved[0], parts[0], sources, ops, *arrived)))
    adds = deposit(targets, spots, amounts, bounds, add_rows + 8, n_gx)
    table = whole_table(table, arrived, tops)
    cell_steps = cell_count // LANES
    slot_steps = 8 * slots // LANES
    slot_fields = m2l(sources, block_class, table, ops, cell_steps, slot_steps, True, slots)
    returned = exchange(slot_fields[:3], slot_fields[3:6], slot_fields[6:], adds[0])
    own_fields = m2l(sources, block_class, table, ops, 0, cell_steps, False, slots)
    parts.append(send(after(carved[1], parts[1], own_fields, *returned)))

    tables = fourier_tables(n_gx * width)
    spectrum = None
    for part, (at, size) in zip(parts, spans):
        spectrum = fourier(part, size, adds, tables, at, planes, spectrum, own_rows)

    field_tensors = add_back(lists, counts, own_fields, returned, coef_count)
    return (field_tensors, spectrum)


def solution(mesh):
    placed = (
        P(None, ("gx", "gy")),
        P(("gx", "gy"), None, None),
        P(("gx", "gy"), None),
        P(("gx", "gy")),
        P(("gx", "gy")),
        P(("gx", "gy")),
        P(),
        P(("gx", "gy")),
        P("gy", None, "gx"),
    )
    return jax.shard_map(
        functools.partial(on_device, n_gx=mesh.shape["gx"], n_gy=mesh.shape["gy"]),
        mesh=mesh,
        in_specs=placed,
        out_specs=(P(None, ("gx", "gy")), P(None, "gy", "gx", None)),
        check_vma=False,
    )
```

```python
import functools

import jax
import jax.numpy as jnp
import ml_dtypes
import numpy as np
from jax import lax
from jax.experimental import pallas as pl
from jax.experimental.pallas import tpu as pltpu
from jax.sharding import PartitionSpec as P

TOP = 32
BLOCK = 64
LANES = 128
KPAD = 40
COPIES = 3
PER_WINDOW = 8
SHIFT = 6
LANE_SHIFT = 7
MIB = 1024 * 1024
CHUNKS = (2, 3, 3)
TOP_ROWS = TOP // 2

DEPOSIT_SCALE = 8.0
SENT = ((0, 0), (2, 0), (1, 0), (0, 1), (1, 1), (0, 2), (2, 1), (1, 2))
GOT = ((3, 2), (3, 1), (3, 0), (1, 1), (0, 1), (2, 2), (2, 1), (2, 0))
IN_ROW = 0x57241360

SMEM_WHOLE = pl.BlockSpec(memory_space=pltpu.SMEM)
VMEM_WHOLE = pl.BlockSpec(memory_space=pltpu.VMEM)


def params(mebibytes):
    return pltpu.CompilerParams(vmem_limit_bytes=mebibytes * MIB)


def cost(flops, nbytes):
    return pl.CostEstimate(flops=flops, bytes_accessed=nbytes, transcendentals=0)


def spread(block):
    rest = jnp.zeros((LANES - COPIES * KPAD, LANES), jnp.float32)
    return jnp.concatenate([block] * COPIES + [rest], axis=0).T


def lane_ids(shape):
    return lax.broadcasted_iota(jnp.int32, shape, len(shape) - 1)


def own_table_kernel(cells_ref, out_ref):
    @pl.loop(0, cells_ref.shape[1] // LANES)
    def _(k):
        at = pl.multiple_of(k * LANES, LANES)
        out_ref[pl.ds(at, LANES), :] = spread(cells_ref[:, pl.ds(at, LANES)])


def own_table(cells, rows):
    count = cells.shape[1]
    return pl.pallas_call(
        own_table_kernel,
        grid=(1,),
        out_shape=jax.ShapeDtypeStruct((rows, LANES), jnp.float32),
        in_specs=[pl.BlockSpec((KPAD, count), lambda i: (0, 0))],
        out_specs=pl.BlockSpec((count, LANES), lambda i: (0, 0)),
        compiler_params=params(12),
        cost_estimate=cost(10**6, 12 * 10**6),
        name="own_table",
    )(cells)


def cut_rows(refs, first, stop):
    pieces, at = [], 0
    for ref in refs:
        low, high = max(first - at, 0), min(stop - at, ref.shape[0])
        if low < high:
            pieces.append(ref[low:high, :])
        at += ref.shape[0]
    return jnp.concatenate(pieces, axis=0) if len(pieces) > 1 else pieces[0]


def whole_table_kernel(*refs, slot_steps):
    top_refs, out_ref = refs[4:-2], refs[-1]
    step = pl.program_id(0)
    for k in range(slot_steps):

        @pl.when(step == k)
        def _():
            at = 0
            for n in (2 * k, 2 * k + 1):
                part, place = GOT[n]
                for c in range(refs[part].shape[2] // LANES):
                    block = refs[part][place, :, c * LANES : (c + 1) * LANES]
                    out_ref[at : at + LANES, :] = spread(block)
                    at += LANES

    rows = out_ref.shape[0]
    total = sum(ref.shape[0] for ref in top_refs)
    lanes = lane_ids((rows, LANES))
    for k in range(2 * total // rows):

        @pl.when(step == slot_steps + k)
        def _():
            pieces = []
            for first in range(k * rows, (k + 1) * rows, min(rows, total)):
                group, at = first // total, first % total
                value = cut_rows(top_refs, at, at + min(rows, total))
                pieces.append(pltpu.roll(value, LANES - KPAD, 1) if group else value)
            value = jnp.concatenate(pieces, axis=0) if len(pieces) > 1 else pieces[0]
            value = jnp.where(lanes < KPAD, value, 0.0)
            out_ref[...] = value + pltpu.roll(value, KPAD, 1) + pltpu.roll(value, 2 * KPAD, 1)


def whole_table(table, arrived, tops):
    slots = arrived[0].shape[2]
    rows = 2 * slots
    top_rows = 2 * sum(part.shape[0] for part in tops)
    first = (table.shape[0] - 8 * slots - top_rows) // rows
    return pl.pallas_call(
        functools.partial(whole_table_kernel, slot_steps=4),
        grid=(4 + top_rows // rows,),
        out_shape=jax.ShapeDtypeStruct(table.shape, jnp.float32),
        in_specs=[VMEM_WHOLE] * (4 + len(tops)) + [pl.BlockSpec(memory_space=pl.ANY)],
        out_specs=pl.BlockSpec((rows, LANES), lambda i: (first + i, 0)),
        input_output_aliases={4 + len(tops): 0},
        compiler_params=params(12),
        cost_estimate=cost(10**6, 16 * 10**6),
        name="whole_table",
    )(*arrived, *tops, table)


def as_rows(table):
    return table.reshape(table.shape[0], 1, LANES)


def pack_kernel(list_ref, count_ref, table_ref, *refs):
    outs, held = refs[:3], refs[3:]
    slot_tiles = list_ref.shape[1] // LANES
    for n in range(8):

        @pl.loop(0, slot_tiles, step=len(held))
        def _(i):
            firsts = [pl.multiple_of((i + k) * LANES, LANES) for k in range(len(held))]
            for first, rows in zip(firsts, held):
                for r in range(LANES):
                    rows[r : r + 1, :] = table_ref[list_ref[n, first + r]]
            for first, rows in zip(firsts, held):
                live = (lane_ids((KPAD, LANES)) + first) < count_ref[n]
                part, at = SENT[n]
                outs[part][at, :, pl.ds(first, LANES)] = jnp.where(live, rows[...].T[:KPAD], 0.0)


def pack(table, cell_count, proxy_list, proxy_count):
    slots = proxy_list.shape[1]
    return pl.pallas_call(
        pack_kernel,
        grid=(1,),
        out_shape=tuple(jax.ShapeDtypeStruct((size, KPAD, slots), jnp.float32) for size in (3, 3, 2)),
        in_specs=[
            SMEM_WHOLE,
            SMEM_WHOLE,
            pl.BlockSpec((cell_count, 1, LANES), lambda i: (0, 0, 0)),
        ],
        out_specs=tuple(
            pl.BlockSpec((size, KPAD, slots), lambda i: (0, 0, 0)) for size in (3, 3, 2)
        ),
        scratch_shapes=[pltpu.VMEM((LANES, LANES), jnp.float32)] * 2,
        compiler_params=params(12),
        cost_estimate=cost(10**6, 25 * 10**6),
        name="pack",
    )(proxy_list, proxy_count, as_rows(table))


def exchange(down, up, mid, *before_gx):
    def shift(value, axis, by):
        count = lax.axis_size(axis)
        return lax.ppermute(value, axis, [(i, (i + by) % count) for i in range(count)])

    down, up = shift(down, "gy", -1), shift(up, "gy", 1)
    if before_gx:
        mid = after(mid, *before_gx)
    left = shift(jnp.stack([down[0], mid[0], up[0]]), "gx", -1)
    right = shift(jnp.stack([down[2], mid[1], up[2]]), "gx", 1)
    return down, up, left, right


def order_kernel(packed_ref, out_ref):
    lanes = lane_ids((LANES, LANES))
    within = lanes & (BLOCK - 1)
    base = lanes - within

    @pl.loop(0, packed_ref.shape[0] // LANES)
    def _(k):
        at = pl.ds(pl.multiple_of(k * LANES, LANES), LANES)
        packed = packed_ref[at, :]

        def step(i, ordered):
            value = jnp.take_along_axis(packed, base + i, axis=1, mode="promise_in_bounds")
            return jnp.where((value & (BLOCK - 1)) == within, value, ordered)

        ordered = lax.fori_loop(0, BLOCK, step, jnp.zeros_like(packed), unroll=8)
        out_ref[at, :] = ordered >> SHIFT


def order(packed):
    return pl.pallas_call(
        order_kernel,
        out_shape=jax.ShapeDtypeStruct(packed.shape, jnp.int32),
        in_specs=[VMEM_WHOLE],
        out_specs=VMEM_WHOLE,
        compiler_params=params(6),
        cost_estimate=cost(10**6, 20 * 10**6),
        name="order",
    )(packed)


def split_kernel(ops_ref, out_ref, *, group):
    coefs = ops_ref.shape[1]

    @pl.loop(0, ops_ref.shape[0], step=group)
    def _(c):
        at = pl.ds(c, group)
        value = ops_ref[at]
        high = value.astype(jnp.bfloat16).astype(jnp.float32)
        out_ref[at] = jnp.zeros((group, KPAD, LANES), jnp.float32)
        out_ref[at, :coefs, :coefs] = high
        out_ref[at, :coefs, KPAD : KPAD + coefs] = value - high


def split(turned_ops):
    classes = turned_ops.shape[0]
    group = max(size for size in range(1, 10) if classes % size == 0)
    return pl.pallas_call(
        functools.partial(split_kernel, group=group),
        out_shape=jax.ShapeDtypeStruct((classes, KPAD, LANES), jnp.float32),
        in_specs=[VMEM_WHOLE],
        out_specs=VMEM_WHOLE,
        compiler_params=params(16),
        cost_estimate=cost(10**6, 12 * 10**6),
        name="split",
    )(turned_ops)


def m2l_kernel(source_ref, class_ref, table_ref, ops_ref, out_ref, *refs, first, turned):
    gathered, indices, sems = refs[:6], refs[6:8], refs[8]
    steps = source_ref.shape[0] // 8
    lanes = lane_ids((1, LANES))
    in_first = lanes < KPAD
    in_second = lanes < 2 * KPAD
    rest = jnp.zeros((LANES - COPIES * KPAD, LANES), jnp.float32)
    none = jnp.zeros((KPAD, LANES), jnp.float32)

    def fetch(step, slot):
        rows = pl.ds(pl.multiple_of(step * 8, 8), 8)
        return pltpu.make_async_copy(source_ref.at[rows, :], indices[slot], sems.at[slot])

    def one_step(step, slot):
        def row(b, t):
            return table_ref[indices[slot][b // 2, (b % 2) * BLOCK + t]]

        def gather(u, g):
            b = u * PER_WINDOW + COPIES * g
            for t in range(BLOCK):
                one, two = row(b, t), row(b + 1, t)
                three = row(b + 2, t) if g < 2 else two
                gathered[3 * u + g][t : t + 1, :] = jnp.where(
                    in_first, one, jnp.where(in_second, two, three)
                )

        def product(u, g):
            held = []
            for b in range(COPIES * g, COPIES * g + COPIES):
                if b < PER_WINDOW:
                    block = (first + step) * 2 * PER_WINDOW + u * PER_WINDOW + b
                    held.append(ops_ref[class_ref[block]])
                else:
                    held.append(none)
            weights = jnp.concatenate(held + [rest], axis=0).astype(jnp.bfloat16)
            values = gathered[3 * u + g][...]
            high = values.astype(jnp.bfloat16)
            low = (values - high.astype(jnp.float32)).astype(jnp.bfloat16)
            return jnp.dot(high, weights, preferred_element_type=jnp.float32) + jnp.dot(
                low, weights, preferred_element_type=jnp.float32
            )

        order = [(u, g) for u in range(2) for g in range(3)]
        terms = []
        for i, pair in enumerate(order):
            gather(*pair)
            if i:
                terms.append(product(*order[i - 1]))
        terms.append(product(*order[-1]))
        both = jnp.concatenate([terms[0] + terms[1] + terms[2], terms[3] + terms[4] + terms[5]], axis=0)
        both = both + pltpu.roll(both, LANES - KPAD, 1)
        if turned:
            per = out_ref.shape[2] // LANES
            slot = (IN_ROW >> (4 * (step // per))) & 7
            out_ref[slot, :, pl.ds(pl.multiple_of((step % per) * LANES, LANES), LANES)] = both.T[:KPAD]
        else:
            out_ref[pl.ds(pl.multiple_of(step * LANES, LANES), LANES), :] = both

    fetch(0, 0).start()

    @pl.loop(0, steps // 2)
    def _(i):
        fetch(2 * i, 0).wait()
        fetch(2 * i + 1, 1).start()
        one_step(2 * i, 0)
        fetch(2 * i + 1, 1).wait()

        @pl.when(i < steps // 2 - 1)
        def _():
            fetch(2 * i + 2, 0).start()

        one_step(2 * i + 1, 1)


def m2l(sources, classes, table, ops, first, steps, turned, slots):
    if turned:
        shape = (steps * LANES // slots, KPAD, slots)
    else:
        shape = (steps * LANES, LANES)
    return pl.pallas_call(
        functools.partial(m2l_kernel, first=first, turned=turned),
        out_shape=jax.ShapeDtypeStruct(shape, jnp.float32),
        in_specs=[VMEM_WHOLE, SMEM_WHOLE, VMEM_WHOLE, VMEM_WHOLE],
        out_specs=VMEM_WHOLE,
        scratch_shapes=[pltpu.VMEM((BLOCK, LANES), jnp.float32)] * 6
        + [pltpu.SMEM((8, LANES), jnp.int32)] * 2
        + [pltpu.SemaphoreType.DMA((2,))],
        compiler_params=params(20),
        cost_estimate=cost(10**6, 120 * 10**6),
        name="m2l_slots" if turned else "m2l_cells",
    )(sources[first * 8 : (first + steps) * 8], classes, as_rows(table), ops)


def add_back_kernel(list_ref, count_ref, own_ref, *refs):
    slot_refs, out_ref = refs[:4], refs[4]
    rows, sums = refs[5], refs[6:]
    slots = list_ref.shape[1]
    sums[0][...] = own_ref[...]
    for held in sums[1:]:
        held[...] = jnp.zeros_like(held)
    for n in range(8):
        for k in range(slots // LANES):
            live = (lane_ids((KPAD, LANES)) + k * LANES) < count_ref[n]
            part, place = GOT[n]
            values = jnp.where(live, slot_refs[part][place, :, k * LANES : (k + 1) * LANES], 0.0)
            at = n * slots + k * LANES
            rows[at : at + LANES, :] = spread(values)

    @pl.loop(0, slots, step=4)
    def _(first):
        for j in range(4):
            to = [pl.ds(list_ref[n, first + j], 1) for n in range(8)]
            old = [sums[n][to[n], :] for n in range(8)]
            new = [old[n] + rows[pl.ds(n * slots + first + j, 1), :] for n in range(8)]
            for n in range(8):
                sums[n][to[n], :] = new[n]

    @pl.loop(0, own_ref.shape[0] // LANES)
    def _(k):
        at = pl.ds(pl.multiple_of(k * LANES, LANES), LANES)
        parts = [held[at, :] for held in sums]
        while len(parts) > 1:
            parts = [a + b for a, b in zip(parts[::2], parts[1::2])]
        out_ref[:, at] = parts[0].T[: out_ref.shape[0]]


def add_back(proxy_list, proxy_count, own_rows, slot_fields, coef_count):
    cell_count = own_rows.shape[0]
    slots = proxy_list.shape[1]
    return pl.pallas_call(
        add_back_kernel,
        out_shape=jax.ShapeDtypeStruct((coef_count, cell_count), jnp.float32),
        in_specs=[SMEM_WHOLE, SMEM_WHOLE] + [VMEM_WHOLE] * 5,
        out_specs=VMEM_WHOLE,
        scratch_shapes=[pltpu.VMEM((8 * slots, LANES), jnp.float32)]
        + [pltpu.VMEM((cell_count, LANES), jnp.float32)] * 8,
        compiler_params=params(30),
        cost_estimate=cost(10**6, 30 * 10**6),
        name="add_back",
    )(proxy_list, proxy_count, own_rows, *slot_fields)


def carve_kernel(mesh_ref, out_ref, sems, *, first):
    sources, count, rows, width = out_ref.shape
    copies = [
        pltpu.make_async_copy(
            mesh_ref.at[pl.ds(first, count), pl.ds(s * rows, rows), :], out_ref.at[s], sems.at[s]
        )
        for s in range(sources)
    ]
    for copy in copies:
        copy.start()
    for copy in copies:
        copy.wait()


def carve(mesh, first, count, sources):
    rows, width = mesh.shape[1] // sources, mesh.shape[2]
    return pl.pallas_call(
        functools.partial(carve_kernel, first=first),
        out_shape=jax.ShapeDtypeStruct((sources, count, rows, width), jnp.float32),
        in_specs=[pl.BlockSpec(memory_space=pl.ANY)],
        out_specs=VMEM_WHOLE,
        scratch_shapes=[pltpu.SemaphoreType.DMA((sources,))],
        compiler_params=params(12),
        cost_estimate=cost(0, 8 * count * sources * rows * width),
        name="carve",
    )(mesh)


def first_part_kernel(mesh_ref, place_ref, cells_ref, out_ref, sems, *, count, rows):
    sources, _, width = out_ref.shape
    copies = [
        pltpu.make_async_copy(
            mesh_ref.at[p, pl.ds(s * rows, rows), :],
            out_ref.at[s, pl.ds(p * rows, rows), :],
            sems.at[p, s],
        )
        for p in range(count)
        for s in range(sources)
    ]
    for copy in copies:
        copy.start()
    is_first = lane_ids((TOP_ROWS, LANES)) < KPAD
    rest = jnp.zeros((KPAD - cells_ref.shape[0], LANES), jnp.float32)
    table = spread(jnp.concatenate([cells_ref[:, :LANES], rest], axis=0))
    top = jnp.where(is_first, table[:TOP_ROWS, :], table[TOP_ROWS : 2 * TOP_ROWS, :])
    blocks = [place_ref[...].astype(jnp.float32), cell_lines(cells_ref), top]
    at = count * rows
    for block in blocks:
        high = block.shape[0] * LANES // width
        for h in range(width // LANES):
            for s in range(sources):
                out_ref[s, at : at + high, h * LANES : (h + 1) * LANES] = block[
                    h * high : (h + 1) * high, :
                ]
        at += high
    for copy in copies:
        copy.wait()


def cell_lines(cells_ref):
    lines = [cells_ref[0:1, k : k + LANES] for k in range(0, cells_ref.shape[1], LANES)]
    return DEPOSIT_SCALE * jnp.concatenate(lines, axis=0)


def first_part(mesh, place, multipoles, sources, count):
    rows, width = mesh.shape[1] // sources, mesh.shape[2]
    extra = (2 * place.size + TOP_ROWS * LANES) // width
    return pl.pallas_call(
        functools.partial(first_part_kernel, count=count, rows=rows),
        out_shape=jax.ShapeDtypeStruct((sources, count * rows + extra, width), jnp.float32),
        in_specs=[pl.BlockSpec(memory_space=pl.ANY), VMEM_WHOLE, VMEM_WHOLE],
        out_specs=VMEM_WHOLE,
        scratch_shapes=[
            pltpu.SemaphoreType.DMA((count, sources)),
        ],
        compiler_params=params(10),
        cost_estimate=cost(0, 8 * sources * rows * width),
        name="first_part",
    )(mesh, place.reshape(-1, LANES), multipoles)


def log2(value):
    return value.bit_length() - 1


def sift_kernel(mine_ref, part_ref, code_ref, value_ref, bound_ref, top_ref, ride, sem, *, count, planes, rows):
    sources, extra, width = ride.shape
    lines = code_ref.shape[0] // sources
    copy = pltpu.make_async_copy(part_ref.at[:, pl.ds(count * rows, extra), :], ride, sem)
    copy.start()
    copy.wait()

    def unfold(first, count):
        high = count * LANES // width
        return jnp.concatenate(
            [
                ride[s, first : first + high, h * LANES : (h + 1) * LANES]
                for s in range(sources)
                for h in range(width // LANES)
            ],
            axis=0,
        )

    step = lines * LANES // width
    place = unfold(0, lines).astype(jnp.int32)
    value = unfold(step, lines)
    top_ref[...] = unfold(2 * step, TOP_ROWS)

    row_at, mesh_rows = log2(width), rows * sources
    plane = place >> (row_at + log2(mesh_rows))
    row = (place >> row_at) & (mesh_rows - 1)
    column = place & (width - 1)
    tiles = width // LANES
    target = (plane * tiles + (column >> LANE_SHIFT)) * rows + (row & (rows - 1))
    none = planes * tiles * rows * LANES
    mine = (row >> log2(rows)) == mine_ref[0]
    lanes = lane_ids(place.shape)
    code = jnp.where(mine, target * LANES + (column & (LANES - 1)), none)
    value = jnp.where(mine, value, 0.0)
    ahead = jnp.where(mine, 1, 0)
    for b in range(LANE_SHIFT):
        ahead = ahead + jnp.where(lanes >= (1 << b), pltpu.roll(ahead, 1 << b, 1), 0)
    shift = jnp.where(mine, lanes + 1 - ahead, 0)
    for b in range(LANE_SHIFT):
        back = LANES - (1 << b)
        moves = (shift >> b) & 1
        comes = pltpu.roll(moves, back, 1) == 1
        goes = moves == 1
        code = jnp.where(comes, pltpu.roll(code, back, 1), jnp.where(goes, none, code))
        value = jnp.where(comes, pltpu.roll(value, back, 1), jnp.where(goes, 0.0, value))
        shift = jnp.where(comes, pltpu.roll(shift, back, 1), jnp.where(goes, 0, shift))
    code_ref[...] = code
    value_ref[...] = value
    counts = jnp.sum(jnp.where(mine, 1.0, 0.0), axis=1, keepdims=True)
    counts = jnp.broadcast_to(counts, mine.shape).reshape(2 * sources, lines // 2, LANES)
    bound_ref[...] = jnp.max(counts, axis=0).astype(jnp.int32)


def sift(part, mine, count, planes, rows, lines):
    sources, whole_rows, width = part.shape
    extra = whole_rows - count * rows
    shape = (sources * lines, LANES)
    return pl.pallas_call(
        functools.partial(sift_kernel, count=count, planes=planes, rows=rows),
        out_shape=(
            jax.ShapeDtypeStruct(shape, jnp.int32),
            jax.ShapeDtypeStruct(shape, jnp.float32),
            jax.ShapeDtypeStruct((lines // 2, LANES), jnp.int32),
            jax.ShapeDtypeStruct((sources * TOP_ROWS, LANES), jnp.float32),
        ),
        in_specs=[SMEM_WHOLE, pl.BlockSpec(memory_space=pl.ANY)],
        out_specs=(VMEM_WHOLE,) * 4,
        scratch_shapes=[pltpu.VMEM((sources, extra, width), jnp.float32), pltpu.SemaphoreType.DMA],
        compiler_params=params(8),
        cost_estimate=cost(10**6, 8 * 10**6),
        name="sift",
    )(mine, part)


def deposit_kernel(code_ref, value_ref, bound_ref, *refs):
    sources = len(refs) // 2
    outs, others = refs[:sources], refs[sources:]
    lines = code_ref.shape[0] // (2 * sources)
    lanes = lane_ids((1, LANES))
    for held in refs:
        held[...] = jnp.zeros_like(held)

    def line(g, _):
        def one(j):
            at = [((2 * s + h) * lines + g, j) for h in range(2) for s in range(sources)]
            codes = [code_ref[i] for i in at]
            to = [pl.ds(code >> LANE_SHIFT, 1) for code in codes]
            old = [held[rows, :] for held, rows in zip(refs, to)]
            new = [
                row + jnp.where(lanes == (code & (LANES - 1)), value_ref[i], 0.0)
                for row, code, i in zip(old, codes, at)
            ]
            for held, rows, row in zip(refs, to, new):
                held[rows, :] = row

        def four(i, _):
            for j in range(4):
                one(4 * i + j)
            return 0

        return lax.fori_loop(0, (bound_ref[g, 0] + 3) >> 2, four, 0)

    lax.fori_loop(0, lines, line, 0)
    for out_ref, held in zip(outs, others):
        out_ref[...] = out_ref[...] + held[...]


def deposit(codes, values, bounds, rows, sources):
    return pl.pallas_call(
        deposit_kernel,
        out_shape=(jax.ShapeDtypeStruct((rows, LANES), jnp.float32),) * sources,
        in_specs=[SMEM_WHOLE] * 3,
        out_specs=(VMEM_WHOLE,) * sources,
        scratch_shapes=[pltpu.VMEM((rows, LANES), jnp.float32)] * sources,
        compiler_params=params(26),
        cost_estimate=cost(10**6, 40 * 10**6),
        name="deposit",
    )(codes, values, bounds)


def fourier_tables(length):
    points, half = length // 2, length // 4
    positions = np.arange(points)
    scale = 1.0 / np.sqrt(length)
    parts = []
    for odd in range(2):
        ks = 2 * np.arange(half) + odd
        angles = (positions[:, None] * ks[None, :] % length) * (2.0 * np.pi / length)
        imag = -np.sin(angles) * scale
        if not odd:
            imag[:, 0] = np.where(positions % 2 == 0, scale, -scale)
        parts.append(np.concatenate([np.cos(angles) * scale, imag], axis=1))
    whole = np.stack(parts)
    high = whole.astype(ml_dtypes.bfloat16)
    low = (whole - high.astype(np.float64)).astype(ml_dtypes.bfloat16)
    return high, low


def fourier_kernel(*refs, sources):
    mesh_ref, add_refs = refs[0], refs[1 : 1 + sources]
    high_ref, low_ref = refs[1 + sources], refs[2 + sources]
    out_ref = refs[-1]
    rows, width = mesh_ref.shape[1:]
    pieces = []
    for s in range(sources):
        for h in range(width // LANES):
            pieces.append(
                mesh_ref[s, :, h * LANES : (h + 1) * LANES]
                + add_refs[s][h * rows : (h + 1) * rows, :]
            )
    mid = len(pieces) // 2
    halves = []
    for odd in range(2):
        if odd:
            folded = [a - b for a, b in zip(pieces[:mid], pieces[mid:])]
        else:
            folded = [a + b for a, b in zip(pieces[:mid], pieces[mid:])]
        values = jnp.concatenate(folded, axis=1)
        high = values.astype(jnp.bfloat16)
        low = (values - high.astype(jnp.float32)).astype(jnp.bfloat16)
        both = jnp.dot(
            jnp.concatenate([high, low], axis=0), high_ref[odd], preferred_element_type=jnp.float32
        )
        halves.append(
            both[:rows]
            + both[rows:]
            + jnp.dot(high, low_ref[odd], preferred_element_type=jnp.float32)
        )
    lanes = lane_ids((rows, LANES))
    is_first = lanes == 0
    is_odd = (lanes & 1) == 1
    steps = lanes >> 1
    tiles = len(pieces)
    per = tiles // 4

    def tile(odd, part, j):
        at = (part * per + j) * LANES
        return halves[odd][:, at : at + LANES]

    def pick(value, lane):
        return jnp.take_along_axis(value, lane, axis=1, mode="promise_in_bounds")

    for j in range(tiles):
        for part in range(2):
            if j < tiles // 2:
                at = BLOCK * j
                lane = (at % LANES) + steps
                even = pick(tile(0, part, at // LANES), lane)
                odd = pick(tile(1, part, at // LANES), lane)
                if j == 0 and part == 1:
                    even = jnp.where(is_first, 0.0, even)
            else:
                at = BLOCK * (tiles - j)
                last = (at - 1) // LANES
                even = pick(tile(0, part, last), (at - steps) & (LANES - 1))
                odd = pick(tile(1, part, last), ((at - 1) % LANES) - steps)
                if at % LANES == 0 and j > tiles // 2:
                    even = jnp.where(is_first, tile(0, part, at // LANES), even)
                if part == 1:
                    even, odd = -even, -odd
                if j == tiles // 2:
                    even = jnp.where(is_first, 0.0 if part else tile(0, 1, 0), even)
            out_ref[part, 0, :, j * LANES : (j + 1) * LANES] = jnp.where(is_odd, odd, even)


def fourier(mesh_part, count, adds, tables, first, planes, so_far, rows):
    sources, _, width = mesh_part.shape
    length = sources * width
    add_rows = (width // LANES) * rows
    operands = [mesh_part, *adds, *tables]
    in_specs = (
        [pl.BlockSpec((sources, rows, width), lambda p: (0, p, 0))]
        + [pl.BlockSpec((add_rows, LANES), lambda p: (first + p, 0))] * sources
        + [
            pl.BlockSpec((2, length // 2, length // 2), lambda p: (0, 0, 0), pipeline_mode=pl.Buffered(1))
        ]
        * 2
    )
    aliases = {}
    if so_far is not None:
        aliases = {len(operands): 0}
        operands.append(so_far)
        in_specs.append(pl.BlockSpec(memory_space=pl.ANY))
    return pl.pallas_call(
        functools.partial(fourier_kernel, sources=sources),
        grid=(count,),
        out_shape=jax.ShapeDtypeStruct((2, planes, rows, length), jnp.float32),
        in_specs=in_specs,
        out_specs=pl.BlockSpec((2, 1, rows, length), lambda p: (0, first + p, 0, 0)),
        input_output_aliases=aliases,
        compiler_params=params(24),
        cost_estimate=cost(10**6, count * 10 * 10**6),
        name="fourier",
    )(*operands)


def after(value, *others):
    return lax.optimization_barrier((value, *others))[0]


def on_device(
    multipoles,
    proxy_list,
    proxy_count,
    pair_source,
    pair_target,
    block_class,
    m2l_ops,
    cell_mesh,
    pm_density,
    *,
    n_gx,
    n_gy,
):
    coef_count, cell_count = multipoles.shape
    slots = proxy_list.shape[2]
    planes, mesh_rows, width = pm_density.shape
    own_rows = mesh_rows // n_gx
    domains = n_gx * n_gy
    lists, counts = proxy_list[0], proxy_count[0]

    def send(part):
        return lax.all_to_all(part, "gx", 0, 0, tiled=True)

    spans = []
    first = 0
    for size in CHUNKS:
        spans.append((first, size))
        first += size

    parts = [send(first_part(pm_density, cell_mesh, multipoles, n_gx, spans[0][1]))]
    carved = [
        carve(pm_density, at, size, n_gx).reshape(n_gx, size * own_rows, width)
        for at, size in spans[1:]
    ]

    cells = jnp.pad(multipoles, ((0, KPAD - coef_count), (0, 0)))
    base = cell_count + 8 * slots
    table = own_table(cells, base + TOP * domains)
    outgoing = pack(table, cell_count, lists, counts)

    top = pair_source - base
    domain = top >> log2(TOP)
    along = (domain & (n_gy - 1)) ^ lax.axis_index("gy")
    place = (along * n_gx + (domain >> log2(n_gy))) * TOP_ROWS + (top & (TOP_ROWS - 1))
    top = base + ((top >> log2(TOP_ROWS)) & 1) * (TOP_ROWS * domains) + place
    wanted = jnp.where(pair_source < base, pair_source, top)
    sources = order(((wanted << SHIFT) | (pair_target & (BLOCK - 1))).reshape(-1, LANES))

    arrived = exchange(*outgoing, sources)

    ops = split(m2l_ops.transpose(0, 2, 1))

    tiles = width // LANES
    add_rows = planes * tiles * own_rows
    mine = lax.axis_index("gx").astype(jnp.int32).reshape(1)
    codes, amounts, bounds, top_own = sift(
        parts[0], mine, spans[0][1], planes, own_rows, cell_count // LANES
    )
    tops = [top_own]
    for bit in range(log2(n_gy)):
        held = jnp.concatenate(tops, axis=0) if bit else top_own
        tops.append(lax.ppermute(held, "gy", [(i, i ^ (1 << bit)) for i in range(n_gy)]))

    parts.append(send(after(carved[0], parts[0], ops, *arrived)))
    adds = deposit(codes, amounts, bounds, add_rows + 8, n_gx)
    table = whole_table(table, arrived, tops)
    cell_steps = cell_count // LANES
    slot_steps = 8 * slots // LANES
    slot_fields = m2l(sources, block_class, table, ops, cell_steps, slot_steps, True, slots)
    returned = exchange(slot_fields[:3], slot_fields[3:6], slot_fields[6:], adds[0])
    own_fields = m2l(sources, block_class, table, ops, 0, cell_steps, False, slots)
    parts.append(send(after(carved[1], parts[1], slot_fields, adds[0])))

    tables = fourier_tables(n_gx * width)
    spectrum = None
    for part, (at, size) in zip(parts, spans):
        spectrum = fourier(part, size, adds, tables, at, planes, spectrum, own_rows)

    field_tensors = add_back(lists, counts, own_fields, returned, coef_count)
    return (field_tensors, spectrum)


def solution(mesh):
    placed = (
        P(None, ("gx", "gy")),
        P(("gx", "gy"), None, None),
        P(("gx", "gy"), None),
        P(("gx", "gy")),
        P(("gx", "gy")),
        P(("gx", "gy")),
        P(),
        P(("gx", "gy")),
        P("gy", None, "gx"),
    )
    return jax.shard_map(
        functools.partial(on_device, n_gx=mesh.shape["gx"], n_gy=mesh.shape["gy"]),
        mesh=mesh,
        in_specs=placed,
        out_specs=(P(None, ("gx", "gy")), P(None, "gy", "gx", None)),
        check_vma=False,
    )
```

```python
import functools

import jax
import jax.numpy as jnp
import ml_dtypes
import numpy as np
from jax import lax
from jax.experimental import pallas as pl
from jax.experimental.pallas import tpu as pltpu
from jax.sharding import PartitionSpec as P

TOP = 32
BLOCK = 64
LANES = 128
KPAD = 40
COPIES = 3
PER_WINDOW = 8
SHIFT = 6
LANE_SHIFT = 7
VMEM_BYTES = 48 * 1024 * 1024
CHUNKS = (1, 4, 3)
TOP_ROWS = TOP // 2

DEPOSIT_SCALE = 8.0
SENT = ((0, 0), (2, 0), (1, 0), (0, 1), (1, 1), (0, 2), (2, 1), (1, 2))
GOT = ((3, 2), (3, 1), (3, 0), (1, 1), (0, 1), (2, 2), (2, 1), (2, 0))
IN_ROW = 0x57241360

SMEM_WHOLE = pl.BlockSpec(memory_space=pltpu.SMEM)
VMEM_WHOLE = pl.BlockSpec(memory_space=pltpu.VMEM)


def params():
    return pltpu.CompilerParams(vmem_limit_bytes=VMEM_BYTES)


def cost(flops, nbytes):
    return pl.CostEstimate(flops=flops, bytes_accessed=nbytes, transcendentals=0)


def spread(block):
    rest = jnp.zeros((LANES - COPIES * KPAD, LANES), jnp.float32)
    return jnp.concatenate([block] * COPIES + [rest], axis=0).T


def lane_ids(shape):
    return lax.broadcasted_iota(jnp.int32, shape, len(shape) - 1)


def own_table_kernel(cells_ref, out_ref):
    @pl.loop(0, cells_ref.shape[1] // LANES)
    def _(k):
        at = pl.multiple_of(k * LANES, LANES)
        out_ref[pl.ds(at, LANES), :] = spread(cells_ref[:, pl.ds(at, LANES)])


def own_table(cells, rows):
    count = cells.shape[1]
    return pl.pallas_call(
        own_table_kernel,
        grid=(1,),
        out_shape=jax.ShapeDtypeStruct((rows, LANES), jnp.float32),
        in_specs=[pl.BlockSpec((KPAD, count), lambda i: (0, 0))],
        out_specs=pl.BlockSpec((count, LANES), lambda i: (0, 0)),
        compiler_params=params(),
        cost_estimate=cost(10**6, 12 * 10**6),
        name="own_table",
    )(cells)


def cut_rows(refs, first, stop):
    pieces, at = [], 0
    for ref in refs:
        low, high = max(first - at, 0), min(stop - at, ref.shape[0])
        if low < high:
            pieces.append(ref[low:high, :])
        at += ref.shape[0]
    return jnp.concatenate(pieces, axis=0) if len(pieces) > 1 else pieces[0]


def whole_table_kernel(*refs, slot_steps):
    top_refs, out_ref = refs[4:-2], refs[-1]
    step = pl.program_id(0)
    for k in range(slot_steps):

        @pl.when(step == k)
        def _():
            at = 0
            for n in (2 * k, 2 * k + 1):
                part, place = GOT[n]
                for c in range(refs[part].shape[2] // LANES):
                    block = refs[part][place, :, c * LANES : (c + 1) * LANES]
                    out_ref[at : at + LANES, :] = spread(block)
                    at += LANES

    rows = out_ref.shape[0]
    total = sum(ref.shape[0] for ref in top_refs)
    lanes = lane_ids((rows, LANES))
    for k in range(2 * total // rows):

        @pl.when(step == slot_steps + k)
        def _():
            pieces = []
            for first in range(k * rows, (k + 1) * rows, min(rows, total)):
                group, at = first // total, first % total
                value = cut_rows(top_refs, at, at + min(rows, total))
                pieces.append(pltpu.roll(value, LANES - KPAD, 1) if group else value)
            value = jnp.concatenate(pieces, axis=0) if len(pieces) > 1 else pieces[0]
            value = jnp.where(lanes < KPAD, value, 0.0)
            out_ref[...] = value + pltpu.roll(value, KPAD, 1) + pltpu.roll(value, 2 * KPAD, 1)


def whole_table(table, arrived, tops):
    slots = arrived[0].shape[2]
    rows = 2 * slots
    top_rows = 2 * sum(part.shape[0] for part in tops)
    first = (table.shape[0] - 8 * slots - top_rows) // rows
    return pl.pallas_call(
        functools.partial(whole_table_kernel, slot_steps=4),
        grid=(4 + top_rows // rows,),
        out_shape=jax.ShapeDtypeStruct(table.shape, jnp.float32),
        in_specs=[VMEM_WHOLE] * (4 + len(tops)) + [pl.BlockSpec(memory_space=pl.ANY)],
        out_specs=pl.BlockSpec((rows, LANES), lambda i: (first + i, 0)),
        input_output_aliases={4 + len(tops): 0},
        compiler_params=params(),
        cost_estimate=cost(10**6, 16 * 10**6),
        name="whole_table",
    )(*arrived, *tops, table)


def as_rows(table):
    return table.reshape(table.shape[0], 1, LANES)


def pack_kernel(list_ref, count_ref, table_ref, *refs):
    outs, held = refs[:3], refs[3:]
    slot_tiles = list_ref.shape[1] // LANES
    for n in range(8):

        @pl.loop(0, slot_tiles, step=len(held))
        def _(i):
            firsts = [pl.multiple_of((i + k) * LANES, LANES) for k in range(len(held))]
            for first, rows in zip(firsts, held):
                for r in range(LANES):
                    rows[r : r + 1, :] = table_ref[list_ref[n, first + r]]
            for first, rows in zip(firsts, held):
                live = (lane_ids((KPAD, LANES)) + first) < count_ref[n]
                part, at = SENT[n]
                outs[part][at, :, pl.ds(first, LANES)] = jnp.where(live, rows[...].T[:KPAD], 0.0)


def pack(table, cell_count, proxy_list, proxy_count):
    slots = proxy_list.shape[1]
    return pl.pallas_call(
        pack_kernel,
        grid=(1,),
        out_shape=tuple(jax.ShapeDtypeStruct((size, KPAD, slots), jnp.float32) for size in (3, 3, 2)),
        in_specs=[
            SMEM_WHOLE,
            SMEM_WHOLE,
            pl.BlockSpec((cell_count, 1, LANES), lambda i: (0, 0, 0)),
        ],
        out_specs=tuple(
            pl.BlockSpec((size, KPAD, slots), lambda i: (0, 0, 0)) for size in (3, 3, 2)
        ),
        scratch_shapes=[pltpu.VMEM((LANES, LANES), jnp.float32)] * 2,
        compiler_params=params(),
        cost_estimate=cost(10**6, 25 * 10**6),
        name="pack",
    )(proxy_list, proxy_count, as_rows(table))


def shift(value, axis, by):
    count = lax.axis_size(axis)
    return lax.ppermute(value, axis, [(i, (i + by) % count) for i in range(count)])


def along_gy(down, up):
    return shift(down, "gy", -1), shift(up, "gy", 1)


def along_gx(down, up, mid):
    left = shift(jnp.stack([down[0], mid[0], up[0]]), "gx", -1)
    right = shift(jnp.stack([down[2], mid[1], up[2]]), "gx", 1)
    return down, up, left, right


def order_kernel(packed_ref, out_ref):
    lanes = lane_ids((LANES, LANES))
    within = lanes & (BLOCK - 1)
    base = lanes - within

    @pl.loop(0, packed_ref.shape[0] // LANES)
    def _(k):
        at = pl.ds(pl.multiple_of(k * LANES, LANES), LANES)
        packed = packed_ref[at, :]

        def step(i, ordered):
            value = jnp.take_along_axis(packed, base + i, axis=1, mode="promise_in_bounds")
            return jnp.where((value & (BLOCK - 1)) == within, value, ordered)

        ordered = lax.fori_loop(0, BLOCK, step, jnp.zeros_like(packed), unroll=8)
        out_ref[at, :] = ordered >> SHIFT


def order(packed):
    return pl.pallas_call(
        order_kernel,
        out_shape=jax.ShapeDtypeStruct(packed.shape, jnp.int32),
        in_specs=[VMEM_WHOLE],
        out_specs=VMEM_WHOLE,
        compiler_params=params(),
        cost_estimate=cost(10**6, 20 * 10**6),
        name="order",
    )(packed)


def split_kernel(ops_ref, out_ref, *, group):
    coefs = ops_ref.shape[1]

    @pl.loop(0, ops_ref.shape[0], step=group)
    def _(c):
        at = pl.ds(c, group)
        value = ops_ref[at]
        high = value.astype(jnp.bfloat16).astype(jnp.float32)
        out_ref[at] = jnp.zeros((group, KPAD, LANES), jnp.float32)
        out_ref[at, :coefs, :coefs] = high
        out_ref[at, :coefs, KPAD : KPAD + coefs] = value - high


def split(turned_ops):
    classes = turned_ops.shape[0]
    group = max(size for size in range(1, 10) if classes % size == 0)
    return pl.pallas_call(
        functools.partial(split_kernel, group=group),
        out_shape=jax.ShapeDtypeStruct((classes, KPAD, LANES), jnp.float32),
        in_specs=[VMEM_WHOLE],
        out_specs=VMEM_WHOLE,
        compiler_params=params(),
        cost_estimate=cost(10**6, 12 * 10**6),
        name="split",
    )(turned_ops)


def m2l_kernel(source_ref, class_ref, table_ref, ops_ref, out_ref, *gathered, first, turned):
    step = first + pl.program_id(0)
    lanes = lane_ids((1, LANES))
    in_first = lanes < KPAD
    in_second = lanes < 2 * KPAD

    def row(b, t):
        return table_ref[source_ref[b // 2, (b % 2) * BLOCK + t]]

    for u in range(2):
        for t in range(BLOCK):
            for g in range(3):
                b = u * PER_WINDOW + 3 * g
                one, two = row(b, t), row(b + 1, t)
                three = row(b + 2, t) if g < 2 else two
                gathered[u][g, t : t + 1, :] = jnp.where(
                    in_first, one, jnp.where(in_second, two, three)
                )

    rest = jnp.zeros((LANES - COPIES * KPAD, LANES), jnp.float32)
    none = jnp.zeros((KPAD, LANES), jnp.float32)
    results = []
    for u in range(2):
        total = jnp.zeros((BLOCK, LANES), jnp.float32)
        for g in range(3):
            held = []
            for s in range(3):
                b = 3 * g + s
                if b < PER_WINDOW:
                    held.append(ops_ref[class_ref[step * 2 * PER_WINDOW + u * PER_WINDOW + b]])
                else:
                    held.append(none)
            weights = jnp.concatenate(held + [rest], axis=0).astype(jnp.bfloat16)
            values = gathered[u][g]
            high = values.astype(jnp.bfloat16)
            low = (values - high.astype(jnp.float32)).astype(jnp.bfloat16)
            total += jnp.dot(high, weights, preferred_element_type=jnp.float32)
            total += jnp.dot(low, weights, preferred_element_type=jnp.float32)
        results.append(total)
    both = jnp.concatenate(results, axis=0)
    both = both + pltpu.roll(both, LANES - KPAD, 1)
    if turned:
        out_ref[0] = both.T[:KPAD]
    else:
        out_ref[...] = both


def m2l(sources, classes, table, ops, first, steps, turned, slots):
    if turned:
        per = slots // LANES
        shape = (steps // per, KPAD, slots)
        out_spec = pl.BlockSpec(
            (1, KPAD, LANES), lambda i: ((IN_ROW >> (4 * (i // per))) & 7, 0, i % per)
        )
    else:
        shape = (steps * LANES, LANES)
        out_spec = pl.BlockSpec((LANES, LANES), lambda i: (i, 0))
    return pl.pallas_call(
        functools.partial(m2l_kernel, first=first, turned=turned),
        grid=(steps,),
        out_shape=jax.ShapeDtypeStruct(shape, jnp.float32),
        in_specs=[
            pl.BlockSpec((8, LANES), lambda i: (first + i, 0), memory_space=pltpu.SMEM),
            SMEM_WHOLE,
            VMEM_WHOLE,
            VMEM_WHOLE,
        ],
        out_specs=out_spec,
        scratch_shapes=[pltpu.VMEM((3, BLOCK, LANES), jnp.float32)] * 2,
        compiler_params=params(),
        cost_estimate=cost(10**6, 150 * 10**6),
        name="m2l_slots" if turned else "m2l_cells",
    )(sources, classes, as_rows(table), ops)


def add_back_kernel(list_ref, count_ref, own_ref, *refs):
    slot_refs, out_ref = refs[:4], refs[4]
    rows, sums = refs[5], refs[6:]
    slots = list_ref.shape[1]
    sums[0][...] = own_ref[...]
    for held in sums[1:]:
        held[...] = jnp.zeros_like(held)
    for n in range(8):
        for k in range(slots // LANES):
            live = (lane_ids((KPAD, LANES)) + k * LANES) < count_ref[n]
            part, place = GOT[n]
            values = jnp.where(live, slot_refs[part][place, :, k * LANES : (k + 1) * LANES], 0.0)
            at = n * slots + k * LANES
            rows[at : at + LANES, :] = spread(values)

    @pl.loop(0, slots, step=4)
    def _(first):
        for j in range(4):
            to = [pl.ds(list_ref[n, first + j], 1) for n in range(8)]
            old = [sums[n][to[n], :] for n in range(8)]
            new = [old[n] + rows[pl.ds(n * slots + first + j, 1), :] for n in range(8)]
            for n in range(8):
                sums[n][to[n], :] = new[n]

    @pl.loop(0, own_ref.shape[0] // LANES)
    def _(k):
        at = pl.ds(pl.multiple_of(k * LANES, LANES), LANES)
        parts = [held[at, :] for held in sums]
        while len(parts) > 1:
            parts = [a + b for a, b in zip(parts[::2], parts[1::2])]
        out_ref[:, at] = parts[0].T[: out_ref.shape[0]]


def add_back(proxy_list, proxy_count, own_rows, slot_fields, coef_count):
    cell_count = own_rows.shape[0]
    slots = proxy_list.shape[1]
    return pl.pallas_call(
        add_back_kernel,
        out_shape=jax.ShapeDtypeStruct((coef_count, cell_count), jnp.float32),
        in_specs=[SMEM_WHOLE, SMEM_WHOLE] + [VMEM_WHOLE] * 5,
        out_specs=VMEM_WHOLE,
        scratch_shapes=[pltpu.VMEM((8 * slots, LANES), jnp.float32)]
        + [pltpu.VMEM((cell_count, LANES), jnp.float32)] * 8,
        compiler_params=params(),
        cost_estimate=cost(10**6, 30 * 10**6),
        name="add_back",
    )(proxy_list, proxy_count, own_rows, *slot_fields)


def carve_kernel(mesh_ref, out_ref, sems, *, first):
    sources, count, rows, width = out_ref.shape
    copies = [
        pltpu.make_async_copy(
            mesh_ref.at[pl.ds(first, count), pl.ds(s * rows, rows), :], out_ref.at[s], sems.at[s]
        )
        for s in range(sources)
    ]
    for copy in copies:
        copy.start()
    for copy in copies:
        copy.wait()


def carve(mesh, first, count, sources):
    rows, width = mesh.shape[1] // sources, mesh.shape[2]
    return pl.pallas_call(
        functools.partial(carve_kernel, first=first),
        out_shape=jax.ShapeDtypeStruct((sources, count, rows, width), jnp.float32),
        in_specs=[pl.BlockSpec(memory_space=pl.ANY)],
        out_specs=VMEM_WHOLE,
        scratch_shapes=[pltpu.SemaphoreType.DMA((sources,))],
        compiler_params=params(),
        cost_estimate=cost(0, 8 * count * sources * rows * width),
        name="carve",
    )(mesh)


def first_part_kernel(mesh_ref, place_ref, cells_ref, out_ref, sems, *, count, rows):
    sources, _, width = out_ref.shape
    copies = [
        pltpu.make_async_copy(
            mesh_ref.at[p, pl.ds(s * rows, rows), :],
            out_ref.at[s, pl.ds(p * rows, rows), :],
            sems.at[p, s],
        )
        for p in range(count)
        for s in range(sources)
    ]
    for copy in copies:
        copy.start()
    is_first = lane_ids((TOP_ROWS, LANES)) < KPAD
    rest = jnp.zeros((KPAD - cells_ref.shape[0], LANES), jnp.float32)
    table = spread(jnp.concatenate([cells_ref[:, :LANES], rest], axis=0))
    top = jnp.where(is_first, table[:TOP_ROWS, :], table[TOP_ROWS : 2 * TOP_ROWS, :])
    blocks = [place_ref[...].astype(jnp.float32), cell_lines(cells_ref), top]
    at = count * rows
    for block in blocks:
        high = block.shape[0] * LANES // width
        for h in range(width // LANES):
            for s in range(sources):
                out_ref[s, at : at + high, h * LANES : (h + 1) * LANES] = block[
                    h * high : (h + 1) * high, :
                ]
        at += high
    for copy in copies:
        copy.wait()


def cell_lines(cells_ref):
    lines = [cells_ref[0:1, k : k + LANES] for k in range(0, cells_ref.shape[1], LANES)]
    return DEPOSIT_SCALE * jnp.concatenate(lines, axis=0)


def first_part(mesh, place, multipoles, sources, count):
    rows, width = mesh.shape[1] // sources, mesh.shape[2]
    extra = (2 * place.size + TOP_ROWS * LANES) // width
    return pl.pallas_call(
        functools.partial(first_part_kernel, count=count, rows=rows),
        out_shape=jax.ShapeDtypeStruct((sources, count * rows + extra, width), jnp.float32),
        in_specs=[pl.BlockSpec(memory_space=pl.ANY), VMEM_WHOLE, VMEM_WHOLE],
        out_specs=VMEM_WHOLE,
        scratch_shapes=[
            pltpu.SemaphoreType.DMA((count, sources)),
        ],
        compiler_params=params(),
        cost_estimate=cost(0, 8 * sources * rows * width),
        name="first_part",
    )(mesh, place.reshape(-1, LANES), multipoles)


def log2(value):
    return value.bit_length() - 1


def sift_kernel(mine_ref, part_ref, code_ref, value_ref, bound_ref, top_ref, ride, sem, *, count, planes, rows):
    sources, extra, width = ride.shape
    lines = code_ref.shape[0] // sources
    copy = pltpu.make_async_copy(part_ref.at[:, pl.ds(count * rows, extra), :], ride, sem)
    copy.start()
    copy.wait()

    def unfold(first, count):
        high = count * LANES // width
        return jnp.concatenate(
            [
                ride[s, first : first + high, h * LANES : (h + 1) * LANES]
                for s in range(sources)
                for h in range(width // LANES)
            ],
            axis=0,
        )

    step = lines * LANES // width
    place = unfold(0, lines).astype(jnp.int32)
    value = unfold(step, lines)
    top_ref[...] = unfold(2 * step, TOP_ROWS)

    row_at, mesh_rows = log2(width), rows * sources
    plane = place >> (row_at + log2(mesh_rows))
    row = (place >> row_at) & (mesh_rows - 1)
    column = place & (width - 1)
    tiles = width // LANES
    target = (plane * tiles + (column >> LANE_SHIFT)) * rows + (row & (rows - 1))
    none = planes * tiles * rows * LANES
    mine = (row >> log2(rows)) == mine_ref[0]
    lanes = lane_ids(place.shape)
    code = jnp.where(mine, target * LANES + (column & (LANES - 1)), none)
    value = jnp.where(mine, value, 0.0)
    ahead = jnp.where(mine, 1, 0)
    for b in range(LANE_SHIFT):
        ahead = ahead + jnp.where(lanes >= (1 << b), pltpu.roll(ahead, 1 << b, 1), 0)
    shift = jnp.where(mine, lanes + 1 - ahead, 0)
    for b in range(LANE_SHIFT):
        back = LANES - (1 << b)
        moves = (shift >> b) & 1
        comes = pltpu.roll(moves, back, 1) == 1
        goes = moves == 1
        code = jnp.where(comes, pltpu.roll(code, back, 1), jnp.where(goes, none, code))
        value = jnp.where(comes, pltpu.roll(value, back, 1), jnp.where(goes, 0.0, value))
        shift = jnp.where(comes, pltpu.roll(shift, back, 1), jnp.where(goes, 0, shift))
    code_ref[...] = code
    value_ref[...] = value
    counts = jnp.sum(jnp.where(mine, 1.0, 0.0), axis=1, keepdims=True)
    counts = jnp.broadcast_to(counts, mine.shape).reshape(2 * sources, lines // 2, LANES)
    bound_ref[...] = jnp.max(counts, axis=0).astype(jnp.int32)


def sift(part, mine, count, planes, rows, lines):
    sources, whole_rows, width = part.shape
    extra = whole_rows - count * rows
    shape = (sources * lines, LANES)
    return pl.pallas_call(
        functools.partial(sift_kernel, count=count, planes=planes, rows=rows),
        out_shape=(
            jax.ShapeDtypeStruct(shape, jnp.int32),
            jax.ShapeDtypeStruct(shape, jnp.float32),
            jax.ShapeDtypeStruct((lines // 2, LANES), jnp.int32),
            jax.ShapeDtypeStruct((sources * TOP_ROWS, LANES), jnp.float32),
        ),
        in_specs=[SMEM_WHOLE, pl.BlockSpec(memory_space=pl.ANY)],
        out_specs=(VMEM_WHOLE,) * 4,
        scratch_shapes=[pltpu.VMEM((sources, extra, width), jnp.float32), pltpu.SemaphoreType.DMA],
        compiler_params=params(),
        cost_estimate=cost(10**6, 8 * 10**6),
        name="sift",
    )(mine, part)


def deposit_kernel(code_ref, value_ref, bound_ref, *refs):
    sources = len(refs) // 2
    outs, others = refs[:sources], refs[sources:]
    lines = code_ref.shape[0] // (2 * sources)
    lanes = lane_ids((1, LANES))
    for held in refs:
        held[...] = jnp.zeros_like(held)

    def line(g, _):
        def one(j):
            at = [((2 * s + h) * lines + g, j) for h in range(2) for s in range(sources)]
            codes = [code_ref[i] for i in at]
            to = [pl.ds(code >> LANE_SHIFT, 1) for code in codes]
            old = [held[rows, :] for held, rows in zip(refs, to)]
            new = [
                row + jnp.where(lanes == (code & (LANES - 1)), value_ref[i], 0.0)
                for row, code, i in zip(old, codes, at)
            ]
            for held, rows, row in zip(refs, to, new):
                held[rows, :] = row

        def four(i, _):
            for j in range(4):
                one(4 * i + j)
            return 0

        return lax.fori_loop(0, (bound_ref[g, 0] + 3) >> 2, four, 0)

    lax.fori_loop(0, lines, line, 0)
    for out_ref, held in zip(outs, others):
        out_ref[...] = out_ref[...] + held[...]


def deposit(codes, values, bounds, rows, sources):
    return pl.pallas_call(
        deposit_kernel,
        out_shape=(jax.ShapeDtypeStruct((rows, LANES), jnp.float32),) * sources,
        in_specs=[SMEM_WHOLE] * 3,
        out_specs=(VMEM_WHOLE,) * sources,
        scratch_shapes=[pltpu.VMEM((rows, LANES), jnp.float32)] * sources,
        compiler_params=params(),
        cost_estimate=cost(10**6, 40 * 10**6),
        name="deposit",
    )(codes, values, bounds)


def fourier_tables(length):
    points, half = length // 2, length // 4
    positions = np.arange(points)
    scale = 1.0 / np.sqrt(length)
    parts = []
    for odd in range(2):
        ks = 2 * np.arange(half) + odd
        angles = (positions[:, None] * ks[None, :] % length) * (2.0 * np.pi / length)
        imag = -np.sin(angles) * scale
        if not odd:
            imag[:, 0] = np.where(positions % 2 == 0, scale, -scale)
        parts.append(np.concatenate([np.cos(angles) * scale, imag], axis=1))
    whole = np.stack(parts)
    high = whole.astype(ml_dtypes.bfloat16)
    low = (whole - high.astype(np.float64)).astype(ml_dtypes.bfloat16)
    return high, low


def fourier_kernel(*refs, sources):
    mesh_ref, add_refs = refs[0], refs[1 : 1 + sources]
    high_ref, low_ref = refs[1 + sources], refs[2 + sources]
    out_ref = refs[-1]
    rows, width = mesh_ref.shape[1:]
    pieces = []
    for s in range(sources):
        for h in range(width // LANES):
            pieces.append(
                mesh_ref[s, :, h * LANES : (h + 1) * LANES]
                + add_refs[s][h * rows : (h + 1) * rows, :]
            )
    mid = len(pieces) // 2
    halves = []
    for odd in range(2):
        if odd:
            folded = [a - b for a, b in zip(pieces[:mid], pieces[mid:])]
        else:
            folded = [a + b for a, b in zip(pieces[:mid], pieces[mid:])]
        values = jnp.concatenate(folded, axis=1)
        high = values.astype(jnp.bfloat16)
        low = (values - high.astype(jnp.float32)).astype(jnp.bfloat16)
        both = jnp.dot(
            jnp.concatenate([high, low], axis=0), high_ref[odd], preferred_element_type=jnp.float32
        )
        halves.append(
            both[:rows]
            + both[rows:]
            + jnp.dot(high, low_ref[odd], preferred_element_type=jnp.float32)
        )
    lanes = lane_ids((rows, LANES))
    is_first = lanes == 0
    is_odd = (lanes & 1) == 1
    steps = lanes >> 1
    tiles = len(pieces)
    per = tiles // 4

    def tile(odd, part, j):
        at = (part * per + j) * LANES
        return halves[odd][:, at : at + LANES]

    def pick(value, lane):
        return jnp.take_along_axis(value, lane, axis=1, mode="promise_in_bounds")

    for j in range(tiles):
        for part in range(2):
            if j < tiles // 2:
                at = BLOCK * j
                lane = (at % LANES) + steps
                even = pick(tile(0, part, at // LANES), lane)
                odd = pick(tile(1, part, at // LANES), lane)
                if j == 0 and part == 1:
                    even = jnp.where(is_first, 0.0, even)
            else:
                at = BLOCK * (tiles - j)
                last = (at - 1) // LANES
                even = pick(tile(0, part, last), (at - steps) & (LANES - 1))
                odd = pick(tile(1, part, last), ((at - 1) % LANES) - steps)
                if at % LANES == 0 and j > tiles // 2:
                    even = jnp.where(is_first, tile(0, part, at // LANES), even)
                if part == 1:
                    even, odd = -even, -odd
                if j == tiles // 2:
                    even = jnp.where(is_first, 0.0 if part else tile(0, 1, 0), even)
            out_ref[part, 0, :, j * LANES : (j + 1) * LANES] = jnp.where(is_odd, odd, even)


def fourier(mesh_part, count, adds, tables, first, planes, so_far, rows):
    sources, _, width = mesh_part.shape
    length = sources * width
    add_rows = (width // LANES) * rows
    operands = [mesh_part, *adds, *tables]
    in_specs = (
        [pl.BlockSpec((sources, rows, width), lambda p: (0, p, 0))]
        + [pl.BlockSpec((add_rows, LANES), lambda p: (first + p, 0))] * sources
        + [
            pl.BlockSpec((2, length // 2, length // 2), lambda p: (0, 0, 0), pipeline_mode=pl.Buffered(1))
        ]
        * 2
    )
    aliases = {}
    if so_far is not None:
        aliases = {len(operands): 0}
        operands.append(so_far)
        in_specs.append(pl.BlockSpec(memory_space=pl.ANY))
    return pl.pallas_call(
        functools.partial(fourier_kernel, sources=sources),
        grid=(count,),
        out_shape=jax.ShapeDtypeStruct((2, planes, rows, length), jnp.float32),
        in_specs=in_specs,
        out_specs=pl.BlockSpec((2, 1, rows, length), lambda p: (0, first + p, 0, 0)),
        input_output_aliases=aliases,
        compiler_params=params(),
        cost_estimate=cost(10**6, count * 10 * 10**6),
        name="fourier",
    )(*operands)


def after(value, *others):
    return lax.optimization_barrier((value, *others))[0]


def on_device(
    multipoles,
    proxy_list,
    proxy_count,
    pair_source,
    pair_target,
    block_class,
    m2l_ops,
    cell_mesh,
    pm_density,
    *,
    n_gx,
    n_gy,
):
    coef_count, cell_count = multipoles.shape
    slots = proxy_list.shape[2]
    planes, mesh_rows, width = pm_density.shape
    own_rows = mesh_rows // n_gx
    domains = n_gx * n_gy
    lists, counts = proxy_list[0], proxy_count[0]

    def send(part):
        return lax.all_to_all(part, "gx", 0, 0, tiled=True)

    spans = []
    first = 0
    for size in CHUNKS:
        spans.append((first, size))
        first += size

    parts = [send(first_part(pm_density, cell_mesh, multipoles, n_gx, spans[0][1]))]
    carved = [
        carve(pm_density, at, size, n_gx).reshape(n_gx, size * own_rows, width)
        for at, size in spans[1:]
    ]

    cells = jnp.pad(multipoles, ((0, KPAD - coef_count), (0, 0)))
    base = cell_count + 8 * slots
    table = own_table(cells, base + TOP * domains)
    outgoing = pack(table, cell_count, lists, counts)

    top = pair_source - base
    domain = top >> log2(TOP)
    along = (domain & (n_gy - 1)) ^ lax.axis_index("gy")
    place = (along * n_gx + (domain >> log2(n_gy))) * TOP_ROWS + (top & (TOP_ROWS - 1))
    top = base + ((top >> log2(TOP_ROWS)) & 1) * (TOP_ROWS * domains) + place
    wanted = jnp.where(pair_source < base, pair_source, top)
    sources = order(((wanted << SHIFT) | (pair_target & (BLOCK - 1))).reshape(-1, LANES))

    arrived = along_gx(*along_gy(*outgoing[:2]), after(outgoing[2], sources))

    ops = split(m2l_ops.transpose(0, 2, 1))

    tiles = width // LANES
    add_rows = planes * tiles * own_rows
    mine = lax.axis_index("gx").astype(jnp.int32).reshape(1)
    codes, amounts, bounds, top_own = sift(
        parts[0], mine, spans[0][1], planes, own_rows, cell_count // LANES
    )
    tops = [top_own]
    for bit in range(log2(n_gy)):
        held = jnp.concatenate(tops, axis=0) if bit else top_own
        tops.append(lax.ppermute(held, "gy", [(i, i ^ (1 << bit)) for i in range(n_gy)]))

    parts.append(send(after(carved[0], parts[0], ops, *arrived)))
    adds = deposit(codes, amounts, bounds, add_rows + 8, n_gx)
    table = whole_table(table, arrived, tops)
    cell_steps = cell_count // LANES
    slot_steps = 8 * slots // LANES
    slot_fields = m2l(sources, block_class, table, ops, cell_steps, slot_steps, True, slots)
    tables = fourier_tables(n_gx * width)
    spectrum = fourier(parts[0], spans[0][1], adds, tables, 0, planes, None, own_rows)
    crossed = along_gy(slot_fields[:3], slot_fields[3:6])
    parts.append(send(after(carved[1], parts[1], spectrum, *crossed)))
    returned = along_gx(*crossed, slot_fields[6:])
    own_fields = m2l(sources, block_class, table, ops, 0, cell_steps, False, slots)
    spectrum = fourier(parts[1], spans[1][1], adds, tables, spans[1][0], planes, spectrum, own_rows)
    own_fields = after(own_fields, spectrum)
    field_tensors = add_back(lists, counts, own_fields, returned, coef_count)
    spectrum = fourier(parts[2], spans[2][1], adds, tables, spans[2][0], planes, spectrum, own_rows)
    return (field_tensors, spectrum)


def solution(mesh):
    placed = (
        P(None, ("gx", "gy")),
        P(("gx", "gy"), None, None),
        P(("gx", "gy"), None),
        P(("gx", "gy")),
        P(("gx", "gy")),
        P(("gx", "gy")),
        P(),
        P(("gx", "gy")),
        P("gy", None, "gx"),
    )
    return jax.shard_map(
        functools.partial(on_device, n_gx=mesh.shape["gx"], n_gy=mesh.shape["gy"]),
        mesh=mesh,
        in_specs=placed,
        out_specs=(P(None, ("gx", "gy")), P(None, "gy", "gx", None)),
        check_vma=False,
    )
```

```python
import functools

import jax
import jax.numpy as jnp
import ml_dtypes
import numpy as np
from jax import lax
from jax.experimental import pallas as pl
from jax.experimental.pallas import tpu as pltpu
from jax.sharding import PartitionSpec as P

TOP = 32
BLOCK = 64
LANES = 128
KPAD = 40
COPIES = 3
PER_WINDOW = 8
SHIFT = 6
LANE_SHIFT = 7
VMEM_BYTES = 48 * 1024 * 1024
CHUNKS = (1, 4, 3)
TOP_ROWS = TOP // 2

DEPOSIT_SCALE = 8.0
SENT = ((0, 0), (2, 0), (1, 0), (0, 1), (1, 1), (0, 2), (2, 1), (1, 2))
GOT = ((3, 2), (3, 1), (3, 0), (1, 1), (0, 1), (2, 2), (2, 1), (2, 0))
IN_ROW = 0x57241360

SMEM_WHOLE = pl.BlockSpec(memory_space=pltpu.SMEM)
VMEM_WHOLE = pl.BlockSpec(memory_space=pltpu.VMEM)


def params():
    return pltpu.CompilerParams(vmem_limit_bytes=VMEM_BYTES)


def cost(flops, nbytes):
    return pl.CostEstimate(flops=flops, bytes_accessed=nbytes, transcendentals=0)


def spread(block):
    rest = jnp.zeros((LANES - COPIES * KPAD, LANES), jnp.float32)
    return jnp.concatenate([block] * COPIES + [rest], axis=0).T


def lane_ids(shape):
    return lax.broadcasted_iota(jnp.int32, shape, len(shape) - 1)


def own_table_kernel(cells_ref, out_ref):
    @pl.loop(0, cells_ref.shape[1] // LANES)
    def _(k):
        at = pl.multiple_of(k * LANES, LANES)
        out_ref[pl.ds(at, LANES), :] = spread(cells_ref[:, pl.ds(at, LANES)])


def own_table(cells, rows):
    count = cells.shape[1]
    return pl.pallas_call(
        own_table_kernel,
        grid=(1,),
        out_shape=jax.ShapeDtypeStruct((rows, LANES), jnp.float32),
        in_specs=[pl.BlockSpec((KPAD, count), lambda i: (0, 0))],
        out_specs=pl.BlockSpec((count, LANES), lambda i: (0, 0)),
        compiler_params=params(),
        cost_estimate=cost(10**6, 12 * 10**6),
        name="own_table",
    )(cells)


def cut_rows(refs, first, stop):
    pieces, at = [], 0
    for ref in refs:
        low, high = max(first - at, 0), min(stop - at, ref.shape[0])
        if low < high:
            pieces.append(ref[low:high, :])
        at += ref.shape[0]
    return jnp.concatenate(pieces, axis=0) if len(pieces) > 1 else pieces[0]


def whole_table_kernel(*refs, slot_steps):
    top_refs, out_ref = refs[4:-2], refs[-1]
    step = pl.program_id(0)
    for k in range(slot_steps):

        @pl.when(step == k)
        def _():
            at = 0
            for n in (2 * k, 2 * k + 1):
                part, place = GOT[n]
                for c in range(refs[part].shape[2] // LANES):
                    block = refs[part][place, :, c * LANES : (c + 1) * LANES]
                    out_ref[at : at + LANES, :] = spread(block)
                    at += LANES

    rows = out_ref.shape[0]
    total = sum(ref.shape[0] for ref in top_refs)
    lanes = lane_ids((rows, LANES))
    for k in range(2 * total // rows):

        @pl.when(step == slot_steps + k)
        def _():
            pieces = []
            for first in range(k * rows, (k + 1) * rows, min(rows, total)):
                group, at = first // total, first % total
                value = cut_rows(top_refs, at, at + min(rows, total))
                pieces.append(pltpu.roll(value, LANES - KPAD, 1) if group else value)
            value = jnp.concatenate(pieces, axis=0) if len(pieces) > 1 else pieces[0]
            value = jnp.where(lanes < KPAD, value, 0.0)
            out_ref[...] = value + pltpu.roll(value, KPAD, 1) + pltpu.roll(value, 2 * KPAD, 1)


def whole_table(table, arrived, tops):
    slots = arrived[0].shape[2]
    rows = 2 * slots
    top_rows = 2 * sum(part.shape[0] for part in tops)
    first = (table.shape[0] - 8 * slots - top_rows) // rows
    return pl.pallas_call(
        functools.partial(whole_table_kernel, slot_steps=4),
        grid=(4 + top_rows // rows,),
        out_shape=jax.ShapeDtypeStruct(table.shape, jnp.float32),
        in_specs=[VMEM_WHOLE] * (4 + len(tops)) + [pl.BlockSpec(memory_space=pl.ANY)],
        out_specs=pl.BlockSpec((rows, LANES), lambda i: (first + i, 0)),
        input_output_aliases={4 + len(tops): 0},
        compiler_params=params(),
        cost_estimate=cost(10**6, 16 * 10**6),
        name="whole_table",
    )(*arrived, *tops, table)


def as_rows(table):
    return table.reshape(table.shape[0], 1, LANES)


def pack_kernel(list_ref, count_ref, table_ref, *refs):
    outs, held = refs[:3], refs[3:]
    slot_tiles = list_ref.shape[1] // LANES
    for n in range(8):

        @pl.loop(0, slot_tiles, step=len(held))
        def _(i):
            firsts = [pl.multiple_of((i + k) * LANES, LANES) for k in range(len(held))]
            for first, rows in zip(firsts, held):
                for r in range(LANES):
                    rows[r : r + 1, :] = table_ref[list_ref[n, first + r]]
            for first, rows in zip(firsts, held):
                live = (lane_ids((KPAD, LANES)) + first) < count_ref[n]
                part, at = SENT[n]
                outs[part][at, :, pl.ds(first, LANES)] = jnp.where(live, rows[...].T[:KPAD], 0.0)


def pack(table, cell_count, proxy_list, proxy_count):
    slots = proxy_list.shape[1]
    return pl.pallas_call(
        pack_kernel,
        grid=(1,),
        out_shape=tuple(jax.ShapeDtypeStruct((size, KPAD, slots), jnp.float32) for size in (3, 3, 2)),
        in_specs=[
            SMEM_WHOLE,
            SMEM_WHOLE,
            pl.BlockSpec((cell_count, 1, LANES), lambda i: (0, 0, 0)),
        ],
        out_specs=tuple(
            pl.BlockSpec((size, KPAD, slots), lambda i: (0, 0, 0)) for size in (3, 3, 2)
        ),
        scratch_shapes=[pltpu.VMEM((LANES, LANES), jnp.float32)] * 2,
        compiler_params=params(),
        cost_estimate=cost(10**6, 25 * 10**6),
        name="pack",
    )(proxy_list, proxy_count, as_rows(table))


def shift(value, axis, by):
    count = lax.axis_size(axis)
    return lax.ppermute(value, axis, [(i, (i + by) % count) for i in range(count)])


def along_gy(down, up):
    return shift(down, "gy", -1), shift(up, "gy", 1)


def along_gx(down, up, mid):
    left = shift(jnp.stack([down[0], mid[0], up[0]]), "gx", -1)
    right = shift(jnp.stack([down[2], mid[1], up[2]]), "gx", 1)
    return down, up, left, right


def order_kernel(packed_ref, out_ref):
    lanes = lane_ids((LANES, LANES))
    within = lanes & (BLOCK - 1)
    base = lanes - within

    @pl.loop(0, packed_ref.shape[0] // LANES)
    def _(k):
        at = pl.ds(pl.multiple_of(k * LANES, LANES), LANES)
        packed = packed_ref[at, :]

        def step(i, ordered):
            value = jnp.take_along_axis(packed, base + i, axis=1, mode="promise_in_bounds")
            return jnp.where((value & (BLOCK - 1)) == within, value, ordered)

        ordered = lax.fori_loop(0, BLOCK, step, jnp.zeros_like(packed), unroll=8)
        out_ref[at, :] = ordered >> SHIFT


def order(packed):
    return pl.pallas_call(
        order_kernel,
        out_shape=jax.ShapeDtypeStruct(packed.shape, jnp.int32),
        in_specs=[VMEM_WHOLE],
        out_specs=VMEM_WHOLE,
        compiler_params=params(),
        cost_estimate=cost(10**6, 20 * 10**6),
        name="order",
    )(packed)


def split_kernel(ops_ref, out_ref, *, group):
    coefs = ops_ref.shape[1]

    @pl.loop(0, ops_ref.shape[0], step=group)
    def _(c):
        at = pl.ds(c, group)
        value = ops_ref[at]
        high = value.astype(jnp.bfloat16).astype(jnp.float32)
        out_ref[at] = jnp.zeros((group, KPAD, LANES), jnp.float32)
        out_ref[at, :coefs, :coefs] = high
        out_ref[at, :coefs, KPAD : KPAD + coefs] = value - high


def split(turned_ops):
    classes = turned_ops.shape[0]
    group = max(size for size in range(1, 10) if classes % size == 0)
    return pl.pallas_call(
        functools.partial(split_kernel, group=group),
        out_shape=jax.ShapeDtypeStruct((classes, KPAD, LANES), jnp.float32),
        in_specs=[VMEM_WHOLE],
        out_specs=VMEM_WHOLE,
        compiler_params=params(),
        cost_estimate=cost(10**6, 12 * 10**6),
        name="split",
    )(turned_ops)


def m2l_kernel(source_ref, class_ref, table_ref, ops_ref, out_ref, *gathered, first, turned):
    step = first + pl.program_id(0)
    lanes = lane_ids((1, LANES))
    in_first = lanes < KPAD
    in_second = lanes < 2 * KPAD

    def row(b, t):
        return table_ref[source_ref[b // 2, (b % 2) * BLOCK + t]]

    for u in range(2):
        for t in range(BLOCK):
            for g in range(3):
                b = u * PER_WINDOW + 3 * g
                one, two = row(b, t), row(b + 1, t)
                three = row(b + 2, t) if g < 2 else two
                gathered[u][g, t : t + 1, :] = jnp.where(
                    in_first, one, jnp.where(in_second, two, three)
                )

    rest = jnp.zeros((LANES - COPIES * KPAD, LANES), jnp.float32)
    none = jnp.zeros((KPAD, LANES), jnp.float32)
    results = []
    for u in range(2):
        total = jnp.zeros((BLOCK, LANES), jnp.float32)
        for g in range(3):
            held = []
            for s in range(3):
                b = 3 * g + s
                if b < PER_WINDOW:
                    held.append(ops_ref[class_ref[step * 2 * PER_WINDOW + u * PER_WINDOW + b]])
                else:
                    held.append(none)
            weights = jnp.concatenate(held + [rest], axis=0).astype(jnp.bfloat16)
            values = gathered[u][g]
            high = values.astype(jnp.bfloat16)
            low = (values - high.astype(jnp.float32)).astype(jnp.bfloat16)
            total += jnp.dot(high, weights, preferred_element_type=jnp.float32)
            total += jnp.dot(low, weights, preferred_element_type=jnp.float32)
        results.append(total)
    both = jnp.concatenate(results, axis=0)
    both = both + pltpu.roll(both, LANES - KPAD, 1)
    if turned:
        out_ref[0] = both.T[:KPAD]
    else:
        out_ref[...] = both


def m2l(sources, classes, table, ops, first, steps, turned, slots):
    if turned:
        per = slots // LANES
        shape = (steps // per, KPAD, slots)
        out_spec = pl.BlockSpec(
            (1, KPAD, LANES), lambda i: ((IN_ROW >> (4 * (i // per))) & 7, 0, i % per)
        )
    else:
        shape = (steps * LANES, LANES)
        out_spec = pl.BlockSpec((LANES, LANES), lambda i: (i, 0))
    return pl.pallas_call(
        functools.partial(m2l_kernel, first=first, turned=turned),
        grid=(steps,),
        out_shape=jax.ShapeDtypeStruct(shape, jnp.float32),
        in_specs=[
            pl.BlockSpec((8, LANES), lambda i: (first + i, 0), memory_space=pltpu.SMEM),
            SMEM_WHOLE,
            VMEM_WHOLE,
            VMEM_WHOLE,
        ],
        out_specs=out_spec,
        scratch_shapes=[pltpu.VMEM((3, BLOCK, LANES), jnp.float32)] * 2,
        compiler_params=params(),
        cost_estimate=cost(10**6, 150 * 10**6),
        name="m2l_slots" if turned else "m2l_cells",
    )(sources, classes, as_rows(table), ops)


def add_back_kernel(list_ref, count_ref, own_ref, *refs):
    slot_refs, out_ref = refs[:4], refs[4]
    rows, sums = refs[5], refs[6:]
    slots = list_ref.shape[1]
    sums[0][...] = own_ref[...]
    for held in sums[1:]:
        held[...] = jnp.zeros_like(held)
    for n in range(8):
        for k in range(slots // LANES):
            live = (lane_ids((KPAD, LANES)) + k * LANES) < count_ref[n]
            part, place = GOT[n]
            values = jnp.where(live, slot_refs[part][place, :, k * LANES : (k + 1) * LANES], 0.0)
            at = n * slots + k * LANES
            rows[at : at + LANES, :] = spread(values)

    @pl.loop(0, slots, step=4)
    def _(first):
        for j in range(4):
            to = [pl.ds(list_ref[n, first + j], 1) for n in range(8)]
            old = [sums[n][to[n], :] for n in range(8)]
            new = [old[n] + rows[pl.ds(n * slots + first + j, 1), :] for n in range(8)]
            for n in range(8):
                sums[n][to[n], :] = new[n]

    @pl.loop(0, own_ref.shape[0] // LANES)
    def _(k):
        at = pl.ds(pl.multiple_of(k * LANES, LANES), LANES)
        parts = [held[at, :] for held in sums]
        while len(parts) > 1:
            parts = [a + b for a, b in zip(parts[::2], parts[1::2])]
        out_ref[:, at] = parts[0].T[: out_ref.shape[0]]


def add_back(proxy_list, proxy_count, own_rows, slot_fields, coef_count):
    cell_count = own_rows.shape[0]
    slots = proxy_list.shape[1]
    return pl.pallas_call(
        add_back_kernel,
        out_shape=jax.ShapeDtypeStruct((coef_count, cell_count), jnp.float32),
        in_specs=[SMEM_WHOLE, SMEM_WHOLE] + [VMEM_WHOLE] * 5,
        out_specs=VMEM_WHOLE,
        scratch_shapes=[pltpu.VMEM((8 * slots, LANES), jnp.float32)]
        + [pltpu.VMEM((cell_count, LANES), jnp.float32)] * 8,
        compiler_params=params(),
        cost_estimate=cost(10**6, 30 * 10**6),
        name="add_back",
    )(proxy_list, proxy_count, own_rows, *slot_fields)


def carve_kernel(mesh_ref, out_ref, sems, *, first):
    sources, count, rows, width = out_ref.shape
    copies = [
        pltpu.make_async_copy(
            mesh_ref.at[pl.ds(first, count), pl.ds(s * rows, rows), :], out_ref.at[s], sems.at[s]
        )
        for s in range(sources)
    ]
    for copy in copies:
        copy.start()
    for copy in copies:
        copy.wait()


def carve(mesh, first, count, sources):
    rows, width = mesh.shape[1] // sources, mesh.shape[2]
    return pl.pallas_call(
        functools.partial(carve_kernel, first=first),
        out_shape=jax.ShapeDtypeStruct((sources, count, rows, width), jnp.float32),
        in_specs=[pl.BlockSpec(memory_space=pl.ANY)],
        out_specs=VMEM_WHOLE,
        scratch_shapes=[pltpu.SemaphoreType.DMA((sources,))],
        compiler_params=params(),
        cost_estimate=cost(0, 8 * count * sources * rows * width),
        name="carve",
    )(mesh)


def first_part_kernel(mesh_ref, place_ref, cells_ref, out_ref, sems, *, count, rows):
    sources, _, width = out_ref.shape
    copies = [
        pltpu.make_async_copy(
            mesh_ref.at[p, pl.ds(s * rows, rows), :],
            out_ref.at[s, pl.ds(p * rows, rows), :],
            sems.at[p, s],
        )
        for p in range(count)
        for s in range(sources)
    ]
    for copy in copies:
        copy.start()
    is_first = lane_ids((TOP_ROWS, LANES)) < KPAD
    rest = jnp.zeros((KPAD - cells_ref.shape[0], LANES), jnp.float32)
    table = spread(jnp.concatenate([cells_ref[:, :LANES], rest], axis=0))
    top = jnp.where(is_first, table[:TOP_ROWS, :], table[TOP_ROWS : 2 * TOP_ROWS, :])
    blocks = [place_ref[...].astype(jnp.float32), cell_lines(cells_ref), top]
    at = count * rows
    for block in blocks:
        high = block.shape[0] * LANES // width
        for h in range(width // LANES):
            for s in range(sources):
                out_ref[s, at : at + high, h * LANES : (h + 1) * LANES] = block[
                    h * high : (h + 1) * high, :
                ]
        at += high
    for copy in copies:
        copy.wait()


def cell_lines(cells_ref):
    lines = [cells_ref[0:1, k : k + LANES] for k in range(0, cells_ref.shape[1], LANES)]
    return DEPOSIT_SCALE * jnp.concatenate(lines, axis=0)


def first_part(mesh, place, multipoles, sources, count):
    rows, width = mesh.shape[1] // sources, mesh.shape[2]
    extra = (2 * place.size + TOP_ROWS * LANES) // width
    return pl.pallas_call(
        functools.partial(first_part_kernel, count=count, rows=rows),
        out_shape=jax.ShapeDtypeStruct((sources, count * rows + extra, width), jnp.float32),
        in_specs=[pl.BlockSpec(memory_space=pl.ANY), VMEM_WHOLE, VMEM_WHOLE],
        out_specs=VMEM_WHOLE,
        scratch_shapes=[
            pltpu.SemaphoreType.DMA((count, sources)),
        ],
        compiler_params=params(),
        cost_estimate=cost(0, 8 * sources * rows * width),
        name="first_part",
    )(mesh, place.reshape(-1, LANES), multipoles)


def log2(value):
    return value.bit_length() - 1


def sift_kernel(mine_ref, part_ref, code_ref, value_ref, bound_ref, top_ref, ride, sem, *, count, planes, rows):
    sources, extra, width = ride.shape
    lines = code_ref.shape[0] // sources
    copy = pltpu.make_async_copy(part_ref.at[:, pl.ds(count * rows, extra), :], ride, sem)
    copy.start()
    copy.wait()

    def unfold(first, count):
        high = count * LANES // width
        return jnp.concatenate(
            [
                ride[s, first : first + high, h * LANES : (h + 1) * LANES]
                for s in range(sources)
                for h in range(width // LANES)
            ],
            axis=0,
        )

    step = lines * LANES // width
    place = unfold(0, lines).astype(jnp.int32)
    value = unfold(step, lines)
    top_ref[...] = unfold(2 * step, TOP_ROWS)

    row_at, mesh_rows = log2(width), rows * sources
    plane = place >> (row_at + log2(mesh_rows))
    row = (place >> row_at) & (mesh_rows - 1)
    column = place & (width - 1)
    tiles = width // LANES
    target = (plane * tiles + (column >> LANE_SHIFT)) * rows + (row & (rows - 1))
    none = planes * tiles * rows * LANES
    mine = (row >> log2(rows)) == mine_ref[0]
    lanes = lane_ids(place.shape)
    code = jnp.where(mine, target * LANES + (column & (LANES - 1)), none)
    value = jnp.where(mine, value, 0.0)
    ahead = jnp.where(mine, 1, 0)
    for b in range(LANE_SHIFT):
        ahead = ahead + jnp.where(lanes >= (1 << b), pltpu.roll(ahead, 1 << b, 1), 0)
    shift = jnp.where(mine, lanes + 1 - ahead, 0)
    for b in range(LANE_SHIFT):
        back = LANES - (1 << b)
        moves = (shift >> b) & 1
        comes = pltpu.roll(moves, back, 1) == 1
        goes = moves == 1
        code = jnp.where(comes, pltpu.roll(code, back, 1), jnp.where(goes, none, code))
        value = jnp.where(comes, pltpu.roll(value, back, 1), jnp.where(goes, 0.0, value))
        shift = jnp.where(comes, pltpu.roll(shift, back, 1), jnp.where(goes, 0, shift))
    code_ref[...] = code
    value_ref[...] = value
    counts = jnp.sum(jnp.where(mine, 1.0, 0.0), axis=1, keepdims=True)
    counts = jnp.broadcast_to(counts, mine.shape).reshape(2 * sources, lines // 2, LANES)
    bound_ref[...] = jnp.max(counts, axis=0).astype(jnp.int32)


def sift(part, mine, count, planes, rows, lines):
    sources, whole_rows, width = part.shape
    extra = whole_rows - count * rows
    shape = (sources * lines, LANES)
    return pl.pallas_call(
        functools.partial(sift_kernel, count=count, planes=planes, rows=rows),
        out_shape=(
            jax.ShapeDtypeStruct(shape, jnp.int32),
            jax.ShapeDtypeStruct(shape, jnp.float32),
            jax.ShapeDtypeStruct((lines // 2, LANES), jnp.int32),
            jax.ShapeDtypeStruct((sources * TOP_ROWS, LANES), jnp.float32),
        ),
        in_specs=[SMEM_WHOLE, pl.BlockSpec(memory_space=pl.ANY)],
        out_specs=(VMEM_WHOLE,) * 4,
        scratch_shapes=[pltpu.VMEM((sources, extra, width), jnp.float32), pltpu.SemaphoreType.DMA],
        compiler_params=params(),
        cost_estimate=cost(10**6, 8 * 10**6),
        name="sift",
    )(mine, part)


def deposit_kernel(code_ref, value_ref, bound_ref, *refs):
    sources = len(refs) // 2
    outs, others = refs[:sources], refs[sources:]
    lines = code_ref.shape[0] // (2 * sources)
    lanes = lane_ids((1, LANES))
    for held in refs:
        held[...] = jnp.zeros_like(held)

    def line(g, _):
        def one(j):
            at = [((2 * s + h) * lines + g, j) for h in range(2) for s in range(sources)]
            codes = [code_ref[i] for i in at]
            to = [pl.ds(code >> LANE_SHIFT, 1) for code in codes]
            old = [held[rows, :] for held, rows in zip(refs, to)]
            new = [
                row + jnp.where(lanes == (code & (LANES - 1)), value_ref[i], 0.0)
                for row, code, i in zip(old, codes, at)
            ]
            for held, rows, row in zip(refs, to, new):
                held[rows, :] = row

        def four(i, _):
            for j in range(4):
                one(4 * i + j)
            return 0

        return lax.fori_loop(0, (bound_ref[g, 0] + 3) >> 2, four, 0)

    lax.fori_loop(0, lines, line, 0)
    for out_ref, held in zip(outs, others):
        out_ref[...] = out_ref[...] + held[...]


def deposit(codes, values, bounds, rows, sources):
    return pl.pallas_call(
        deposit_kernel,
        out_shape=(jax.ShapeDtypeStruct((rows, LANES), jnp.float32),) * sources,
        in_specs=[SMEM_WHOLE] * 3,
        out_specs=(VMEM_WHOLE,) * sources,
        scratch_shapes=[pltpu.VMEM((rows, LANES), jnp.float32)] * sources,
        compiler_params=params(),
        cost_estimate=cost(10**6, 40 * 10**6),
        name="deposit",
    )(codes, values, bounds)


def fourier_tables(length):
    points, half = length // 2, length // 4
    positions = np.arange(points)
    scale = 1.0 / np.sqrt(length)
    parts = []
    for odd in range(2):
        ks = 2 * np.arange(half) + odd
        angles = (positions[:, None] * ks[None, :] % length) * (2.0 * np.pi / length)
        imag = -np.sin(angles) * scale
        if not odd:
            imag[:, 0] = np.where(positions % 2 == 0, scale, -scale)
        parts.append(np.concatenate([np.cos(angles) * scale, imag], axis=1))
    whole = np.stack(parts)
    high = whole.astype(ml_dtypes.bfloat16)
    low = (whole - high.astype(np.float64)).astype(ml_dtypes.bfloat16)
    return high, low


def fourier_kernel(*refs, sources):
    mesh_ref, add_refs = refs[0], refs[1 : 1 + sources]
    high_ref, low_ref = refs[1 + sources], refs[2 + sources]
    out_ref = refs[-1]
    rows, width = mesh_ref.shape[1:]
    pieces = []
    for s in range(sources):
        for h in range(width // LANES):
            pieces.append(
                mesh_ref[s, :, h * LANES : (h + 1) * LANES]
                + add_refs[s][h * rows : (h + 1) * rows, :]
            )
    mid = len(pieces) // 2
    halves = []
    for odd in range(2):
        if odd:
            folded = [a - b for a, b in zip(pieces[:mid], pieces[mid:])]
        else:
            folded = [a + b for a, b in zip(pieces[:mid], pieces[mid:])]
        values = jnp.concatenate(folded, axis=1)
        high = values.astype(jnp.bfloat16)
        low = (values - high.astype(jnp.float32)).astype(jnp.bfloat16)
        both = jnp.dot(
            jnp.concatenate([high, low], axis=0), high_ref[odd], preferred_element_type=jnp.float32
        )
        halves.append(
            both[:rows]
            + both[rows:]
            + jnp.dot(high, low_ref[odd], preferred_element_type=jnp.float32)
        )
    lanes = lane_ids((rows, LANES))
    is_first = lanes == 0
    is_odd = (lanes & 1) == 1
    steps = lanes >> 1
    tiles = len(pieces)
    per = tiles // 4

    def tile(odd, part, j):
        at = (part * per + j) * LANES
        return halves[odd][:, at : at + LANES]

    def pick(value, lane):
        return jnp.take_along_axis(value, lane, axis=1, mode="promise_in_bounds")

    for j in range(tiles):
        for part in range(2):
            if j < tiles // 2:
                at = BLOCK * j
                lane = (at % LANES) + steps
                even = pick(tile(0, part, at // LANES), lane)
                odd = pick(tile(1, part, at // LANES), lane)
                if j == 0 and part == 1:
                    even = jnp.where(is_first, 0.0, even)
            else:
                at = BLOCK * (tiles - j)
                last = (at - 1) // LANES
                even = pick(tile(0, part, last), (at - steps) & (LANES - 1))
                odd = pick(tile(1, part, last), ((at - 1) % LANES) - steps)
                if at % LANES == 0 and j > tiles // 2:
                    even = jnp.where(is_first, tile(0, part, at // LANES), even)
                if part == 1:
                    even, odd = -even, -odd
                if j == tiles // 2:
                    even = jnp.where(is_first, 0.0 if part else tile(0, 1, 0), even)
            out_ref[part, 0, :, j * LANES : (j + 1) * LANES] = jnp.where(is_odd, odd, even)


def fourier(mesh_part, count, adds, tables, first, planes, so_far, rows):
    sources, _, width = mesh_part.shape
    length = sources * width
    add_rows = (width // LANES) * rows
    operands = [mesh_part, *adds, *tables]
    in_specs = (
        [pl.BlockSpec((sources, rows, width), lambda p: (0, p, 0))]
        + [pl.BlockSpec((add_rows, LANES), lambda p: (first + p, 0))] * sources
        + [
            pl.BlockSpec((2, length // 2, length // 2), lambda p: (0, 0, 0), pipeline_mode=pl.Buffered(1))
        ]
        * 2
    )
    aliases = {}
    if so_far is not None:
        aliases = {len(operands): 0}
        operands.append(so_far)
        in_specs.append(pl.BlockSpec(memory_space=pl.ANY))
    return pl.pallas_call(
        functools.partial(fourier_kernel, sources=sources),
        grid=(count,),
        out_shape=jax.ShapeDtypeStruct((2, planes, rows, length), jnp.float32),
        in_specs=in_specs,
        out_specs=pl.BlockSpec((2, 1, rows, length), lambda p: (0, first + p, 0, 0)),
        input_output_aliases=aliases,
        compiler_params=params(),
        cost_estimate=cost(10**6, count * 10 * 10**6),
        name="fourier",
    )(*operands)


def after(value, *others):
    return lax.optimization_barrier((value, *others))[0]


def on_device(
    multipoles,
    proxy_list,
    proxy_count,
    pair_source,
    pair_target,
    block_class,
    m2l_ops,
    cell_mesh,
    pm_density,
    *,
    n_gx,
    n_gy,
):
    coef_count, cell_count = multipoles.shape
    slots = proxy_list.shape[2]
    planes, mesh_rows, width = pm_density.shape
    own_rows = mesh_rows // n_gx
    domains = n_gx * n_gy
    lists, counts = proxy_list[0], proxy_count[0]

    def send(part):
        return lax.all_to_all(part, "gx", 0, 0, tiled=True)

    spans = []
    first = 0
    for size in CHUNKS:
        spans.append((first, size))
        first += size

    parts = [send(first_part(pm_density, cell_mesh, multipoles, n_gx, spans[0][1]))]
    carved = [
        carve(pm_density, at, size, n_gx).reshape(n_gx, size * own_rows, width)
        for at, size in spans[1:]
    ]

    cells = jnp.pad(multipoles, ((0, KPAD - coef_count), (0, 0)))
    base = cell_count + 8 * slots
    table = own_table(cells, base + TOP * domains)
    outgoing = pack(table, cell_count, lists, counts)

    top = pair_source - base
    domain = top >> log2(TOP)
    along = (domain & (n_gy - 1)) ^ lax.axis_index("gy")
    place = (along * n_gx + (domain >> log2(n_gy))) * TOP_ROWS + (top & (TOP_ROWS - 1))
    top = base + ((top >> log2(TOP_ROWS)) & 1) * (TOP_ROWS * domains) + place
    wanted = jnp.where(pair_source < base, pair_source, top)
    sources = order(((wanted << SHIFT) | (pair_target & (BLOCK - 1))).reshape(-1, LANES))

    arrived = along_gx(*along_gy(*outgoing[:2]), after(outgoing[2], sources))

    ops = split(m2l_ops.transpose(0, 2, 1))

    tiles = width // LANES
    add_rows = planes * tiles * own_rows
    mine = lax.axis_index("gx").astype(jnp.int32).reshape(1)
    codes, amounts, bounds, top_own = sift(
        parts[0], mine, spans[0][1], planes, own_rows, cell_count // LANES
    )
    tops = [top_own]
    for bit in range(log2(n_gy)):
        held = jnp.concatenate(tops, axis=0) if bit else top_own
        tops.append(lax.ppermute(held, "gy", [(i, i ^ (1 << bit)) for i in range(n_gy)]))

    parts.append(send(after(carved[0], parts[0], ops, *arrived)))
    adds = deposit(codes, amounts, bounds, add_rows + 8, n_gx)
    table = whole_table(table, arrived, tops)
    cell_steps = cell_count // LANES
    slot_steps = 8 * slots // LANES
    slot_fields = m2l(sources, block_class, table, ops, cell_steps, slot_steps, True, slots)
    returned = along_gx(*along_gy(slot_fields[:3], slot_fields[3:6]), slot_fields[6:])
    parts.append(send(after(carved[1], parts[1], adds[0], *returned)))
    tables = fourier_tables(n_gx * width)
    spectrum = fourier(parts[0], spans[0][1], adds, tables, 0, planes, None, own_rows)
    own_fields = m2l(sources, block_class, table, ops, 0, cell_steps, False, slots)
    spectrum = fourier(parts[1], spans[1][1], adds, tables, spans[1][0], planes, spectrum, own_rows)
    own_fields = after(own_fields, spectrum)
    field_tensors = add_back(lists, counts, own_fields, returned, coef_count)
    spectrum = fourier(parts[2], spans[2][1], adds, tables, spans[2][0], planes, spectrum, own_rows)
    return (field_tensors, spectrum)


def solution(mesh):
    placed = (
        P(None, ("gx", "gy")),
        P(("gx", "gy"), None, None),
        P(("gx", "gy"), None),
        P(("gx", "gy")),
        P(("gx", "gy")),
        P(("gx", "gy")),
        P(),
        P(("gx", "gy")),
        P("gy", None, "gx"),
    )
    return jax.shard_map(
        functools.partial(on_device, n_gx=mesh.shape["gx"], n_gy=mesh.shape["gy"]),
        mesh=mesh,
        in_specs=placed,
        out_specs=(P(None, ("gx", "gy")), P(None, "gy", "gx", None)),
        check_vma=False,
    )
```

```python
import functools

import jax
import jax.numpy as jnp
import ml_dtypes
import numpy as np
from jax import lax
from jax.experimental import pallas as pl
from jax.experimental.pallas import tpu as pltpu
from jax.sharding import PartitionSpec as P

TOP = 32
BLOCK = 64
LANES = 128
KPAD = 40
COPIES = 3
PER_WINDOW = 8
SHIFT = 6
LANE_SHIFT = 7
VMEM_BYTES = 48 * 1024 * 1024
CHUNKS = (1, 4, 3)
TOP_ROWS = TOP // 2

DEPOSIT_SCALE = 8.0
SENT = ((0, 0), (2, 0), (1, 0), (0, 1), (1, 1), (0, 2), (2, 1), (1, 2))
GOT = ((3, 2), (3, 1), (3, 0), (1, 1), (0, 1), (2, 2), (2, 1), (2, 0))
IN_ROW = 0x57241360

SMEM_WHOLE = pl.BlockSpec(memory_space=pltpu.SMEM)
VMEM_WHOLE = pl.BlockSpec(memory_space=pltpu.VMEM)


def params():
    return pltpu.CompilerParams(vmem_limit_bytes=VMEM_BYTES)


def cost(flops, nbytes):
    return pl.CostEstimate(flops=flops, bytes_accessed=nbytes, transcendentals=0)


def spread(block):
    rest = jnp.zeros((LANES - COPIES * KPAD, LANES), jnp.float32)
    return jnp.concatenate([block] * COPIES + [rest], axis=0).T


def lane_ids(shape):
    return lax.broadcasted_iota(jnp.int32, shape, len(shape) - 1)


def own_table_kernel(cells_ref, out_ref):
    @pl.loop(0, cells_ref.shape[1] // LANES)
    def _(k):
        at = pl.multiple_of(k * LANES, LANES)
        out_ref[pl.ds(at, LANES), :] = spread(cells_ref[:, pl.ds(at, LANES)])


def own_table(cells, rows):
    count = cells.shape[1]
    return pl.pallas_call(
        own_table_kernel,
        grid=(1,),
        out_shape=jax.ShapeDtypeStruct((rows, LANES), jnp.float32),
        in_specs=[pl.BlockSpec((KPAD, count), lambda i: (0, 0))],
        out_specs=pl.BlockSpec((count, LANES), lambda i: (0, 0)),
        compiler_params=params(),
        cost_estimate=cost(10**6, 12 * 10**6),
        name="own_table",
    )(cells)


def cut_rows(refs, first, stop):
    pieces, at = [], 0
    for ref in refs:
        low, high = max(first - at, 0), min(stop - at, ref.shape[0])
        if low < high:
            pieces.append(ref[low:high, :])
        at += ref.shape[0]
    return jnp.concatenate(pieces, axis=0) if len(pieces) > 1 else pieces[0]


def whole_table_kernel(*refs, slot_steps):
    top_refs, out_ref = refs[4:-2], refs[-1]
    step = pl.program_id(0)
    for k in range(slot_steps):

        @pl.when(step == k)
        def _():
            at = 0
            for n in (2 * k, 2 * k + 1):
                part, place = GOT[n]
                for c in range(refs[part].shape[2] // LANES):
                    block = refs[part][place, :, c * LANES : (c + 1) * LANES]
                    out_ref[at : at + LANES, :] = spread(block)
                    at += LANES

    rows = out_ref.shape[0]
    total = sum(ref.shape[0] for ref in top_refs)
    lanes = lane_ids((rows, LANES))
    for k in range(2 * total // rows):

        @pl.when(step == slot_steps + k)
        def _():
            pieces = []
            for first in range(k * rows, (k + 1) * rows, min(rows, total)):
                group, at = first // total, first % total
                value = cut_rows(top_refs, at, at + min(rows, total))
                pieces.append(pltpu.roll(value, LANES - KPAD, 1) if group else value)
            value = jnp.concatenate(pieces, axis=0) if len(pieces) > 1 else pieces[0]
            value = jnp.where(lanes < KPAD, value, 0.0)
            out_ref[...] = value + pltpu.roll(value, KPAD, 1) + pltpu.roll(value, 2 * KPAD, 1)


def whole_table(table, arrived, tops):
    slots = arrived[0].shape[2]
    rows = 2 * slots
    top_rows = 2 * sum(part.shape[0] for part in tops)
    first = (table.shape[0] - 8 * slots - top_rows) // rows
    return pl.pallas_call(
        functools.partial(whole_table_kernel, slot_steps=4),
        grid=(4 + top_rows // rows,),
        out_shape=jax.ShapeDtypeStruct(table.shape, jnp.float32),
        in_specs=[VMEM_WHOLE] * (4 + len(tops)) + [pl.BlockSpec(memory_space=pl.ANY)],
        out_specs=pl.BlockSpec((rows, LANES), lambda i: (first + i, 0)),
        input_output_aliases={4 + len(tops): 0},
        compiler_params=params(),
        cost_estimate=cost(10**6, 16 * 10**6),
        name="whole_table",
    )(*arrived, *tops, table)


def as_rows(table):
    return table.reshape(table.shape[0], 1, LANES)


def pack_kernel(list_ref, count_ref, table_ref, *refs):
    outs, held = refs[:3], refs[3:]
    slot_tiles = list_ref.shape[1] // LANES
    for n in range(8):

        @pl.loop(0, slot_tiles, step=len(held))
        def _(i):
            firsts = [pl.multiple_of((i + k) * LANES, LANES) for k in range(len(held))]
            for first, rows in zip(firsts, held):
                for r in range(LANES):
                    rows[r : r + 1, :] = table_ref[list_ref[n, first + r]]
            for first, rows in zip(firsts, held):
                live = (lane_ids((KPAD, LANES)) + first) < count_ref[n]
                part, at = SENT[n]
                outs[part][at, :, pl.ds(first, LANES)] = jnp.where(live, rows[...].T[:KPAD], 0.0)


def pack(table, cell_count, proxy_list, proxy_count):
    slots = proxy_list.shape[1]
    return pl.pallas_call(
        pack_kernel,
        grid=(1,),
        out_shape=tuple(jax.ShapeDtypeStruct((size, KPAD, slots), jnp.float32) for size in (3, 3, 2)),
        in_specs=[
            SMEM_WHOLE,
            SMEM_WHOLE,
            pl.BlockSpec((cell_count, 1, LANES), lambda i: (0, 0, 0)),
        ],
        out_specs=tuple(
            pl.BlockSpec((size, KPAD, slots), lambda i: (0, 0, 0)) for size in (3, 3, 2)
        ),
        scratch_shapes=[pltpu.VMEM((LANES, LANES), jnp.float32)] * 2,
        compiler_params=params(),
        cost_estimate=cost(10**6, 25 * 10**6),
        name="pack",
    )(proxy_list, proxy_count, as_rows(table))


def shift(value, axis, by):
    count = lax.axis_size(axis)
    return lax.ppermute(value, axis, [(i, (i + by) % count) for i in range(count)])


def along_gy(down, up):
    return shift(down, "gy", -1), shift(up, "gy", 1)


def along_gx(down, up, mid):
    left = shift(jnp.stack([down[0], mid[0], up[0]]), "gx", -1)
    right = shift(jnp.stack([down[2], mid[1], up[2]]), "gx", 1)
    return down, up, left, right


def order_kernel(packed_ref, out_ref):
    lanes = lane_ids((LANES, LANES))
    within = lanes & (BLOCK - 1)
    base = lanes - within

    @pl.loop(0, packed_ref.shape[0] // LANES)
    def _(k):
        at = pl.ds(pl.multiple_of(k * LANES, LANES), LANES)
        packed = packed_ref[at, :]

        def step(i, ordered):
            value = jnp.take_along_axis(packed, base + i, axis=1, mode="promise_in_bounds")
            return jnp.where((value & (BLOCK - 1)) == within, value, ordered)

        ordered = lax.fori_loop(0, BLOCK, step, jnp.zeros_like(packed), unroll=8)
        out_ref[at, :] = ordered >> SHIFT


def order(packed):
    return pl.pallas_call(
        order_kernel,
        out_shape=jax.ShapeDtypeStruct(packed.shape, jnp.int32),
        in_specs=[VMEM_WHOLE],
        out_specs=VMEM_WHOLE,
        compiler_params=params(),
        cost_estimate=cost(10**6, 20 * 10**6),
        name="order",
    )(packed)


def split_kernel(ops_ref, out_ref, *, group):
    coefs = ops_ref.shape[1]

    @pl.loop(0, ops_ref.shape[0], step=group)
    def _(c):
        at = pl.ds(c, group)
        value = ops_ref[at]
        high = value.astype(jnp.bfloat16).astype(jnp.float32)
        out_ref[at] = jnp.zeros((group, KPAD, LANES), jnp.float32)
        out_ref[at, :coefs, :coefs] = high
        out_ref[at, :coefs, KPAD : KPAD + coefs] = value - high


def split(turned_ops):
    classes = turned_ops.shape[0]
    group = max(size for size in range(1, 10) if classes % size == 0)
    return pl.pallas_call(
        functools.partial(split_kernel, group=group),
        out_shape=jax.ShapeDtypeStruct((classes, KPAD, LANES), jnp.float32),
        in_specs=[VMEM_WHOLE],
        out_specs=VMEM_WHOLE,
        compiler_params=params(),
        cost_estimate=cost(10**6, 12 * 10**6),
        name="split",
    )(turned_ops)


def m2l_kernel(source_ref, class_ref, table_ref, ops_ref, out_ref, *gathered, first, turned):
    step = first + pl.program_id(0)
    lanes = lane_ids((1, LANES))
    in_first = lanes < KPAD
    in_second = lanes < 2 * KPAD

    def row(b, t):
        return table_ref[source_ref[b // 2, (b % 2) * BLOCK + t]]

    for u in range(2):
        for t in range(BLOCK):
            for g in range(3):
                b = u * PER_WINDOW + 3 * g
                one, two = row(b, t), row(b + 1, t)
                three = row(b + 2, t) if g < 2 else two
                gathered[u][g, t : t + 1, :] = jnp.where(
                    in_first, one, jnp.where(in_second, two, three)
                )

    rest = jnp.zeros((LANES - COPIES * KPAD, LANES), jnp.float32)
    none = jnp.zeros((KPAD, LANES), jnp.float32)
    results = []
    for u in range(2):
        total = jnp.zeros((BLOCK, LANES), jnp.float32)
        for g in range(3):
            held = []
            for s in range(3):
                b = 3 * g + s
                if b < PER_WINDOW:
                    held.append(ops_ref[class_ref[step * 2 * PER_WINDOW + u * PER_WINDOW + b]])
                else:
                    held.append(none)
            weights = jnp.concatenate(held + [rest], axis=0).astype(jnp.bfloat16)
            values = gathered[u][g]
            high = values.astype(jnp.bfloat16)
            low = (values - high.astype(jnp.float32)).astype(jnp.bfloat16)
            total += jnp.dot(high, weights, preferred_element_type=jnp.float32)
            total += jnp.dot(low, weights, preferred_element_type=jnp.float32)
        results.append(total)
    both = jnp.concatenate(results, axis=0)
    both = both + pltpu.roll(both, LANES - KPAD, 1)
    if turned:
        out_ref[0] = both.T[:KPAD]
    else:
        out_ref[...] = both


def m2l(sources, classes, table, ops, first, steps, turned, slots):
    if turned:
        per = slots // LANES
        shape = (steps // per, KPAD, slots)
        out_spec = pl.BlockSpec(
            (1, KPAD, LANES), lambda i: ((IN_ROW >> (4 * (i // per))) & 7, 0, i % per)
        )
    else:
        shape = (steps * LANES, LANES)
        out_spec = pl.BlockSpec((LANES, LANES), lambda i: (i, 0))
    return pl.pallas_call(
        functools.partial(m2l_kernel, first=first, turned=turned),
        grid=(steps,),
        out_shape=jax.ShapeDtypeStruct(shape, jnp.float32),
        in_specs=[
            pl.BlockSpec((8, LANES), lambda i: (first + i, 0), memory_space=pltpu.SMEM),
            SMEM_WHOLE,
            VMEM_WHOLE,
            VMEM_WHOLE,
        ],
        out_specs=out_spec,
        scratch_shapes=[pltpu.VMEM((3, BLOCK, LANES), jnp.float32)] * 2,
        compiler_params=params(),
        cost_estimate=cost(10**6, 150 * 10**6),
        name="m2l_slots" if turned else "m2l_cells",
    )(sources, classes, as_rows(table), ops)


def add_back_kernel(list_ref, count_ref, own_ref, *refs):
    slot_refs, out_ref = refs[:4], refs[4]
    rows, sums = refs[5], refs[6:]
    slots = list_ref.shape[1]
    sums[0][...] = own_ref[...]
    for held in sums[1:]:
        held[...] = jnp.zeros_like(held)
    for n in range(8):
        for k in range(slots // LANES):
            live = (lane_ids((KPAD, LANES)) + k * LANES) < count_ref[n]
            part, place = GOT[n]
            values = jnp.where(live, slot_refs[part][place, :, k * LANES : (k + 1) * LANES], 0.0)
            at = n * slots + k * LANES
            rows[at : at + LANES, :] = spread(values)

    @pl.loop(0, slots, step=4)
    def _(first):
        for j in range(4):
            to = [pl.ds(list_ref[n, first + j], 1) for n in range(8)]
            old = [sums[n][to[n], :] for n in range(8)]
            new = [old[n] + rows[pl.ds(n * slots + first + j, 1), :] for n in range(8)]
            for n in range(8):
                sums[n][to[n], :] = new[n]

    @pl.loop(0, own_ref.shape[0] // LANES)
    def _(k):
        at = pl.ds(pl.multiple_of(k * LANES, LANES), LANES)
        parts = [held[at, :] for held in sums]
        while len(parts) > 1:
            parts = [a + b for a, b in zip(parts[::2], parts[1::2])]
        out_ref[:, at] = parts[0].T[: out_ref.shape[0]]


def add_back(proxy_list, proxy_count, own_rows, slot_fields, coef_count):
    cell_count = own_rows.shape[0]
    slots = proxy_list.shape[1]
    return pl.pallas_call(
        add_back_kernel,
        out_shape=jax.ShapeDtypeStruct((coef_count, cell_count), jnp.float32),
        in_specs=[SMEM_WHOLE, SMEM_WHOLE] + [VMEM_WHOLE] * 5,
        out_specs=VMEM_WHOLE,
        scratch_shapes=[pltpu.VMEM((8 * slots, LANES), jnp.float32)]
        + [pltpu.VMEM((cell_count, LANES), jnp.float32)] * 8,
        compiler_params=params(),
        cost_estimate=cost(10**6, 30 * 10**6),
        name="add_back",
    )(proxy_list, proxy_count, own_rows, *slot_fields)


def carve_kernel(mesh_ref, out_ref, sems, *, first):
    sources, count, rows, width = out_ref.shape
    copies = [
        pltpu.make_async_copy(
            mesh_ref.at[pl.ds(first, count), pl.ds(s * rows, rows), :], out_ref.at[s], sems.at[s]
        )
        for s in range(sources)
    ]
    for copy in copies:
        copy.start()
    for copy in copies:
        copy.wait()


def carve(mesh, first, count, sources):
    rows, width = mesh.shape[1] // sources, mesh.shape[2]
    return pl.pallas_call(
        functools.partial(carve_kernel, first=first),
        out_shape=jax.ShapeDtypeStruct((sources, count, rows, width), jnp.float32),
        in_specs=[pl.BlockSpec(memory_space=pl.ANY)],
        out_specs=VMEM_WHOLE,
        scratch_shapes=[pltpu.SemaphoreType.DMA((sources,))],
        compiler_params=params(),
        cost_estimate=cost(0, 8 * count * sources * rows * width),
        name="carve",
    )(mesh)


def first_part_kernel(mesh_ref, place_ref, cells_ref, out_ref, sems, *, count, rows):
    sources, _, width = out_ref.shape
    copies = [
        pltpu.make_async_copy(
            mesh_ref.at[p, pl.ds(s * rows, rows), :],
            out_ref.at[s, pl.ds(p * rows, rows), :],
            sems.at[p, s],
        )
        for p in range(count)
        for s in range(sources)
    ]
    for copy in copies:
        copy.start()
    is_first = lane_ids((TOP_ROWS, LANES)) < KPAD
    rest = jnp.zeros((KPAD - cells_ref.shape[0], LANES), jnp.float32)
    table = spread(jnp.concatenate([cells_ref[:, :LANES], rest], axis=0))
    top = jnp.where(is_first, table[:TOP_ROWS, :], table[TOP_ROWS : 2 * TOP_ROWS, :])
    blocks = [place_ref[...].astype(jnp.float32), cell_lines(cells_ref), top]
    at = count * rows
    for block in blocks:
        high = block.shape[0] * LANES // width
        for h in range(width // LANES):
            for s in range(sources):
                out_ref[s, at : at + high, h * LANES : (h + 1) * LANES] = block[
                    h * high : (h + 1) * high, :
                ]
        at += high
    for copy in copies:
        copy.wait()


def cell_lines(cells_ref):
    lines = [cells_ref[0:1, k : k + LANES] for k in range(0, cells_ref.shape[1], LANES)]
    return DEPOSIT_SCALE * jnp.concatenate(lines, axis=0)


def first_part(mesh, place, multipoles, sources, count):
    rows, width = mesh.shape[1] // sources, mesh.shape[2]
    extra = (2 * place.size + TOP_ROWS * LANES) // width
    return pl.pallas_call(
        functools.partial(first_part_kernel, count=count, rows=rows),
        out_shape=jax.ShapeDtypeStruct((sources, count * rows + extra, width), jnp.float32),
        in_specs=[pl.BlockSpec(memory_space=pl.ANY), VMEM_WHOLE, VMEM_WHOLE],
        out_specs=VMEM_WHOLE,
        scratch_shapes=[
            pltpu.SemaphoreType.DMA((count, sources)),
        ],
        compiler_params=params(),
        cost_estimate=cost(0, 8 * sources * rows * width),
        name="first_part",
    )(mesh, place.reshape(-1, LANES), multipoles)


def log2(value):
    return value.bit_length() - 1


def sift_kernel(mine_ref, part_ref, code_ref, value_ref, bound_ref, top_ref, ride, sem, *, count, planes, rows):
    sources, extra, width = ride.shape
    lines = code_ref.shape[0] // sources
    copy = pltpu.make_async_copy(part_ref.at[:, pl.ds(count * rows, extra), :], ride, sem)
    copy.start()
    copy.wait()

    def unfold(first, count):
        high = count * LANES // width
        return jnp.concatenate(
            [
                ride[s, first : first + high, h * LANES : (h + 1) * LANES]
                for s in range(sources)
                for h in range(width // LANES)
            ],
            axis=0,
        )

    step = lines * LANES // width
    place = unfold(0, lines).astype(jnp.int32)
    value = unfold(step, lines)
    top_ref[...] = unfold(2 * step, TOP_ROWS)

    row_at, mesh_rows = log2(width), rows * sources
    plane = place >> (row_at + log2(mesh_rows))
    row = (place >> row_at) & (mesh_rows - 1)
    column = place & (width - 1)
    tiles = width // LANES
    target = (plane * tiles + (column >> LANE_SHIFT)) * rows + (row & (rows - 1))
    none = planes * tiles * rows * LANES
    mine = (row >> log2(rows)) == mine_ref[0]
    lanes = lane_ids(place.shape)
    code = jnp.where(mine, target * LANES + (column & (LANES - 1)), none)
    value = jnp.where(mine, value, 0.0)
    ahead = jnp.where(mine, 1, 0)
    for b in range(LANE_SHIFT):
        ahead = ahead + jnp.where(lanes >= (1 << b), pltpu.roll(ahead, 1 << b, 1), 0)
    shift = jnp.where(mine, lanes + 1 - ahead, 0)
    for b in range(LANE_SHIFT):
        back = LANES - (1 << b)
        moves = (shift >> b) & 1
        comes = pltpu.roll(moves, back, 1) == 1
        goes = moves == 1
        code = jnp.where(comes, pltpu.roll(code, back, 1), jnp.where(goes, none, code))
        value = jnp.where(comes, pltpu.roll(value, back, 1), jnp.where(goes, 0.0, value))
        shift = jnp.where(comes, pltpu.roll(shift, back, 1), jnp.where(goes, 0, shift))
    code_ref[...] = code
    value_ref[...] = value
    counts = jnp.sum(jnp.where(mine, 1.0, 0.0), axis=1, keepdims=True)
    counts = jnp.broadcast_to(counts, mine.shape).reshape(2 * sources, lines // 2, LANES)
    bound_ref[...] = jnp.max(counts, axis=0).astype(jnp.int32)


def sift(part, mine, count, planes, rows, lines):
    sources, whole_rows, width = part.shape
    extra = whole_rows - count * rows
    shape = (sources * lines, LANES)
    return pl.pallas_call(
        functools.partial(sift_kernel, count=count, planes=planes, rows=rows),
        out_shape=(
            jax.ShapeDtypeStruct(shape, jnp.int32),
            jax.ShapeDtypeStruct(shape, jnp.float32),
            jax.ShapeDtypeStruct((lines // 2, LANES), jnp.int32),
            jax.ShapeDtypeStruct((sources * TOP_ROWS, LANES), jnp.float32),
        ),
        in_specs=[SMEM_WHOLE, pl.BlockSpec(memory_space=pl.ANY)],
        out_specs=(VMEM_WHOLE,) * 4,
        scratch_shapes=[pltpu.VMEM((sources, extra, width), jnp.float32), pltpu.SemaphoreType.DMA],
        compiler_params=params(),
        cost_estimate=cost(10**6, 8 * 10**6),
        name="sift",
    )(mine, part)


def deposit_kernel(code_ref, value_ref, bound_ref, *refs):
    sources = len(refs) // 2
    outs, others = refs[:sources], refs[sources:]
    lines = code_ref.shape[0] // (2 * sources)
    lanes = lane_ids((1, LANES))
    for held in refs:
        held[...] = jnp.zeros_like(held)

    def line(g, _):
        def one(j):
            at = [((2 * s + h) * lines + g, j) for h in range(2) for s in range(sources)]
            codes = [code_ref[i] for i in at]
            to = [pl.ds(code >> LANE_SHIFT, 1) for code in codes]
            old = [held[rows, :] for held, rows in zip(refs, to)]
            new = [
                row + jnp.where(lanes == (code & (LANES - 1)), value_ref[i], 0.0)
                for row, code, i in zip(old, codes, at)
            ]
            for held, rows, row in zip(refs, to, new):
                held[rows, :] = row

        def four(i, _):
            for j in range(4):
                one(4 * i + j)
            return 0

        return lax.fori_loop(0, (bound_ref[g, 0] + 3) >> 2, four, 0)

    lax.fori_loop(0, lines, line, 0)
    for out_ref, held in zip(outs, others):
        out_ref[...] = out_ref[...] + held[...]


def deposit(codes, values, bounds, rows, sources):
    return pl.pallas_call(
        deposit_kernel,
        out_shape=(jax.ShapeDtypeStruct((rows, LANES), jnp.float32),) * sources,
        in_specs=[SMEM_WHOLE] * 3,
        out_specs=(VMEM_WHOLE,) * sources,
        scratch_shapes=[pltpu.VMEM((rows, LANES), jnp.float32)] * sources,
        compiler_params=params(),
        cost_estimate=cost(10**6, 40 * 10**6),
        name="deposit",
    )(codes, values, bounds)


def fourier_tables(length):
    points, half = length // 2, length // 4
    positions = np.arange(points)
    scale = 1.0 / np.sqrt(length)
    parts = []
    for odd in range(2):
        ks = 2 * np.arange(half) + odd
        angles = (positions[:, None] * ks[None, :] % length) * (2.0 * np.pi / length)
        imag = -np.sin(angles) * scale
        if not odd:
            imag[:, 0] = np.where(positions % 2 == 0, scale, -scale)
        parts.append(np.concatenate([np.cos(angles) * scale, imag], axis=1))
    whole = np.stack(parts)
    high = whole.astype(ml_dtypes.bfloat16)
    low = (whole - high.astype(np.float64)).astype(ml_dtypes.bfloat16)
    return high, low


def fourier_kernel(*refs, sources):
    mesh_ref, add_refs = refs[0], refs[1 : 1 + sources]
    high_ref, low_ref = refs[1 + sources], refs[2 + sources]
    out_ref = refs[-1]
    rows, width = mesh_ref.shape[1:]
    pieces = []
    for s in range(sources):
        for h in range(width // LANES):
            pieces.append(
                mesh_ref[s, :, h * LANES : (h + 1) * LANES]
                + add_refs[s][h * rows : (h + 1) * rows, :]
            )
    mid = len(pieces) // 2
    halves = []
    for odd in range(2):
        if odd:
            folded = [a - b for a, b in zip(pieces[:mid], pieces[mid:])]
        else:
            folded = [a + b for a, b in zip(pieces[:mid], pieces[mid:])]
        values = jnp.concatenate(folded, axis=1)
        high = values.astype(jnp.bfloat16)
        low = (values - high.astype(jnp.float32)).astype(jnp.bfloat16)
        both = jnp.dot(
            jnp.concatenate([high, low], axis=0), high_ref[odd], preferred_element_type=jnp.float32
        )
        halves.append(
            both[:rows]
            + both[rows:]
            + jnp.dot(high, low_ref[odd], preferred_element_type=jnp.float32)
        )
    lanes = lane_ids((rows, LANES))
    is_first = lanes == 0
    is_odd = (lanes & 1) == 1
    steps = lanes >> 1
    tiles = len(pieces)
    per = tiles // 4

    def tile(odd, part, j):
        at = (part * per + j) * LANES
        return halves[odd][:, at : at + LANES]

    def pick(value, lane):
        return jnp.take_along_axis(value, lane, axis=1, mode="promise_in_bounds")

    for j in range(tiles):
        for part in range(2):
            if j < tiles // 2:
                at = BLOCK * j
                lane = (at % LANES) + steps
                even = pick(tile(0, part, at // LANES), lane)
                odd = pick(tile(1, part, at // LANES), lane)
                if j == 0 and part == 1:
                    even = jnp.where(is_first, 0.0, even)
            else:
                at = BLOCK * (tiles - j)
                last = (at - 1) // LANES
                even = pick(tile(0, part, last), (at - steps) & (LANES - 1))
                odd = pick(tile(1, part, last), ((at - 1) % LANES) - steps)
                if at % LANES == 0 and j > tiles // 2:
                    even = jnp.where(is_first, tile(0, part, at // LANES), even)
                if part == 1:
                    even, odd = -even, -odd
                if j == tiles // 2:
                    even = jnp.where(is_first, 0.0 if part else tile(0, 1, 0), even)
            out_ref[part, 0, :, j * LANES : (j + 1) * LANES] = jnp.where(is_odd, odd, even)


def fourier(mesh_part, count, adds, tables, first, planes, so_far, rows):
    sources, _, width = mesh_part.shape
    length = sources * width
    add_rows = (width // LANES) * rows
    operands = [mesh_part, *adds, *tables]
    in_specs = (
        [pl.BlockSpec((sources, rows, width), lambda p: (0, p, 0))]
        + [pl.BlockSpec((add_rows, LANES), lambda p: (first + p, 0))] * sources
        + [
            pl.BlockSpec((2, length // 2, length // 2), lambda p: (0, 0, 0), pipeline_mode=pl.Buffered(1))
        ]
        * 2
    )
    aliases = {}
    if so_far is not None:
        aliases = {len(operands): 0}
        operands.append(so_far)
        in_specs.append(pl.BlockSpec(memory_space=pl.ANY))
    return pl.pallas_call(
        functools.partial(fourier_kernel, sources=sources),
        grid=(count,),
        out_shape=jax.ShapeDtypeStruct((2, planes, rows, length), jnp.float32),
        in_specs=in_specs,
        out_specs=pl.BlockSpec((2, 1, rows, length), lambda p: (0, first + p, 0, 0)),
        input_output_aliases=aliases,
        compiler_params=params(),
        cost_estimate=cost(10**6, count * 10 * 10**6),
        name="fourier",
    )(*operands)


def after(value, *others):
    return lax.optimization_barrier((value, *others))[0]


def on_device(
    multipoles,
    proxy_list,
    proxy_count,
    pair_source,
    pair_target,
    block_class,
    m2l_ops,
    cell_mesh,
    pm_density,
    *,
    n_gx,
    n_gy,
):
    coef_count, cell_count = multipoles.shape
    slots = proxy_list.shape[2]
    planes, mesh_rows, width = pm_density.shape
    own_rows = mesh_rows // n_gx
    domains = n_gx * n_gy
    lists, counts = proxy_list[0], proxy_count[0]

    def send(part):
        return lax.all_to_all(part, "gx", 0, 0, tiled=True)

    spans = []
    first = 0
    for size in CHUNKS:
        spans.append((first, size))
        first += size

    parts = [send(first_part(pm_density, cell_mesh, multipoles, n_gx, spans[0][1]))]
    carved = [
        carve(pm_density, at, size, n_gx).reshape(n_gx, size * own_rows, width)
        for at, size in spans[1:]
    ]

    cells = jnp.pad(multipoles, ((0, KPAD - coef_count), (0, 0)))
    base = cell_count + 8 * slots
    table = own_table(cells, base + TOP * domains)
    outgoing = pack(table, cell_count, lists, counts)

    top = pair_source - base
    domain = top >> log2(TOP)
    along = (domain & (n_gy - 1)) ^ lax.axis_index("gy")
    place = (along * n_gx + (domain >> log2(n_gy))) * TOP_ROWS + (top & (TOP_ROWS - 1))
    top = base + ((top >> log2(TOP_ROWS)) & 1) * (TOP_ROWS * domains) + place
    wanted = jnp.where(pair_source < base, pair_source, top)
    sources = order(((wanted << SHIFT) | (pair_target & (BLOCK - 1))).reshape(-1, LANES))

    arrived = along_gx(*along_gy(*outgoing[:2]), after(outgoing[2], sources))

    ops = split(m2l_ops.transpose(0, 2, 1))

    tiles = width // LANES
    add_rows = planes * tiles * own_rows
    mine = lax.axis_index("gx").astype(jnp.int32).reshape(1)
    codes, amounts, bounds, top_own = sift(
        parts[0], mine, spans[0][1], planes, own_rows, cell_count // LANES
    )
    tops = [top_own]
    for bit in range(log2(n_gy)):
        held = jnp.concatenate(tops, axis=0) if bit else top_own
        tops.append(lax.ppermute(held, "gy", [(i, i ^ (1 << bit)) for i in range(n_gy)]))

    parts.append(send(after(carved[0], parts[0], *arrived)))
    adds = deposit(codes, amounts, bounds, add_rows + 8, n_gx)
    table = whole_table(table, arrived, tops)
    cell_steps = cell_count // LANES
    slot_steps = 8 * slots // LANES
    slot_fields = m2l(sources, block_class, table, ops, cell_steps, slot_steps, True, slots)
    mid = after(slot_fields[6:], carved[1])
    returned = along_gx(*along_gy(slot_fields[:3], slot_fields[3:6]), mid)
    parts.append(send(after(carved[1], parts[1], adds[0], *returned)))
    tables = fourier_tables(n_gx * width)
    spectrum = fourier(parts[0], spans[0][1], adds, tables, 0, planes, None, own_rows)
    own_fields = m2l(sources, block_class, table, ops, 0, cell_steps, False, slots)
    spectrum = fourier(parts[1], spans[1][1], adds, tables, spans[1][0], planes, spectrum, own_rows)
    own_fields = after(own_fields, spectrum)
    field_tensors = add_back(lists, counts, own_fields, returned, coef_count)
    spectrum = fourier(parts[2], spans[2][1], adds, tables, spans[2][0], planes, spectrum, own_rows)
    return (field_tensors, spectrum)


def solution(mesh):
    placed = (
        P(None, ("gx", "gy")),
        P(("gx", "gy"), None, None),
        P(("gx", "gy"), None),
        P(("gx", "gy")),
        P(("gx", "gy")),
        P(("gx", "gy")),
        P(),
        P(("gx", "gy")),
        P("gy", None, "gx"),
    )
    return jax.shard_map(
        functools.partial(on_device, n_gx=mesh.shape["gx"], n_gy=mesh.shape["gy"]),
        mesh=mesh,
        in_specs=placed,
        out_specs=(P(None, ("gx", "gy")), P(None, "gy", "gx", None)),
        check_vma=False,
    )
```

```python
import functools

import jax
import jax.numpy as jnp
import ml_dtypes
import numpy as np
from jax import lax
from jax.experimental import pallas as pl
from jax.experimental.pallas import tpu as pltpu
from jax.sharding import PartitionSpec as P

TOP = 32
BLOCK = 64
LANES = 128
KPAD = 40
COPIES = 3
PER_WINDOW = 8
SHIFT = 6
LANE_SHIFT = 7
VMEM_BYTES = 48 * 1024 * 1024
CHUNKS = (1, 4, 3)
TOP_ROWS = TOP // 2

DEPOSIT_SCALE = 8.0
SENT = ((0, 0), (2, 0), (1, 0), (0, 1), (1, 1), (0, 2), (2, 1), (1, 2))
GOT = ((3, 2), (3, 1), (3, 0), (1, 1), (0, 1), (2, 2), (2, 1), (2, 0))
IN_ROW = 0x57241360

SMEM_WHOLE = pl.BlockSpec(memory_space=pltpu.SMEM)
VMEM_WHOLE = pl.BlockSpec(memory_space=pltpu.VMEM)


def params():
    return pltpu.CompilerParams(vmem_limit_bytes=VMEM_BYTES)


def cost(flops, nbytes):
    return pl.CostEstimate(flops=flops, bytes_accessed=nbytes, transcendentals=0)


def spread(block):
    rest = jnp.zeros((LANES - COPIES * KPAD, LANES), jnp.float32)
    return jnp.concatenate([block] * COPIES + [rest], axis=0).T


def lane_ids(shape):
    return lax.broadcasted_iota(jnp.int32, shape, len(shape) - 1)


def own_table_kernel(cells_ref, out_ref):
    @pl.loop(0, cells_ref.shape[1] // LANES)
    def _(k):
        at = pl.multiple_of(k * LANES, LANES)
        out_ref[pl.ds(at, LANES), :] = spread(cells_ref[:, pl.ds(at, LANES)])


def own_table(cells, rows):
    count = cells.shape[1]
    return pl.pallas_call(
        own_table_kernel,
        grid=(1,),
        out_shape=jax.ShapeDtypeStruct((rows, LANES), jnp.float32),
        in_specs=[pl.BlockSpec((KPAD, count), lambda i: (0, 0))],
        out_specs=pl.BlockSpec((count, LANES), lambda i: (0, 0)),
        compiler_params=params(),
        cost_estimate=cost(10**6, 12 * 10**6),
        name="own_table",
    )(cells)


def cut_rows(refs, first, stop):
    pieces, at = [], 0
    for ref in refs:
        low, high = max(first - at, 0), min(stop - at, ref.shape[0])
        if low < high:
            pieces.append(ref[low:high, :])
        at += ref.shape[0]
    return jnp.concatenate(pieces, axis=0) if len(pieces) > 1 else pieces[0]


def whole_table_kernel(*refs, slot_steps):
    top_refs, out_ref = refs[4:-2], refs[-1]
    step = pl.program_id(0)
    for k in range(slot_steps):

        @pl.when(step == k)
        def _():
            at = 0
            for n in (2 * k, 2 * k + 1):
                part, place = GOT[n]
                for c in range(refs[part].shape[2] // LANES):
                    block = refs[part][place, :, c * LANES : (c + 1) * LANES]
                    out_ref[at : at + LANES, :] = spread(block)
                    at += LANES

    rows = out_ref.shape[0]
    total = sum(ref.shape[0] for ref in top_refs)
    lanes = lane_ids((rows, LANES))
    for k in range(2 * total // rows):

        @pl.when(step == slot_steps + k)
        def _():
            pieces = []
            for first in range(k * rows, (k + 1) * rows, min(rows, total)):
                group, at = first // total, first % total
                value = cut_rows(top_refs, at, at + min(rows, total))
                pieces.append(pltpu.roll(value, LANES - KPAD, 1) if group else value)
            value = jnp.concatenate(pieces, axis=0) if len(pieces) > 1 else pieces[0]
            value = jnp.where(lanes < KPAD, value, 0.0)
            out_ref[...] = value + pltpu.roll(value, KPAD, 1) + pltpu.roll(value, 2 * KPAD, 1)


def whole_table(table, arrived, tops):
    slots = arrived[0].shape[2]
    rows = 2 * slots
    top_rows = 2 * sum(part.shape[0] for part in tops)
    first = (table.shape[0] - 8 * slots - top_rows) // rows
    return pl.pallas_call(
        functools.partial(whole_table_kernel, slot_steps=4),
        grid=(4 + top_rows // rows,),
        out_shape=jax.ShapeDtypeStruct(table.shape, jnp.float32),
        in_specs=[VMEM_WHOLE] * (4 + len(tops)) + [pl.BlockSpec(memory_space=pl.ANY)],
        out_specs=pl.BlockSpec((rows, LANES), lambda i: (first + i, 0)),
        input_output_aliases={4 + len(tops): 0},
        compiler_params=params(),
        cost_estimate=cost(10**6, 16 * 10**6),
        name="whole_table",
    )(*arrived, *tops, table)


def as_rows(table):
    return table.reshape(table.shape[0], 1, LANES)


def pack_kernel(list_ref, count_ref, table_ref, *refs):
    outs, held = refs[:3], refs[3:]
    slot_tiles = list_ref.shape[1] // LANES
    for n in range(8):

        @pl.loop(0, slot_tiles, step=len(held))
        def _(i):
            firsts = [pl.multiple_of((i + k) * LANES, LANES) for k in range(len(held))]
            for first, rows in zip(firsts, held):
                for r in range(LANES):
                    rows[r : r + 1, :] = table_ref[list_ref[n, first + r]]
            for first, rows in zip(firsts, held):
                live = (lane_ids((KPAD, LANES)) + first) < count_ref[n]
                part, at = SENT[n]
                outs[part][at, :, pl.ds(first, LANES)] = jnp.where(live, rows[...].T[:KPAD], 0.0)


def pack(table, cell_count, proxy_list, proxy_count):
    slots = proxy_list.shape[1]
    return pl.pallas_call(
        pack_kernel,
        grid=(1,),
        out_shape=tuple(jax.ShapeDtypeStruct((size, KPAD, slots), jnp.float32) for size in (3, 3, 2)),
        in_specs=[
            SMEM_WHOLE,
            SMEM_WHOLE,
            pl.BlockSpec((cell_count, 1, LANES), lambda i: (0, 0, 0)),
        ],
        out_specs=tuple(
            pl.BlockSpec((size, KPAD, slots), lambda i: (0, 0, 0)) for size in (3, 3, 2)
        ),
        scratch_shapes=[pltpu.VMEM((LANES, LANES), jnp.float32)] * 2,
        compiler_params=params(),
        cost_estimate=cost(10**6, 25 * 10**6),
        name="pack",
    )(proxy_list, proxy_count, as_rows(table))


def shift(value, axis, by):
    count = lax.axis_size(axis)
    return lax.ppermute(value, axis, [(i, (i + by) % count) for i in range(count)])


def along_gy(down, up):
    return shift(down, "gy", -1), shift(up, "gy", 1)


def along_gx(down, up, mid):
    left = shift(jnp.stack([down[0], mid[0], up[0]]), "gx", -1)
    right = shift(jnp.stack([down[2], mid[1], up[2]]), "gx", 1)
    return down, up, left, right


def order_kernel(packed_ref, out_ref):
    lanes = lane_ids((LANES, LANES))
    within = lanes & (BLOCK - 1)
    base = lanes - within

    @pl.loop(0, packed_ref.shape[0] // LANES)
    def _(k):
        at = pl.ds(pl.multiple_of(k * LANES, LANES), LANES)
        packed = packed_ref[at, :]

        def step(i, ordered):
            value = jnp.take_along_axis(packed, base + i, axis=1, mode="promise_in_bounds")
            return jnp.where((value & (BLOCK - 1)) == within, value, ordered)

        ordered = lax.fori_loop(0, BLOCK, step, jnp.zeros_like(packed), unroll=8)
        out_ref[at, :] = ordered >> SHIFT


def order(packed):
    return pl.pallas_call(
        order_kernel,
        out_shape=jax.ShapeDtypeStruct(packed.shape, jnp.int32),
        in_specs=[VMEM_WHOLE],
        out_specs=VMEM_WHOLE,
        compiler_params=params(),
        cost_estimate=cost(10**6, 20 * 10**6),
        name="order",
    )(packed)


def split_kernel(ops_ref, out_ref, *, group):
    coefs = ops_ref.shape[1]

    @pl.loop(0, ops_ref.shape[0], step=group)
    def _(c):
        at = pl.ds(c, group)
        value = ops_ref[at]
        high = value.astype(jnp.bfloat16).astype(jnp.float32)
        out_ref[at] = jnp.zeros((group, KPAD, LANES), jnp.float32)
        out_ref[at, :coefs, :coefs] = high
        out_ref[at, :coefs, KPAD : KPAD + coefs] = value - high


def split(turned_ops):
    classes = turned_ops.shape[0]
    group = max(size for size in range(1, 10) if classes % size == 0)
    return pl.pallas_call(
        functools.partial(split_kernel, group=group),
        out_shape=jax.ShapeDtypeStruct((classes, KPAD, LANES), jnp.float32),
        in_specs=[VMEM_WHOLE],
        out_specs=VMEM_WHOLE,
        compiler_params=params(),
        cost_estimate=cost(10**6, 12 * 10**6),
        name="split",
    )(turned_ops)


def m2l_kernel(source_ref, class_ref, table_ref, ops_ref, out_ref, *gathered, first, turned):
    step = first + pl.program_id(0)
    lanes = lane_ids((1, LANES))
    in_first = lanes < KPAD
    in_second = lanes < 2 * KPAD

    def row(b, t):
        return table_ref[source_ref[b // 2, (b % 2) * BLOCK + t]]

    for u in range(2):
        for t in range(BLOCK):
            for g in range(3):
                b = u * PER_WINDOW + 3 * g
                one, two = row(b, t), row(b + 1, t)
                three = row(b + 2, t) if g < 2 else two
                gathered[u][g, t : t + 1, :] = jnp.where(
                    in_first, one, jnp.where(in_second, two, three)
                )

    rest = jnp.zeros((LANES - COPIES * KPAD, LANES), jnp.float32)
    none = jnp.zeros((KPAD, LANES), jnp.float32)
    results = []
    for u in range(2):
        total = jnp.zeros((BLOCK, LANES), jnp.float32)
        for g in range(3):
            held = []
            for s in range(3):
                b = 3 * g + s
                if b < PER_WINDOW:
                    held.append(ops_ref[class_ref[step * 2 * PER_WINDOW + u * PER_WINDOW + b]])
                else:
                    held.append(none)
            weights = jnp.concatenate(held + [rest], axis=0).astype(jnp.bfloat16)
            values = gathered[u][g]
            high = values.astype(jnp.bfloat16)
            low = (values - high.astype(jnp.float32)).astype(jnp.bfloat16)
            total += jnp.dot(high, weights, preferred_element_type=jnp.float32)
            total += jnp.dot(low, weights, preferred_element_type=jnp.float32)
        results.append(total)
    both = jnp.concatenate(results, axis=0)
    both = both + pltpu.roll(both, LANES - KPAD, 1)
    if turned:
        out_ref[0] = both.T[:KPAD]
    else:
        out_ref[...] = both


def m2l(sources, classes, table, ops, first, steps, turned, slots):
    if turned:
        per = slots // LANES
        shape = (steps // per, KPAD, slots)
        out_spec = pl.BlockSpec(
            (1, KPAD, LANES), lambda i: ((IN_ROW >> (4 * (i // per))) & 7, 0, i % per)
        )
    else:
        shape = (steps * LANES, LANES)
        out_spec = pl.BlockSpec((LANES, LANES), lambda i: (i, 0))
    return pl.pallas_call(
        functools.partial(m2l_kernel, first=first, turned=turned),
        grid=(steps,),
        out_shape=jax.ShapeDtypeStruct(shape, jnp.float32),
        in_specs=[
            pl.BlockSpec((8, LANES), lambda i: (first + i, 0), memory_space=pltpu.SMEM),
            SMEM_WHOLE,
            VMEM_WHOLE,
            VMEM_WHOLE,
        ],
        out_specs=out_spec,
        scratch_shapes=[pltpu.VMEM((3, BLOCK, LANES), jnp.float32)] * 2,
        compiler_params=params(),
        cost_estimate=cost(10**6, 150 * 10**6),
        name="m2l_slots" if turned else "m2l_cells",
    )(sources, classes, as_rows(table), ops)


def add_back_kernel(list_ref, count_ref, own_ref, *refs):
    slot_refs, out_ref = refs[:4], refs[4]
    rows, sums = refs[5], refs[6:]
    slots = list_ref.shape[1]
    sums[0][...] = own_ref[...]
    for held in sums[1:]:
        held[...] = jnp.zeros_like(held)
    for n in range(8):
        for k in range(slots // LANES):
            live = (lane_ids((KPAD, LANES)) + k * LANES) < count_ref[n]
            part, place = GOT[n]
            values = jnp.where(live, slot_refs[part][place, :, k * LANES : (k + 1) * LANES], 0.0)
            at = n * slots + k * LANES
            rows[at : at + LANES, :] = spread(values)

    @pl.loop(0, slots, step=4)
    def _(first):
        for j in range(4):
            to = [pl.ds(list_ref[n, first + j], 1) for n in range(8)]
            old = [sums[n][to[n], :] for n in range(8)]
            new = [old[n] + rows[pl.ds(n * slots + first + j, 1), :] for n in range(8)]
            for n in range(8):
                sums[n][to[n], :] = new[n]

    @pl.loop(0, own_ref.shape[0] // LANES)
    def _(k):
        at = pl.ds(pl.multiple_of(k * LANES, LANES), LANES)
        parts = [held[at, :] for held in sums]
        while len(parts) > 1:
            parts = [a + b for a, b in zip(parts[::2], parts[1::2])]
        out_ref[:, at] = parts[0].T[: out_ref.shape[0]]


def add_back(proxy_list, proxy_count, own_rows, slot_fields, coef_count):
    cell_count = own_rows.shape[0]
    slots = proxy_list.shape[1]
    return pl.pallas_call(
        add_back_kernel,
        out_shape=jax.ShapeDtypeStruct((coef_count, cell_count), jnp.float32),
        in_specs=[SMEM_WHOLE, SMEM_WHOLE] + [VMEM_WHOLE] * 5,
        out_specs=VMEM_WHOLE,
        scratch_shapes=[pltpu.VMEM((8 * slots, LANES), jnp.float32)]
        + [pltpu.VMEM((cell_count, LANES), jnp.float32)] * 8,
        compiler_params=params(),
        cost_estimate=cost(10**6, 30 * 10**6),
        name="add_back",
    )(proxy_list, proxy_count, own_rows, *slot_fields)


def carve_kernel(mesh_ref, out_ref, sems, *, first):
    sources, count, rows, width = out_ref.shape
    copies = [
        pltpu.make_async_copy(
            mesh_ref.at[pl.ds(first, count), pl.ds(s * rows, rows), :], out_ref.at[s], sems.at[s]
        )
        for s in range(sources)
    ]
    for copy in copies:
        copy.start()
    for copy in copies:
        copy.wait()


def carve(mesh, first, count, sources):
    rows, width = mesh.shape[1] // sources, mesh.shape[2]
    return pl.pallas_call(
        functools.partial(carve_kernel, first=first),
        out_shape=jax.ShapeDtypeStruct((sources, count, rows, width), jnp.float32),
        in_specs=[pl.BlockSpec(memory_space=pl.ANY)],
        out_specs=VMEM_WHOLE,
        scratch_shapes=[pltpu.SemaphoreType.DMA((sources,))],
        compiler_params=params(),
        cost_estimate=cost(0, 8 * count * sources * rows * width),
        name="carve",
    )(mesh)


def first_part_kernel(mesh_ref, place_ref, cells_ref, out_ref, sems, *, count, rows):
    sources, _, width = out_ref.shape
    copies = [
        pltpu.make_async_copy(
            mesh_ref.at[p, pl.ds(s * rows, rows), :],
            out_ref.at[s, pl.ds(p * rows, rows), :],
            sems.at[p, s],
        )
        for p in range(count)
        for s in range(sources)
    ]
    for copy in copies:
        copy.start()
    is_first = lane_ids((TOP_ROWS, LANES)) < KPAD
    rest = jnp.zeros((KPAD - cells_ref.shape[0], LANES), jnp.float32)
    table = spread(jnp.concatenate([cells_ref[:, :LANES], rest], axis=0))
    top = jnp.where(is_first, table[:TOP_ROWS, :], table[TOP_ROWS : 2 * TOP_ROWS, :])
    blocks = [place_ref[...].astype(jnp.float32), cell_lines(cells_ref), top]
    at = count * rows
    for block in blocks:
        high = block.shape[0] * LANES // width
        for h in range(width // LANES):
            for s in range(sources):
                out_ref[s, at : at + high, h * LANES : (h + 1) * LANES] = block[
                    h * high : (h + 1) * high, :
                ]
        at += high
    for copy in copies:
        copy.wait()


def cell_lines(cells_ref):
    lines = [cells_ref[0:1, k : k + LANES] for k in range(0, cells_ref.shape[1], LANES)]
    return DEPOSIT_SCALE * jnp.concatenate(lines, axis=0)


def first_part(mesh, place, multipoles, sources, count):
    rows, width = mesh.shape[1] // sources, mesh.shape[2]
    extra = (2 * place.size + TOP_ROWS * LANES) // width
    return pl.pallas_call(
        functools.partial(first_part_kernel, count=count, rows=rows),
        out_shape=jax.ShapeDtypeStruct((sources, count * rows + extra, width), jnp.float32),
        in_specs=[pl.BlockSpec(memory_space=pl.ANY), VMEM_WHOLE, VMEM_WHOLE],
        out_specs=VMEM_WHOLE,
        scratch_shapes=[
            pltpu.SemaphoreType.DMA((count, sources)),
        ],
        compiler_params=params(),
        cost_estimate=cost(0, 8 * sources * rows * width),
        name="first_part",
    )(mesh, place.reshape(-1, LANES), multipoles)


def log2(value):
    return value.bit_length() - 1


def sift_kernel(mine_ref, part_ref, code_ref, value_ref, bound_ref, top_ref, ride, sem, *, count, planes, rows):
    sources, extra, width = ride.shape
    lines = code_ref.shape[0] // sources
    copy = pltpu.make_async_copy(part_ref.at[:, pl.ds(count * rows, extra), :], ride, sem)
    copy.start()
    copy.wait()

    def unfold(first, count):
        high = count * LANES // width
        return jnp.concatenate(
            [
                ride[s, first : first + high, h * LANES : (h + 1) * LANES]
                for s in range(sources)
                for h in range(width // LANES)
            ],
            axis=0,
        )

    step = lines * LANES // width
    place = unfold(0, lines).astype(jnp.int32)
    value = unfold(step, lines)
    top_ref[...] = unfold(2 * step, TOP_ROWS)

    row_at, mesh_rows = log2(width), rows * sources
    plane = place >> (row_at + log2(mesh_rows))
    row = (place >> row_at) & (mesh_rows - 1)
    column = place & (width - 1)
    tiles = width // LANES
    target = (plane * tiles + (column >> LANE_SHIFT)) * rows + (row & (rows - 1))
    none = planes * tiles * rows * LANES
    mine = (row >> log2(rows)) == mine_ref[0]
    lanes = lane_ids(place.shape)
    code = jnp.where(mine, target * LANES + (column & (LANES - 1)), none)
    value = jnp.where(mine, value, 0.0)
    ahead = jnp.where(mine, 1, 0)
    for b in range(LANE_SHIFT):
        ahead = ahead + jnp.where(lanes >= (1 << b), pltpu.roll(ahead, 1 << b, 1), 0)
    shift = jnp.where(mine, lanes + 1 - ahead, 0)
    for b in range(LANE_SHIFT):
        back = LANES - (1 << b)
        moves = (shift >> b) & 1
        comes = pltpu.roll(moves, back, 1) == 1
        goes = moves == 1
        code = jnp.where(comes, pltpu.roll(code, back, 1), jnp.where(goes, none, code))
        value = jnp.where(comes, pltpu.roll(value, back, 1), jnp.where(goes, 0.0, value))
        shift = jnp.where(comes, pltpu.roll(shift, back, 1), jnp.where(goes, 0, shift))
    code_ref[...] = code
    value_ref[...] = value
    counts = jnp.sum(jnp.where(mine, 1.0, 0.0), axis=1, keepdims=True)
    counts = jnp.broadcast_to(counts, mine.shape).reshape(2 * sources, lines // 2, LANES)
    bound_ref[...] = jnp.max(counts, axis=0).astype(jnp.int32)


def sift(part, mine, count, planes, rows, lines):
    sources, whole_rows, width = part.shape
    extra = whole_rows - count * rows
    shape = (sources * lines, LANES)
    return pl.pallas_call(
        functools.partial(sift_kernel, count=count, planes=planes, rows=rows),
        out_shape=(
            jax.ShapeDtypeStruct(shape, jnp.int32),
            jax.ShapeDtypeStruct(shape, jnp.float32),
            jax.ShapeDtypeStruct((lines // 2, LANES), jnp.int32),
            jax.ShapeDtypeStruct((sources * TOP_ROWS, LANES), jnp.float32),
        ),
        in_specs=[SMEM_WHOLE, pl.BlockSpec(memory_space=pl.ANY)],
        out_specs=(VMEM_WHOLE,) * 4,
        scratch_shapes=[pltpu.VMEM((sources, extra, width), jnp.float32), pltpu.SemaphoreType.DMA],
        compiler_params=params(),
        cost_estimate=cost(10**6, 8 * 10**6),
        name="sift",
    )(mine, part)


def deposit_kernel(code_ref, value_ref, bound_ref, *refs):
    sources = len(refs) // 2
    outs, others = refs[:sources], refs[sources:]
    lines = code_ref.shape[0] // (2 * sources)
    lanes = lane_ids((1, LANES))
    for held in refs:
        held[...] = jnp.zeros_like(held)

    def line(g, _):
        def one(j):
            at = [((2 * s + h) * lines + g, j) for h in range(2) for s in range(sources)]
            codes = [code_ref[i] for i in at]
            to = [pl.ds(code >> LANE_SHIFT, 1) for code in codes]
            old = [held[rows, :] for held, rows in zip(refs, to)]
            new = [
                row + jnp.where(lanes == (code & (LANES - 1)), value_ref[i], 0.0)
                for row, code, i in zip(old, codes, at)
            ]
            for held, rows, row in zip(refs, to, new):
                held[rows, :] = row

        def four(i, _):
            for j in range(4):
                one(4 * i + j)
            return 0

        return lax.fori_loop(0, (bound_ref[g, 0] + 3) >> 2, four, 0)

    lax.fori_loop(0, lines, line, 0)
    for out_ref, held in zip(outs, others):
        out_ref[...] = out_ref[...] + held[...]


def deposit(codes, values, bounds, rows, sources):
    return pl.pallas_call(
        deposit_kernel,
        out_shape=(jax.ShapeDtypeStruct((rows, LANES), jnp.float32),) * sources,
        in_specs=[SMEM_WHOLE] * 3,
        out_specs=(VMEM_WHOLE,) * sources,
        scratch_shapes=[pltpu.VMEM((rows, LANES), jnp.float32)] * sources,
        compiler_params=params(),
        cost_estimate=cost(10**6, 40 * 10**6),
        name="deposit",
    )(codes, values, bounds)


def fourier_tables(length):
    points, half = length // 2, length // 4
    positions = np.arange(points)
    scale = 1.0 / np.sqrt(length)
    parts = []
    for odd in range(2):
        ks = 2 * np.arange(half) + odd
        angles = (positions[:, None] * ks[None, :] % length) * (2.0 * np.pi / length)
        imag = -np.sin(angles) * scale
        if not odd:
            imag[:, 0] = np.where(positions % 2 == 0, scale, -scale)
        parts.append(np.concatenate([np.cos(angles) * scale, imag], axis=1))
    whole = np.stack(parts)
    high = whole.astype(ml_dtypes.bfloat16)
    low = (whole - high.astype(np.float64)).astype(ml_dtypes.bfloat16)
    return high, low


def fourier_kernel(*refs, sources):
    mesh_ref, add_refs = refs[0], refs[1 : 1 + sources]
    high_ref, low_ref = refs[1 + sources], refs[2 + sources]
    out_ref = refs[-1]
    rows, width = mesh_ref.shape[1:]
    pieces = []
    for s in range(sources):
        for h in range(width // LANES):
            pieces.append(
                mesh_ref[s, :, h * LANES : (h + 1) * LANES]
                + add_refs[s][h * rows : (h + 1) * rows, :]
            )
    mid = len(pieces) // 2
    halves = []
    for odd in range(2):
        if odd:
            folded = [a - b for a, b in zip(pieces[:mid], pieces[mid:])]
        else:
            folded = [a + b for a, b in zip(pieces[:mid], pieces[mid:])]
        values = jnp.concatenate(folded, axis=1)
        high = values.astype(jnp.bfloat16)
        low = (values - high.astype(jnp.float32)).astype(jnp.bfloat16)
        both = jnp.dot(
            jnp.concatenate([high, low], axis=0), high_ref[odd], preferred_element_type=jnp.float32
        )
        halves.append(
            both[:rows]
            + both[rows:]
            + jnp.dot(high, low_ref[odd], preferred_element_type=jnp.float32)
        )
    lanes = lane_ids((rows, LANES))
    is_first = lanes == 0
    is_odd = (lanes & 1) == 1
    steps = lanes >> 1
    tiles = len(pieces)
    per = tiles // 4

    def tile(odd, part, j):
        at = (part * per + j) * LANES
        return halves[odd][:, at : at + LANES]

    def pick(value, lane):
        return jnp.take_along_axis(value, lane, axis=1, mode="promise_in_bounds")

    for j in range(tiles):
        for part in range(2):
            if j < tiles // 2:
                at = BLOCK * j
                lane = (at % LANES) + steps
                even = pick(tile(0, part, at // LANES), lane)
                odd = pick(tile(1, part, at // LANES), lane)
                if j == 0 and part == 1:
                    even = jnp.where(is_first, 0.0, even)
            else:
                at = BLOCK * (tiles - j)
                last = (at - 1) // LANES
                even = pick(tile(0, part, last), (at - steps) & (LANES - 1))
                odd = pick(tile(1, part, last), ((at - 1) % LANES) - steps)
                if at % LANES == 0 and j > tiles // 2:
                    even = jnp.where(is_first, tile(0, part, at // LANES), even)
                if part == 1:
                    even, odd = -even, -odd
                if j == tiles // 2:
                    even = jnp.where(is_first, 0.0 if part else tile(0, 1, 0), even)
            out_ref[part, 0, :, j * LANES : (j + 1) * LANES] = jnp.where(is_odd, odd, even)


def fourier(mesh_part, count, adds, tables, first, planes, so_far, rows):
    sources, _, width = mesh_part.shape
    length = sources * width
    add_rows = (width // LANES) * rows
    operands = [mesh_part, *adds, *tables]
    in_specs = (
        [pl.BlockSpec((sources, rows, width), lambda p: (0, p, 0))]
        + [pl.BlockSpec((add_rows, LANES), lambda p: (first + p, 0))] * sources
        + [
            pl.BlockSpec((2, length // 2, length // 2), lambda p: (0, 0, 0), pipeline_mode=pl.Buffered(1))
        ]
        * 2
    )
    aliases = {}
    if so_far is not None:
        aliases = {len(operands): 0}
        operands.append(so_far)
        in_specs.append(pl.BlockSpec(memory_space=pl.ANY))
    return pl.pallas_call(
        functools.partial(fourier_kernel, sources=sources),
        grid=(count,),
        out_shape=jax.ShapeDtypeStruct((2, planes, rows, length), jnp.float32),
        in_specs=in_specs,
        out_specs=pl.BlockSpec((2, 1, rows, length), lambda p: (0, first + p, 0, 0)),
        input_output_aliases=aliases,
        compiler_params=params(),
        cost_estimate=cost(10**6, count * 10 * 10**6),
        name="fourier",
    )(*operands)


def after(value, *others):
    return lax.optimization_barrier((value, *others))[0]


def on_device(
    multipoles,
    proxy_list,
    proxy_count,
    pair_source,
    pair_target,
    block_class,
    m2l_ops,
    cell_mesh,
    pm_density,
    *,
    n_gx,
    n_gy,
):
    coef_count, cell_count = multipoles.shape
    slots = proxy_list.shape[2]
    planes, mesh_rows, width = pm_density.shape
    own_rows = mesh_rows // n_gx
    domains = n_gx * n_gy
    lists, counts = proxy_list[0], proxy_count[0]

    def send(part):
        return lax.all_to_all(part, "gx", 0, 0, tiled=True)

    spans = []
    first = 0
    for size in CHUNKS:
        spans.append((first, size))
        first += size

    parts = [send(first_part(pm_density, cell_mesh, multipoles, n_gx, spans[0][1]))]
    carved = [
        carve(pm_density, at, size, n_gx).reshape(n_gx, size * own_rows, width)
        for at, size in spans[1:]
    ]

    cells = jnp.pad(multipoles, ((0, KPAD - coef_count), (0, 0)))
    base = cell_count + 8 * slots
    table = own_table(cells, base + TOP * domains)
    outgoing = pack(table, cell_count, lists, counts)

    top = pair_source - base
    domain = top >> log2(TOP)
    along = (domain & (n_gy - 1)) ^ lax.axis_index("gy")
    place = (along * n_gx + (domain >> log2(n_gy))) * TOP_ROWS + (top & (TOP_ROWS - 1))
    top = base + ((top >> log2(TOP_ROWS)) & 1) * (TOP_ROWS * domains) + place
    wanted = jnp.where(pair_source < base, pair_source, top)
    sources = order(((wanted << SHIFT) | (pair_target & (BLOCK - 1))).reshape(-1, LANES))

    arrived = along_gx(*along_gy(*outgoing[:2]), after(outgoing[2], sources))

    ops = split(m2l_ops.transpose(0, 2, 1))

    tiles = width // LANES
    add_rows = planes * tiles * own_rows
    mine = lax.axis_index("gx").astype(jnp.int32).reshape(1)
    codes, amounts, bounds, top_own = sift(
        parts[0], mine, spans[0][1], planes, own_rows, cell_count // LANES
    )
    tops = [top_own]
    for bit in range(log2(n_gy)):
        held = jnp.concatenate(tops, axis=0) if bit else top_own
        tops.append(lax.ppermute(held, "gy", [(i, i ^ (1 << bit)) for i in range(n_gy)]))

    parts.append(send(after(carved[0], parts[0], *arrived)))
    adds = deposit(codes, amounts, bounds, add_rows + 8, n_gx)
    table = whole_table(table, arrived, tops)
    cell_steps = cell_count // LANES
    slot_steps = 8 * slots // LANES
    slot_fields = m2l(sources, block_class, table, ops, cell_steps, slot_steps, True, slots)
    mid = after(slot_fields[6:], carved[1])
    returned = along_gx(*along_gy(slot_fields[:3], slot_fields[3:6]), mid)
    tables = fourier_tables(n_gx * width)
    spectrum = fourier(parts[0], spans[0][1], adds, tables, 0, planes, None, own_rows)
    parts.append(send(after(carved[1], parts[1], spectrum, *returned)))
    own_fields = m2l(sources, block_class, table, ops, 0, cell_steps, False, slots)
    spectrum = fourier(parts[1], spans[1][1], adds, tables, spans[1][0], planes, spectrum, own_rows)
    own_fields = after(own_fields, spectrum)
    field_tensors = add_back(lists, counts, own_fields, returned, coef_count)
    spectrum = fourier(parts[2], spans[2][1], adds, tables, spans[2][0], planes, spectrum, own_rows)
    return (field_tensors, spectrum)


def solution(mesh):
    placed = (
        P(None, ("gx", "gy")),
        P(("gx", "gy"), None, None),
        P(("gx", "gy"), None),
        P(("gx", "gy")),
        P(("gx", "gy")),
        P(("gx", "gy")),
        P(),
        P(("gx", "gy")),
        P("gy", None, "gx"),
    )
    return jax.shard_map(
        functools.partial(on_device, n_gx=mesh.shape["gx"], n_gy=mesh.shape["gy"]),
        mesh=mesh,
        in_specs=placed,
        out_specs=(P(None, ("gx", "gy")), P(None, "gy", "gx", None)),
        check_vma=False,
    )
```

```python
import functools

import jax
import jax.numpy as jnp
import ml_dtypes
import numpy as np
from jax import lax
from jax.experimental import pallas as pl
from jax.experimental.pallas import tpu as pltpu
from jax.sharding import PartitionSpec as P

TOP = 32
BLOCK = 64
LANES = 128
KPAD = 40
COPIES = 3
PER_WINDOW = 8
SHIFT = 6
LANE_SHIFT = 7
VMEM_BYTES = 48 * 1024 * 1024
CHUNKS = (1, 4, 3)
TOP_ROWS = TOP // 2

DEPOSIT_SCALE = 8.0
SENT = ((0, 0), (2, 0), (1, 0), (0, 1), (1, 1), (0, 2), (2, 1), (1, 2))
GOT = ((3, 2), (3, 1), (3, 0), (1, 1), (0, 1), (2, 2), (2, 1), (2, 0))
IN_ROW = 0x57241360

SMEM_WHOLE = pl.BlockSpec(memory_space=pltpu.SMEM)
VMEM_WHOLE = pl.BlockSpec(memory_space=pltpu.VMEM)


def params():
    return pltpu.CompilerParams(vmem_limit_bytes=VMEM_BYTES)


def cost(flops, nbytes):
    return pl.CostEstimate(flops=flops, bytes_accessed=nbytes, transcendentals=0)


def spread(block):
    rest = jnp.zeros((LANES - COPIES * KPAD, LANES), jnp.float32)
    return jnp.concatenate([block] * COPIES + [rest], axis=0).T


def lane_ids(shape):
    return lax.broadcasted_iota(jnp.int32, shape, len(shape) - 1)


def own_table_kernel(cells_ref, out_ref):
    @pl.loop(0, cells_ref.shape[1] // LANES)
    def _(k):
        at = pl.multiple_of(k * LANES, LANES)
        out_ref[pl.ds(at, LANES), :] = spread(cells_ref[:, pl.ds(at, LANES)])


def own_table(cells, rows):
    count = cells.shape[1]
    return pl.pallas_call(
        own_table_kernel,
        grid=(1,),
        out_shape=jax.ShapeDtypeStruct((rows, LANES), jnp.float32),
        in_specs=[pl.BlockSpec((KPAD, count), lambda i: (0, 0))],
        out_specs=pl.BlockSpec((count, LANES), lambda i: (0, 0)),
        compiler_params=params(),
        cost_estimate=cost(10**6, 12 * 10**6),
        name="own_table",
    )(cells)


def cut_rows(refs, first, stop):
    pieces, at = [], 0
    for ref in refs:
        low, high = max(first - at, 0), min(stop - at, ref.shape[0])
        if low < high:
            pieces.append(ref[low:high, :])
        at += ref.shape[0]
    return jnp.concatenate(pieces, axis=0) if len(pieces) > 1 else pieces[0]


def whole_table_kernel(*refs, slot_steps):
    top_refs, out_ref = refs[4:-2], refs[-1]
    step = pl.program_id(0)
    for k in range(slot_steps):

        @pl.when(step == k)
        def _():
            at = 0
            for n in (2 * k, 2 * k + 1):
                part, place = GOT[n]
                for c in range(refs[part].shape[2] // LANES):
                    block = refs[part][place, :, c * LANES : (c + 1) * LANES]
                    out_ref[at : at + LANES, :] = spread(block)
                    at += LANES

    rows = out_ref.shape[0]
    total = sum(ref.shape[0] for ref in top_refs)
    lanes = lane_ids((rows, LANES))
    for k in range(2 * total // rows):

        @pl.when(step == slot_steps + k)
        def _():
            pieces = []
            for first in range(k * rows, (k + 1) * rows, min(rows, total)):
                group, at = first // total, first % total
                value = cut_rows(top_refs, at, at + min(rows, total))
                pieces.append(pltpu.roll(value, LANES - KPAD, 1) if group else value)
            value = jnp.concatenate(pieces, axis=0) if len(pieces) > 1 else pieces[0]
            value = jnp.where(lanes < KPAD, value, 0.0)
            out_ref[...] = value + pltpu.roll(value, KPAD, 1) + pltpu.roll(value, 2 * KPAD, 1)


def whole_table(table, arrived, tops):
    slots = arrived[0].shape[2]
    rows = 2 * slots
    top_rows = 2 * sum(part.shape[0] for part in tops)
    first = (table.shape[0] - 8 * slots - top_rows) // rows
    return pl.pallas_call(
        functools.partial(whole_table_kernel, slot_steps=4),
        grid=(4 + top_rows // rows,),
        out_shape=jax.ShapeDtypeStruct(table.shape, jnp.float32),
        in_specs=[VMEM_WHOLE] * (4 + len(tops)) + [pl.BlockSpec(memory_space=pl.ANY)],
        out_specs=pl.BlockSpec((rows, LANES), lambda i: (first + i, 0)),
        input_output_aliases={4 + len(tops): 0},
        compiler_params=params(),
        cost_estimate=cost(10**6, 16 * 10**6),
        name="whole_table",
    )(*arrived, *tops, table)


def as_rows(table):
    return table.reshape(table.shape[0], 1, LANES)


def pack_kernel(list_ref, count_ref, table_ref, *refs):
    outs, held = refs[:3], refs[3:]
    slot_tiles = list_ref.shape[1] // LANES
    for n in range(8):

        @pl.loop(0, slot_tiles, step=len(held))
        def _(i):
            firsts = [pl.multiple_of((i + k) * LANES, LANES) for k in range(len(held))]
            for first, rows in zip(firsts, held):
                for r in range(LANES):
                    rows[r : r + 1, :] = table_ref[list_ref[n, first + r]]
            for first, rows in zip(firsts, held):
                live = (lane_ids((KPAD, LANES)) + first) < count_ref[n]
                part, at = SENT[n]
                outs[part][at, :, pl.ds(first, LANES)] = jnp.where(live, rows[...].T[:KPAD], 0.0)


def pack(table, cell_count, proxy_list, proxy_count):
    slots = proxy_list.shape[1]
    return pl.pallas_call(
        pack_kernel,
        grid=(1,),
        out_shape=tuple(jax.ShapeDtypeStruct((size, KPAD, slots), jnp.float32) for size in (3, 3, 2)),
        in_specs=[
            SMEM_WHOLE,
            SMEM_WHOLE,
            pl.BlockSpec((cell_count, 1, LANES), lambda i: (0, 0, 0)),
        ],
        out_specs=tuple(
            pl.BlockSpec((size, KPAD, slots), lambda i: (0, 0, 0)) for size in (3, 3, 2)
        ),
        scratch_shapes=[pltpu.VMEM((LANES, LANES), jnp.float32)] * 2,
        compiler_params=params(),
        cost_estimate=cost(10**6, 25 * 10**6),
        name="pack",
    )(proxy_list, proxy_count, as_rows(table))


def shift(value, axis, by):
    count = lax.axis_size(axis)
    return lax.ppermute(value, axis, [(i, (i + by) % count) for i in range(count)])


def along_gy(down, up):
    return shift(down, "gy", -1), shift(up, "gy", 1)


def along_gx(down, up, mid):
    left = shift(jnp.stack([down[0], mid[0], up[0]]), "gx", -1)
    right = shift(jnp.stack([down[2], mid[1], up[2]]), "gx", 1)
    return down, up, left, right


def order_kernel(packed_ref, out_ref):
    lanes = lane_ids((LANES, LANES))
    within = lanes & (BLOCK - 1)
    base = lanes - within

    @pl.loop(0, packed_ref.shape[0] // LANES)
    def _(k):
        at = pl.ds(pl.multiple_of(k * LANES, LANES), LANES)
        packed = packed_ref[at, :]

        def step(i, ordered):
            value = jnp.take_along_axis(packed, base + i, axis=1, mode="promise_in_bounds")
            return jnp.where((value & (BLOCK - 1)) == within, value, ordered)

        ordered = lax.fori_loop(0, BLOCK, step, jnp.zeros_like(packed), unroll=8)
        out_ref[at, :] = ordered >> SHIFT


def order(packed):
    return pl.pallas_call(
        order_kernel,
        out_shape=jax.ShapeDtypeStruct(packed.shape, jnp.int32),
        in_specs=[VMEM_WHOLE],
        out_specs=VMEM_WHOLE,
        compiler_params=params(),
        cost_estimate=cost(10**6, 20 * 10**6),
        name="order",
    )(packed)


def split_kernel(ops_ref, out_ref, *, group):
    coefs = ops_ref.shape[1]

    @pl.loop(0, ops_ref.shape[0], step=group)
    def _(c):
        at = pl.ds(c, group)
        value = ops_ref[at]
        high = value.astype(jnp.bfloat16).astype(jnp.float32)
        out_ref[at] = jnp.zeros((group, KPAD, LANES), jnp.float32)
        out_ref[at, :coefs, :coefs] = high
        out_ref[at, :coefs, KPAD : KPAD + coefs] = value - high


def split(turned_ops):
    classes = turned_ops.shape[0]
    group = max(size for size in range(1, 10) if classes % size == 0)
    return pl.pallas_call(
        functools.partial(split_kernel, group=group),
        out_shape=jax.ShapeDtypeStruct((classes, KPAD, LANES), jnp.float32),
        in_specs=[VMEM_WHOLE],
        out_specs=VMEM_WHOLE,
        compiler_params=params(),
        cost_estimate=cost(10**6, 12 * 10**6),
        name="split",
    )(turned_ops)


def m2l_kernel(source_ref, class_ref, table_ref, ops_ref, out_ref, *gathered, first, turned):
    step = first + pl.program_id(0)
    lanes = lane_ids((1, LANES))
    in_first = lanes < KPAD
    in_second = lanes < 2 * KPAD

    def row(b, t):
        return table_ref[source_ref[b // 2, (b % 2) * BLOCK + t]]

    for u in range(2):
        for t in range(BLOCK):
            for g in range(3):
                b = u * PER_WINDOW + 3 * g
                one, two = row(b, t), row(b + 1, t)
                three = row(b + 2, t) if g < 2 else two
                gathered[u][g, t : t + 1, :] = jnp.where(
                    in_first, one, jnp.where(in_second, two, three)
                )

    rest = jnp.zeros((LANES - COPIES * KPAD, LANES), jnp.float32)
    none = jnp.zeros((KPAD, LANES), jnp.float32)
    results = []
    for u in range(2):
        total = jnp.zeros((BLOCK, LANES), jnp.float32)
        for g in range(3):
            held = []
            for s in range(3):
                b = 3 * g + s
                if b < PER_WINDOW:
                    held.append(ops_ref[class_ref[step * 2 * PER_WINDOW + u * PER_WINDOW + b]])
                else:
                    held.append(none)
            weights = jnp.concatenate(held + [rest], axis=0).astype(jnp.bfloat16)
            values = gathered[u][g]
            high = values.astype(jnp.bfloat16)
            low = (values - high.astype(jnp.float32)).astype(jnp.bfloat16)
            total += jnp.dot(high, weights, preferred_element_type=jnp.float32)
            total += jnp.dot(low, weights, preferred_element_type=jnp.float32)
        results.append(total)
    both = jnp.concatenate(results, axis=0)
    both = both + pltpu.roll(both, LANES - KPAD, 1)
    if turned:
        out_ref[0] = both.T[:KPAD]
    else:
        out_ref[...] = both


def m2l(sources, classes, table, ops, first, steps, turned, slots):
    if turned:
        per = slots // LANES
        shape = (steps // per, KPAD, slots)
        out_spec = pl.BlockSpec(
            (1, KPAD, LANES), lambda i: ((IN_ROW >> (4 * (i // per))) & 7, 0, i % per)
        )
    else:
        shape = (steps * LANES, LANES)
        out_spec = pl.BlockSpec((LANES, LANES), lambda i: (i, 0))
    return pl.pallas_call(
        functools.partial(m2l_kernel, first=first, turned=turned),
        grid=(steps,),
        out_shape=jax.ShapeDtypeStruct(shape, jnp.float32),
        in_specs=[
            pl.BlockSpec((8, LANES), lambda i: (first + i, 0), memory_space=pltpu.SMEM),
            SMEM_WHOLE,
            VMEM_WHOLE,
            VMEM_WHOLE,
        ],
        out_specs=out_spec,
        scratch_shapes=[pltpu.VMEM((3, BLOCK, LANES), jnp.float32)] * 2,
        compiler_params=params(),
        cost_estimate=cost(10**6, 150 * 10**6),
        name="m2l_slots" if turned else "m2l_cells",
    )(sources, classes, as_rows(table), ops)


def add_back_kernel(list_ref, count_ref, own_ref, *refs):
    slot_refs, out_ref = refs[:4], refs[4]
    rows, sums = refs[5], refs[6:]
    slots = list_ref.shape[1]
    sums[0][...] = own_ref[...]
    for held in sums[1:]:
        held[...] = jnp.zeros_like(held)
    for n in range(8):
        for k in range(slots // LANES):
            live = (lane_ids((KPAD, LANES)) + k * LANES) < count_ref[n]
            part, place = GOT[n]
            values = jnp.where(live, slot_refs[part][place, :, k * LANES : (k + 1) * LANES], 0.0)
            at = n * slots + k * LANES
            rows[at : at + LANES, :] = spread(values)

    @pl.loop(0, slots, step=4)
    def _(first):
        for j in range(4):
            to = [pl.ds(list_ref[n, first + j], 1) for n in range(8)]
            old = [sums[n][to[n], :] for n in range(8)]
            new = [old[n] + rows[pl.ds(n * slots + first + j, 1), :] for n in range(8)]
            for n in range(8):
                sums[n][to[n], :] = new[n]

    @pl.loop(0, own_ref.shape[0] // LANES)
    def _(k):
        at = pl.ds(pl.multiple_of(k * LANES, LANES), LANES)
        parts = [held[at, :] for held in sums]
        while len(parts) > 1:
            parts = [a + b for a, b in zip(parts[::2], parts[1::2])]
        out_ref[:, at] = parts[0].T[: out_ref.shape[0]]


def add_back(proxy_list, proxy_count, own_rows, slot_fields, coef_count):
    cell_count = own_rows.shape[0]
    slots = proxy_list.shape[1]
    return pl.pallas_call(
        add_back_kernel,
        out_shape=jax.ShapeDtypeStruct((coef_count, cell_count), jnp.float32),
        in_specs=[SMEM_WHOLE, SMEM_WHOLE] + [VMEM_WHOLE] * 5,
        out_specs=VMEM_WHOLE,
        scratch_shapes=[pltpu.VMEM((8 * slots, LANES), jnp.float32)]
        + [pltpu.VMEM((cell_count, LANES), jnp.float32)] * 8,
        compiler_params=params(),
        cost_estimate=cost(10**6, 30 * 10**6),
        name="add_back",
    )(proxy_list, proxy_count, own_rows, *slot_fields)


def carve_kernel(mesh_ref, out_ref, sems, *, first):
    sources, count, rows, width = out_ref.shape
    copies = [
        pltpu.make_async_copy(
            mesh_ref.at[pl.ds(first, count), pl.ds(s * rows, rows), :], out_ref.at[s], sems.at[s]
        )
        for s in range(sources)
    ]
    for copy in copies:
        copy.start()
    for copy in copies:
        copy.wait()


def carve(mesh, first, count, sources):
    rows, width = mesh.shape[1] // sources, mesh.shape[2]
    return pl.pallas_call(
        functools.partial(carve_kernel, first=first),
        out_shape=jax.ShapeDtypeStruct((sources, count, rows, width), jnp.float32),
        in_specs=[pl.BlockSpec(memory_space=pl.ANY)],
        out_specs=VMEM_WHOLE,
        scratch_shapes=[pltpu.SemaphoreType.DMA((sources,))],
        compiler_params=params(),
        cost_estimate=cost(0, 8 * count * sources * rows * width),
        name="carve",
    )(mesh)


def first_part_kernel(mesh_ref, place_ref, cells_ref, out_ref, sems, *, count, rows):
    sources, _, width = out_ref.shape
    copies = [
        pltpu.make_async_copy(
            mesh_ref.at[p, pl.ds(s * rows, rows), :],
            out_ref.at[s, pl.ds(p * rows, rows), :],
            sems.at[p, s],
        )
        for p in range(count)
        for s in range(sources)
    ]
    for copy in copies:
        copy.start()
    is_first = lane_ids((TOP_ROWS, LANES)) < KPAD
    rest = jnp.zeros((KPAD - cells_ref.shape[0], LANES), jnp.float32)
    table = spread(jnp.concatenate([cells_ref[:, :LANES], rest], axis=0))
    top = jnp.where(is_first, table[:TOP_ROWS, :], table[TOP_ROWS : 2 * TOP_ROWS, :])
    blocks = [place_ref[...].astype(jnp.float32), cell_lines(cells_ref), top]
    at = count * rows
    for block in blocks:
        high = block.shape[0] * LANES // width
        for h in range(width // LANES):
            for s in range(sources):
                out_ref[s, at : at + high, h * LANES : (h + 1) * LANES] = block[
                    h * high : (h + 1) * high, :
                ]
        at += high
    for copy in copies:
        copy.wait()


def cell_lines(cells_ref):
    lines = [cells_ref[0:1, k : k + LANES] for k in range(0, cells_ref.shape[1], LANES)]
    return DEPOSIT_SCALE * jnp.concatenate(lines, axis=0)


def first_part(mesh, place, multipoles, sources, count):
    rows, width = mesh.shape[1] // sources, mesh.shape[2]
    extra = (2 * place.size + TOP_ROWS * LANES) // width
    return pl.pallas_call(
        functools.partial(first_part_kernel, count=count, rows=rows),
        out_shape=jax.ShapeDtypeStruct((sources, count * rows + extra, width), jnp.float32),
        in_specs=[pl.BlockSpec(memory_space=pl.ANY), VMEM_WHOLE, VMEM_WHOLE],
        out_specs=VMEM_WHOLE,
        scratch_shapes=[
            pltpu.SemaphoreType.DMA((count, sources)),
        ],
        compiler_params=params(),
        cost_estimate=cost(0, 8 * sources * rows * width),
        name="first_part",
    )(mesh, place.reshape(-1, LANES), multipoles)


def log2(value):
    return value.bit_length() - 1


def sift_kernel(mine_ref, part_ref, code_ref, value_ref, bound_ref, top_ref, ride, sem, *, count, planes, rows):
    sources, extra, width = ride.shape
    lines = code_ref.shape[0] // sources
    copy = pltpu.make_async_copy(part_ref.at[:, pl.ds(count * rows, extra), :], ride, sem)
    copy.start()
    copy.wait()

    def unfold(first, count):
        high = count * LANES // width
        return jnp.concatenate(
            [
                ride[s, first : first + high, h * LANES : (h + 1) * LANES]
                for s in range(sources)
                for h in range(width // LANES)
            ],
            axis=0,
        )

    step = lines * LANES // width
    place = unfold(0, lines).astype(jnp.int32)
    value = unfold(step, lines)
    top_ref[...] = unfold(2 * step, TOP_ROWS)

    row_at, mesh_rows = log2(width), rows * sources
    plane = place >> (row_at + log2(mesh_rows))
    row = (place >> row_at) & (mesh_rows - 1)
    column = place & (width - 1)
    tiles = width // LANES
    target = (plane * tiles + (column >> LANE_SHIFT)) * rows + (row & (rows - 1))
    none = planes * tiles * rows * LANES
    mine = (row >> log2(rows)) == mine_ref[0]
    lanes = lane_ids(place.shape)
    code = jnp.where(mine, target * LANES + (column & (LANES - 1)), none)
    value = jnp.where(mine, value, 0.0)
    ahead = jnp.where(mine, 1, 0)
    for b in range(LANE_SHIFT):
        ahead = ahead + jnp.where(lanes >= (1 << b), pltpu.roll(ahead, 1 << b, 1), 0)
    shift = jnp.where(mine, lanes + 1 - ahead, 0)
    for b in range(LANE_SHIFT):
        back = LANES - (1 << b)
        moves = (shift >> b) & 1
        comes = pltpu.roll(moves, back, 1) == 1
        goes = moves == 1
        code = jnp.where(comes, pltpu.roll(code, back, 1), jnp.where(goes, none, code))
        value = jnp.where(comes, pltpu.roll(value, back, 1), jnp.where(goes, 0.0, value))
        shift = jnp.where(comes, pltpu.roll(shift, back, 1), jnp.where(goes, 0, shift))
    code_ref[...] = code
    value_ref[...] = value
    counts = jnp.sum(jnp.where(mine, 1.0, 0.0), axis=1, keepdims=True)
    counts = jnp.broadcast_to(counts, mine.shape).reshape(2 * sources, lines // 2, LANES)
    bound_ref[...] = jnp.max(counts, axis=0).astype(jnp.int32)


def sift(part, mine, count, planes, rows, lines):
    sources, whole_rows, width = part.shape
    extra = whole_rows - count * rows
    shape = (sources * lines, LANES)
    return pl.pallas_call(
        functools.partial(sift_kernel, count=count, planes=planes, rows=rows),
        out_shape=(
            jax.ShapeDtypeStruct(shape, jnp.int32),
            jax.ShapeDtypeStruct(shape, jnp.float32),
            jax.ShapeDtypeStruct((lines // 2, LANES), jnp.int32),
            jax.ShapeDtypeStruct((sources * TOP_ROWS, LANES), jnp.float32),
        ),
        in_specs=[SMEM_WHOLE, pl.BlockSpec(memory_space=pl.ANY)],
        out_specs=(VMEM_WHOLE,) * 4,
        scratch_shapes=[pltpu.VMEM((sources, extra, width), jnp.float32), pltpu.SemaphoreType.DMA],
        compiler_params=params(),
        cost_estimate=cost(10**6, 8 * 10**6),
        name="sift",
    )(mine, part)


def deposit_kernel(code_ref, value_ref, bound_ref, *refs):
    sources = len(refs) // 2
    outs, others = refs[:sources], refs[sources:]
    lines = code_ref.shape[0] // (2 * sources)
    lanes = lane_ids((1, LANES))
    for held in refs:
        held[...] = jnp.zeros_like(held)

    def line(g, _):
        def one(j):
            at = [((2 * s + h) * lines + g, j) for h in range(2) for s in range(sources)]
            codes = [code_ref[i] for i in at]
            to = [pl.ds(code >> LANE_SHIFT, 1) for code in codes]
            old = [held[rows, :] for held, rows in zip(refs, to)]
            new = [
                row + jnp.where(lanes == (code & (LANES - 1)), value_ref[i], 0.0)
                for row, code, i in zip(old, codes, at)
            ]
            for held, rows, row in zip(refs, to, new):
                held[rows, :] = row

        def four(i, _):
            for j in range(4):
                one(4 * i + j)
            return 0

        return lax.fori_loop(0, (bound_ref[g, 0] + 3) >> 2, four, 0)

    lax.fori_loop(0, lines, line, 0)
    for out_ref, held in zip(outs, others):
        out_ref[...] = out_ref[...] + held[...]


def deposit(codes, values, bounds, rows, sources):
    return pl.pallas_call(
        deposit_kernel,
        out_shape=(jax.ShapeDtypeStruct((rows, LANES), jnp.float32),) * sources,
        in_specs=[SMEM_WHOLE] * 3,
        out_specs=(VMEM_WHOLE,) * sources,
        scratch_shapes=[pltpu.VMEM((rows, LANES), jnp.float32)] * sources,
        compiler_params=params(),
        cost_estimate=cost(10**6, 40 * 10**6),
        name="deposit",
    )(codes, values, bounds)


def fourier_tables(length):
    points, half = length // 2, length // 4
    positions = np.arange(points)
    scale = 1.0 / np.sqrt(length)
    parts = []
    for odd in range(2):
        ks = 2 * np.arange(half) + odd
        angles = (positions[:, None] * ks[None, :] % length) * (2.0 * np.pi / length)
        imag = -np.sin(angles) * scale
        if not odd:
            imag[:, 0] = np.where(positions % 2 == 0, scale, -scale)
        parts.append(np.concatenate([np.cos(angles) * scale, imag], axis=1))
    whole = np.stack(parts)
    high = whole.astype(ml_dtypes.bfloat16)
    low = (whole - high.astype(np.float64)).astype(ml_dtypes.bfloat16)
    return high, low


def fourier_kernel(*refs, sources):
    mesh_ref, add_refs = refs[0], refs[1 : 1 + sources]
    high_ref, low_ref = refs[1 + sources], refs[2 + sources]
    out_ref = refs[-1]
    rows, width = mesh_ref.shape[1:]
    pieces = []
    for s in range(sources):
        for h in range(width // LANES):
            pieces.append(
                mesh_ref[s, :, h * LANES : (h + 1) * LANES]
                + add_refs[s][h * rows : (h + 1) * rows, :]
            )
    mid = len(pieces) // 2
    halves = []
    for odd in range(2):
        if odd:
            folded = [a - b for a, b in zip(pieces[:mid], pieces[mid:])]
        else:
            folded = [a + b for a, b in zip(pieces[:mid], pieces[mid:])]
        values = jnp.concatenate(folded, axis=1)
        high = values.astype(jnp.bfloat16)
        low = (values - high.astype(jnp.float32)).astype(jnp.bfloat16)
        both = jnp.dot(
            jnp.concatenate([high, low], axis=0), high_ref[odd], preferred_element_type=jnp.float32
        )
        halves.append(
            both[:rows]
            + both[rows:]
            + jnp.dot(high, low_ref[odd], preferred_element_type=jnp.float32)
        )
    lanes = lane_ids((rows, LANES))
    is_first = lanes == 0
    is_odd = (lanes & 1) == 1
    steps = lanes >> 1
    tiles = len(pieces)
    per = tiles // 4

    def tile(odd, part, j):
        at = (part * per + j) * LANES
        return halves[odd][:, at : at + LANES]

    def pick(value, lane):
        return jnp.take_along_axis(value, lane, axis=1, mode="promise_in_bounds")

    for j in range(tiles):
        for part in range(2):
            if j < tiles // 2:
                at = BLOCK * j
                lane = (at % LANES) + steps
                even = pick(tile(0, part, at // LANES), lane)
                odd = pick(tile(1, part, at // LANES), lane)
                if j == 0 and part == 1:
                    even = jnp.where(is_first, 0.0, even)
            else:
                at = BLOCK * (tiles - j)
                last = (at - 1) // LANES
                even = pick(tile(0, part, last), (at - steps) & (LANES - 1))
                odd = pick(tile(1, part, last), ((at - 1) % LANES) - steps)
                if at % LANES == 0 and j > tiles // 2:
                    even = jnp.where(is_first, tile(0, part, at // LANES), even)
                if part == 1:
                    even, odd = -even, -odd
                if j == tiles // 2:
                    even = jnp.where(is_first, 0.0 if part else tile(0, 1, 0), even)
            out_ref[part, 0, :, j * LANES : (j + 1) * LANES] = jnp.where(is_odd, odd, even)


def fourier(mesh_part, count, adds, tables, first, planes, so_far, rows):
    sources, _, width = mesh_part.shape
    length = sources * width
    add_rows = (width // LANES) * rows
    operands = [mesh_part, *adds, *tables]
    in_specs = (
        [pl.BlockSpec((sources, rows, width), lambda p: (0, p, 0))]
        + [pl.BlockSpec((add_rows, LANES), lambda p: (first + p, 0))] * sources
        + [
            pl.BlockSpec((2, length // 2, length // 2), lambda p: (0, 0, 0), pipeline_mode=pl.Buffered(1))
        ]
        * 2
    )
    aliases = {}
    if so_far is not None:
        aliases = {len(operands): 0}
        operands.append(so_far)
        in_specs.append(pl.BlockSpec(memory_space=pl.ANY))
    return pl.pallas_call(
        functools.partial(fourier_kernel, sources=sources),
        grid=(count,),
        out_shape=jax.ShapeDtypeStruct((2, planes, rows, length), jnp.float32),
        in_specs=in_specs,
        out_specs=pl.BlockSpec((2, 1, rows, length), lambda p: (0, first + p, 0, 0)),
        input_output_aliases=aliases,
        compiler_params=params(),
        cost_estimate=cost(10**6, count * 10 * 10**6),
        name="fourier",
    )(*operands)


def after(value, *others):
    return lax.optimization_barrier((value, *others))[0]


def on_device(
    multipoles,
    proxy_list,
    proxy_count,
    pair_source,
    pair_target,
    block_class,
    m2l_ops,
    cell_mesh,
    pm_density,
    *,
    n_gx,
    n_gy,
):
    coef_count, cell_count = multipoles.shape
    slots = proxy_list.shape[2]
    planes, mesh_rows, width = pm_density.shape
    own_rows = mesh_rows // n_gx
    domains = n_gx * n_gy
    lists, counts = proxy_list[0], proxy_count[0]

    def send(part):
        return lax.all_to_all(part, "gx", 0, 0, tiled=True)

    spans = []
    first = 0
    for size in CHUNKS:
        spans.append((first, size))
        first += size

    parts = [send(first_part(pm_density, cell_mesh, multipoles, n_gx, spans[0][1]))]
    carved = [
        carve(pm_density, at, size, n_gx).reshape(n_gx, size * own_rows, width)
        for at, size in spans[1:]
    ]

    cells = jnp.pad(multipoles, ((0, KPAD - coef_count), (0, 0)))
    base = cell_count + 8 * slots
    table = own_table(cells, base + TOP * domains)
    outgoing = pack(table, cell_count, lists, counts)

    top = pair_source - base
    domain = top >> log2(TOP)
    along = (domain & (n_gy - 1)) ^ lax.axis_index("gy")
    place = (along * n_gx + (domain >> log2(n_gy))) * TOP_ROWS + (top & (TOP_ROWS - 1))
    top = base + ((top >> log2(TOP_ROWS)) & 1) * (TOP_ROWS * domains) + place
    wanted = jnp.where(pair_source < base, pair_source, top)
    sources = order(((wanted << SHIFT) | (pair_target & (BLOCK - 1))).reshape(-1, LANES))

    arrived = along_gx(*along_gy(*outgoing[:2]), outgoing[2])

    ops = split(m2l_ops.transpose(0, 2, 1))

    tiles = width // LANES
    add_rows = planes * tiles * own_rows
    mine = lax.axis_index("gx").astype(jnp.int32).reshape(1)
    codes, amounts, bounds, top_own = sift(
        parts[0], mine, spans[0][1], planes, own_rows, cell_count // LANES
    )
    tops = [top_own]
    for bit in range(log2(n_gy)):
        held = jnp.concatenate(tops, axis=0) if bit else top_own
        tops.append(lax.ppermute(held, "gy", [(i, i ^ (1 << bit)) for i in range(n_gy)]))

    parts.append(send(after(carved[0], parts[0], sources, *arrived)))
    adds = deposit(codes, amounts, bounds, add_rows + 8, n_gx)
    table = whole_table(table, arrived, tops)
    cell_steps = cell_count // LANES
    slot_steps = 8 * slots // LANES
    slot_fields = m2l(sources, block_class, table, ops, cell_steps, slot_steps, True, slots)
    mid = after(slot_fields[6:], carved[1])
    returned = along_gx(*along_gy(slot_fields[:3], slot_fields[3:6]), mid)
    parts.append(send(after(carved[1], parts[1], adds[0], *returned)))
    tables = fourier_tables(n_gx * width)
    spectrum = fourier(parts[0], spans[0][1], adds, tables, 0, planes, None, own_rows)
    own_fields = m2l(sources, block_class, table, ops, 0, cell_steps, False, slots)
    spectrum = fourier(parts[1], spans[1][1], adds, tables, spans[1][0], planes, spectrum, own_rows)
    own_fields = after(own_fields, spectrum)
    field_tensors = add_back(lists, counts, own_fields, returned, coef_count)
    spectrum = fourier(parts[2], spans[2][1], adds, tables, spans[2][0], planes, spectrum, own_rows)
    return (field_tensors, spectrum)


def solution(mesh):
    placed = (
        P(None, ("gx", "gy")),
        P(("gx", "gy"), None, None),
        P(("gx", "gy"), None),
        P(("gx", "gy")),
        P(("gx", "gy")),
        P(("gx", "gy")),
        P(),
        P(("gx", "gy")),
        P("gy", None, "gx"),
    )
    return jax.shard_map(
        functools.partial(on_device, n_gx=mesh.shape["gx"], n_gy=mesh.shape["gy"]),
        mesh=mesh,
        in_specs=placed,
        out_specs=(P(None, ("gx", "gy")), P(None, "gy", "gx", None)),
        check_vma=False,
    )
```
